512 devices in a mesh: blk: 16 (over z_lo, core), wide: 32 (over x, z_hi, y).
Axes of the slice: x: 4, y: 4, z: 16 (z_hi: 2, z_lo: 8; z = z_hi * 8 + z_lo), core: 2. Of those that a mesh axis runs over, the one named last changes fastest.
Arguments:
- images: bfloat16 [196608, 768], P(('blk', 'wide')), may hold values from -0.21875 to 0.21875
- captions: bfloat16 [196608, 768], P(('blk', 'wide')), may hold values from -0.21875 to 0.21875
- logit_scale: float32 [], replicated, may hold values from 10 to 20
- row_lse: float32 [196608], replicated, may hold values from 2 to 5
- col_lse: float32 [196608], replicated, may hold values from 2 to 5
Outputs:
- image_grad: float32 [196608, 768], P(('blk', 'wide'))
- caption_grad: float32 [196608, 768], P(('blk', 'wide'))
The draws below stay inside these ranges and needn't reach their ends.
All inputs are finite; a program needn't handle non-finite values.
Results may differ from the reference program's by a relative error of at most 0.0021.
Values may be sent and summed in bfloat16 or wider, within the bound.
No kernel may reach another device: no remote copies, remote signals or barrier semaphores. Data moves between devices by JAX's collectives and lax.ppermute only.
A program may use at most 64 MiB of HBM per device.

```python
import math
import jax
import jax.numpy as jnp
from jax import lax

E = 768
ROWS = 384
STEPS = 3
BATCH = 196608
N_BLK = 16
N_WIDE = 32


def levels(key, dims, split, smallest, high):
    loudness, own = 1.0, jax.random.fold_in(key, 6)
    for dim, parts in split:
        draws = jnp.exp(jax.random.uniform(jax.random.fold_in(own, dim), (parts,), jnp.float32, smallest / len(split), high / len(split)))
        loudness = loudness * jnp.repeat(draws, dims[dim] // parts).reshape([-1 if axis == dim else 1 for axis in range(len(dims))])
    return loudness


def scatter_about(own_key, dims, deviation, reach, cuts=(), kind=jnp.bfloat16):
    result = jax.random.normal(own_key, dims, jnp.float32) * deviation
    if len(cuts) > 0:
        result = levels(own_key, dims, cuts, -0.22, 0.18) * result
    return jnp.clip(result, min=-reach, max=reach).astype(kind)


def setup_inputs(seed: int = 0) -> dict:
    seeds = jax.random.split(jax.random.key(seed), 6)
    return {
        "images": scatter_about(seeds[0], (BATCH, E), E ** -0.5, 0.21875, ((0, 512),)),
        "captions": scatter_about(seeds[1], (BATCH, E), E ** -0.5, 0.21875, ((0, 512),)),
        "logit_scale": jnp.clip(jnp.exp(jax.random.uniform(seeds[2], (), jnp.float32, math.log(10.0), math.log(20.0))), 10.0, 20.0),
        "row_lse": jnp.clip(jax.random.uniform(seeds[3], (BATCH,), jnp.float32, 2.0, 5.0), 2.0, 5.0),
        "col_lse": jnp.clip(jax.random.uniform(seeds[4], (BATCH,), jnp.float32, 2.0, 5.0), 2.0, 5.0),
    }


def reference(images, captions, logit_scale, row_lse, col_lse):
    block_count = N_BLK * N_WIDE
    image_grid = images.reshape(block_count, ROWS, E)
    caption_grid = captions.reshape(block_count, ROWS, E)
    row_grid = row_lse.reshape(block_count, ROWS)
    col_grid = col_lse.reshape(block_count, ROWS)
    offsets = jnp.arange(STEPS + 1, dtype=jnp.int32)

    def visit_block(running, block_id):
        blk_index = block_id // N_WIDE
        wide_index = block_id % N_WIDE
        near_ids = ((blk_index - offsets) % N_BLK) * N_WIDE + wide_index
        far_ids = ((blk_index - offsets) % N_BLK) * N_WIDE + (wide_index - 1) % N_WIDE
        chosen = jnp.stack([near_ids, far_ids], axis=1).reshape(-1).astype(jnp.int32)
        partners = caption_grid[chosen].reshape(-1, E)
        col_part = col_grid[chosen].reshape(-1)
        image_rows = image_grid[block_id]
        logits = logit_scale * lax.dot_general(image_rows, partners, (((1,), (1,)), ((), ())), preferred_element_type=jnp.float32)
        weights = 0.5 * (jnp.exp(logits - row_grid[block_id][:, None]) + jnp.exp(logits - col_part[None, :]))
        weights = weights - jnp.eye(ROWS, partners.shape[0], dtype=jnp.float32)
        weights = weights.astype(jnp.bfloat16)
        image_part = logit_scale * jnp.dot(weights, partners, preferred_element_type=jnp.float32)
        caption_part = lax.dot_general(weights, image_rows, (((0,), (0,)), ((), ())), preferred_element_type=jnp.float32)
        running = running.at[chosen].add(caption_part.reshape(-1, ROWS, E))
        return running, image_part

    initial = jnp.zeros((block_count, ROWS, E), jnp.float32)
    running, image_parts = lax.scan(visit_block, initial, jnp.arange(block_count, dtype=jnp.int32))
    return image_parts.reshape(-1, E), logit_scale * running.reshape(-1, E)
```

```python
import jax
import jax.numpy as jnp
from jax import lax
from jax.sharding import PartitionSpec as P

AXES = ("blk", "wide")


def coordinates(blk, wide):
    return wide // 8, (wide // 4) % 2, wide % 4, blk // 2, blk % 2


def device_id(x, half, y, z, core):
    return ((z % 8) * 2 + core) * 32 + ((x % 4) * 2 + half) * 4 + y


def pairs(target):
    found = []
    for blk in range(16):
        for wide in range(32):
            x, half, y, z, core = coordinates(blk, wide)
            sign = 1 if core == 1 else -1
            mirrored = y if core == 1 else 3 - y
            there = target(x, half, mirrored, z, core, sign)
            if there is not None:
                x2, half2, mirrored2, z2, core2 = there
                y2 = mirrored2 if core == 1 else 3 - mirrored2
                found.append((blk * 32 + wide, device_id(x2, half2, y2, z2, core2)))
    return found


def crossing(x, half, sign):
    if sign == 1:
        return (x, 1) if half == 0 else (x + 1, 0)
    return (x, 0) if half == 1 else (x - 1, 1)


def to_sibling(x, h, m, z, c, s):
    y = m if c == 1 else 3 - m
    return x, h, (y if c == 1 else 3 - y), z, 1 - c


def to_next_chip(x, h, m, z, c, s):
    return x, h, m, z + s, c


def to_previous_chip(x, h, m, z, c, s):
    return x, h, m, z - s, c


def to_next_wide(x, h, m, z, c, s):
    return (x, h, m + 1, z, c) if m < 3 else None


def across(x, h, m, z, c, s):
    x2, h2 = crossing(x, h, s)
    return x2, h2, m, z + s, c


def line_to_line(here, there):
    return lambda x, h, m, z, c, s: (x, h, there, z, c) if m == here else None


def send(x, target):
    return lax.ppermute(x, AXES, pairs(target))


def on_device(images, captions, logit_scale, row_lse, col_lse):
    rows = images.shape[0]
    quarter = rows // 4
    blk = lax.axis_index("blk")
    wide = lax.axis_index("wide")
    core = blk % 2
    sign = 2 * core - 1
    y = wide % 4
    mirrored = jnp.where(core == 1, y, 3 - y)
    carries_captions = core == 1

    outer = jnp.where(carries_captions, captions, images)
    other = jnp.where(carries_captions, images, captions)

    def wanted(step):
        return quarter * step, quarter * (step + 1)

    def part(block, step):
        low, high = wanted(step)
        return block[low:high]

    inner = send(other, to_sibling)
    outer1 = send(outer, to_next_chip)
    both = [jnp.concatenate([part(inner, q), part(outer, q)], axis=0) for q in range(4)]
    spread0 = send(both[0], line_to_line(3, 0))
    spread1 = send(both[1], line_to_line(3, 2))
    spread2 = send(both[2], line_to_line(3, 1))
    held = jnp.where(
        mirrored == 0,
        spread0,
        jnp.where(mirrored == 2, spread1, jnp.where(mirrored == 1, spread2, both[3])),
    )
    crossed = send(held, across)
    inner1 = send(inner, to_next_chip)
    outer2 = send(outer1, to_next_chip)
    pair0 = send(jnp.concatenate([inner, outer], axis=0), to_next_wide)
    pair1 = send(jnp.concatenate([inner1, outer1], axis=0), to_next_wide)
    far2 = send(outer2, to_next_wide)
    back = send(crossed, to_previous_chip)
    ahead = send(crossed[quarter:], to_next_chip)

    def collect(mine):
        q1 = send(mine, line_to_line(2, 0))
        q2 = send(mine, line_to_line(1, 0))
        q3 = send(mine, line_to_line(3, 0))
        return [mine, q1, q2, q3]

    got1 = collect(crossed)
    got0 = collect(jnp.concatenate([back, ahead], axis=0))
    at_edge = mirrored == 0

    def edge(got, k, usual):
        whole = jnp.concatenate([g[k * quarter : (k + 1) * quarter] for g in got], axis=0)
        return jnp.where(at_edge, whole, usual)

    hop_inner1 = edge(got1, 0, pair1[:rows])
    hop_outer1 = edge(got1, 1, pair1[rows:])
    hop_inner0 = edge(got0, 0, pair0[:rows])
    hop_outer0 = edge(got0, 1, pair0[rows:])
    hop_outer2 = edge(got0, 2, far2)

    sib1 = send(jnp.concatenate([outer1, inner1], axis=0), to_sibling)
    sib2 = send(outer2, to_sibling)
    hop_sib1 = send(jnp.concatenate([hop_outer1, hop_inner1], axis=0), to_sibling)
    hop_sib0 = send(jnp.concatenate([hop_inner0, hop_outer2], axis=0), to_sibling)

    both_lse = jnp.concatenate([row_lse, col_lse])
    batch = row_lse.shape[0]
    near_kind = core * batch
    far_kind = (1 - core) * batch

    def factor(kind, b, w):
        start = kind + ((b % 16) * 32 + (w % 32)) * rows
        return 0.5 * jnp.exp(5.0 - lax.dynamic_slice_in_dim(both_lse, start, rows))

    pal = blk + 1 - 2 * core
    near_query = factor(far_kind, blk, wide)
    far_query = factor(near_kind, blk, wide)

    def near(b, hop):
        return factor(near_kind, b, wide - hop * sign)

    def far(b, hop):
        return factor(far_kind, b, wide + hop * sign)

    diagonal = jnp.eye(rows, dtype=jnp.float32)

    def term(query, query_factor, keys, key_factor, own=False):
        logits = logit_scale * lax.dot_general(
            query, keys, (((1,), (1,)), ((), ())), preferred_element_type=jnp.float32
        )
        weights = jnp.exp(logits - 5.0) * (query_factor[:, None] + key_factor[None, :])
        if own:
            weights = weights - diagonal
        return jnp.dot(weights.astype(jnp.bfloat16), keys, preferred_element_type=jnp.float32)

    near_sum = term(other, near_query, outer, far_query, True)
    far_sum = term(outer, far_query, other, near_query, True)
    for block, b, hop in (
        (inner, pal, 0),
        (outer1, blk - 2 * sign, 0),
        (inner1, pal - 2 * sign, 0),
        (hop_outer1, blk - 2 * sign, 1),
        (hop_inner1, pal - 2 * sign, 1),
        (hop_outer0, blk, 1),
        (hop_inner0, pal, 1),
    ):
        near_sum = near_sum + term(other, near_query, block, near(b, hop))
    for block, b, hop in (
        (sib1[:rows], pal + 2 * sign, 0),
        (sib1[rows:], blk + 2 * sign, 0),
        (sib2, pal + 4 * sign, 0),
        (hop_sib1[:rows], pal + 2 * sign, 1),
        (hop_sib1[rows:], blk + 2 * sign, 1),
        (hop_sib0[:rows], blk, 1),
        (hop_sib0[rows:], pal + 4 * sign, 1),
    ):
        far_sum = far_sum + term(outer, far_query, block, far(b, hop))

    image_grad = logit_scale * jnp.where(carries_captions, near_sum, far_sum)
    caption_grad = logit_scale * jnp.where(carries_captions, far_sum, near_sum)
    return image_grad, caption_grad


def solution(mesh):
    in_specs = (P(("blk", "wide"), None), P(("blk", "wide"), None), P(), P(), P())
    out_specs = (P(("blk", "wide"), None), P(("blk", "wide"), None))
    return jax.shard_map(
        on_device, mesh=mesh, in_specs=in_specs, out_specs=out_specs, check_vma=False
    )
```

```python
import jax
import jax.numpy as jnp
from jax import lax
from jax.experimental import pallas as pl
from jax.experimental.pallas import tpu as pltpu
from jax.sharding import PartitionSpec as P

AXES = ("blk", "wide")


def coordinates(blk, wide):
    return wide // 8, (wide // 4) % 2, wide % 4, blk // 2, blk % 2


def device_id(x, half, y, z, core):
    return ((z % 8) * 2 + core) * 32 + ((x % 4) * 2 + half) * 4 + y


def pairs(target):
    found = []
    for blk in range(16):
        for wide in range(32):
            x, half, y, z, core = coordinates(blk, wide)
            sign = 1 if core == 1 else -1
            mirrored = y if core == 1 else 3 - y
            there = target(x, half, mirrored, z, core, sign)
            if there is not None:
                x2, half2, mirrored2, z2, core2 = there
                y2 = mirrored2 if core == 1 else 3 - mirrored2
                found.append((blk * 32 + wide, device_id(x2, half2, y2, z2, core2)))
    return found


def crossing(x, half, sign):
    if sign == 1:
        return (x, 1) if half == 0 else (x + 1, 0)
    return (x, 0) if half == 1 else (x - 1, 1)


def to_sibling(x, h, m, z, c, s):
    return x, h, m, z, 1 - c


def to_next_chip_sibling(x, h, m, z, c, s):
    return x, h, m, z + s, 1 - c


def to_next_chip(x, h, m, z, c, s):
    return x, h, m, z + s, c


def to_previous_chip(x, h, m, z, c, s):
    return x, h, m, z - s, c


def to_next_wide(x, h, m, z, c, s):
    return (x, h, m + 1, z, c) if m < 3 else None


def to_sibling_next_wide(x, h, m, z, c, s):
    return (x, h, m - 1, z, c) if m > 0 else None


def across(x, h, m, z, c, s):
    x2, h2 = crossing(x, h, s)
    return x2, h2, m, z + s, c


def line_to_line(here, there):
    return lambda x, h, m, z, c, s: (x, h, there, z, c) if m == here else None


def send(name, x, target):
    with jax.named_scope(name):
        return lax.ppermute(x, AXES, pairs(target))


def scalars():
    return pl.BlockSpec(memory_space=pltpu.SMEM)


def whole():
    return pl.BlockSpec(memory_space=pltpu.VMEM)


def call(name, kernel, out_shape, smem, vmem, weight=1):
    many = isinstance(out_shape, (list, tuple))
    outs = [whole() for _ in out_shape] if many else whole()
    with jax.named_scope(name):
        return pl.pallas_call(
            kernel,
            out_shape=out_shape,
            in_specs=[scalars() for _ in smem] + [whole() for _ in vmem],
            out_specs=outs,
            cost_estimate=pl.CostEstimate(
                flops=weight * 1000, bytes_accessed=1000, transcendentals=0
            ),
            compiler_params=pltpu.CompilerParams(vmem_limit_bytes=20 * 1024 * 1024),
        )(*smem, *vmem)


def term(query, query_factor, keys, key_factor, scale, own=False):
    logits = lax.dot_general(
        query, keys, (((1,), (1,)), ((), ())), preferred_element_type=jnp.float32
    )
    weights = jnp.exp(logits * scale - 5.0) * (query_factor + key_factor)
    if own:
        rows = lax.broadcasted_iota(jnp.int32, weights.shape, 0)
        cols = lax.broadcasted_iota(jnp.int32, weights.shape, 1)
        weights = weights - jnp.where(rows == cols, 1.0, 0.0)
    return jnp.dot(weights.astype(jnp.bfloat16), keys, preferred_element_type=jnp.float32)


def add_terms(total, query, query_factor, key_factors, scale, items):
    for keys, row, own in items:
        part = term(query, query_factor, keys, key_factors[row : row + 1, :], scale, own)
        total = part if total is None else total + part
    return total


def cut_kernel(inner, outer, *outs):
    quarter = inner.shape[0] // 4
    for step in range(4):
        low = quarter * step
        outs[step][:quarter, :] = inner[low : low + quarter, :]
        outs[step][quarter:, :] = outer[low : low + quarter, :]


def on_device(images, captions, logit_scale, row_lse, col_lse):
    rows, width = images.shape
    quarter = rows // 4
    half = jnp.bfloat16
    blk = lax.axis_index("blk")
    wide = lax.axis_index("wide")
    core = blk % 2
    sign = 2 * core - 1
    y = wide % 4
    mirrored = jnp.where(core == 1, y, 3 - y)
    carries_captions = core == 1
    at_edge = jnp.where(mirrored == 0, 1, 0).astype(jnp.int32).reshape(1)
    sibling_at_edge = jnp.where(mirrored == 3, 1, 0).astype(jnp.int32).reshape(1)
    core_flag = core.astype(jnp.int32).reshape(1)
    scale = logit_scale.reshape(1)

    def blocks(count):
        return jax.ShapeDtypeStruct((count * rows, width), half)

    outer = jnp.where(carries_captions, captions, images)
    other = jnp.where(carries_captions, images, captions)

    def after(value, *others):
        return lax.optimization_barrier((value, *others))[0]

    inner = send("swap", other, to_sibling)
    outer1 = send("own_outer1", outer, to_next_chip)

    strip = jax.ShapeDtypeStruct((2 * quarter, width), half)
    cuts = call("cut", cut_kernel, [strip] * 4, (), (inner, outer))
    spread0 = send("spread0", cuts[0], line_to_line(3, 0))
    spread1 = send("spread1", cuts[1], line_to_line(3, 2))
    spread2 = send("spread2", cuts[2], line_to_line(3, 1))
    inner1 = send("own_inner1", inner, to_next_chip)
    held = jnp.where(
        mirrored == 0,
        spread0,
        jnp.where(mirrored == 2, spread1, jnp.where(mirrored == 1, spread2, cuts[3])),
    )
    crossed = send("cross", held, across)
    pair0 = send(
        "wide_pair0", jnp.concatenate([after(inner, held), outer], axis=0), to_next_wide
    )
    batch = row_lse.shape[0]

    def part(carried, b, w):
        start = ((b % 16) * 32 + (w % 32)) * rows
        from_rows = lax.dynamic_slice_in_dim(row_lse, start, rows)
        from_cols = lax.dynamic_slice_in_dim(col_lse, start, rows)
        return jnp.where(carries_captions == carried, from_cols, from_rows)

    def factor(values):
        return 0.5 * jnp.exp(5.0 - values)

    pal = blk + 1 - 2 * core
    near_w, far_w = wide - sign, wide + sign
    own_outer = part(True, blk, wide)
    own_other = part(False, blk, wide)
    key_factors = factor(
        jnp.stack(
            [
                own_outer,
                part(True, pal, wide),
                part(True, blk - 2 * sign, wide),
                part(True, pal - 2 * sign, wide),
                part(True, blk - 2 * sign, near_w),
                part(True, pal - 2 * sign, near_w),
                part(True, pal, near_w),
                part(True, blk, near_w),
                own_other,
                part(False, pal + 2 * sign, wide),
                part(False, blk + 2 * sign, wide),
                part(False, pal + 4 * sign, wide),
                part(False, pal + 2 * sign, far_w),
                part(False, blk + 2 * sign, far_w),
                part(False, blk, far_w),
                part(False, pal + 4 * sign, far_w),
            ]
        )
    )
    near_factor = jnp.broadcast_to(factor(own_other)[:, None], (rows, 128))
    far_factor = jnp.broadcast_to(factor(own_outer)[:, None], (rows, 128))
    total = jax.ShapeDtypeStruct((rows, width), jnp.float32)

    def terms(name, near_blocks, far_blocks, sums, weight=1):
        arrays = [array for array, _ in near_blocks + far_blocks]

        def kernel(s, oth, out, nf, ff, kf, *refs):
            keys, refs = refs[: len(arrays)], refs[len(arrays) :]
            starts, ends = (refs[:2], refs[2:]) if sums else ((None, None), refs)

            def add(start, query, query_factor, blocks, refs, end):
                items = []
                for ref, (_, places) in zip(refs, blocks):
                    for k, row in enumerate(places):
                        items.append((ref[k * rows : (k + 1) * rows, :], row, row in (0, 8)))
                before = None if start is None else start[...]
                end[...] = add_terms(before, query[...], query_factor[:, :1], kf, s[0], items)

            add(starts[0], oth, nf, near_blocks, keys[: len(near_blocks)], ends[0])
            add(starts[1], out, ff, far_blocks, keys[len(near_blocks) :], ends[1])

        return call(
            name, kernel, [total, total], (scale,),
            (other, outer, near_factor, far_factor, key_factors, *arrays, *(sums or ())), weight,
        )

    sums = terms("terms_own0", [(outer, [0]), (inner, [1]), (after(outer1, held), [2])], [(other, [8])], None, 100_000_000)
    own1 = jnp.concatenate([outer1, after(inner1, *sums)], axis=0)
    sib1 = send("sibling1", own1, to_sibling)
    pair1 = send("wide_pair1", own1, to_next_wide)
    sums = terms("terms_own1", [(inner1, [3])], [(sib1, [9, 10])], sums)
    crossed = after(crossed, pair0, pair1, *sums)

    back = send("cross_back", crossed, to_previous_chip)
    ahead = send("cross_ahead", crossed[quarter:], to_next_chip)

    def collect(name, mine):
        q1 = send(name + "1", mine, line_to_line(2, 0))
        q2 = send(name + "2", mine, line_to_line(1, 0))
        q3 = send(name + "3", mine, line_to_line(3, 0))
        return [mine, q1, q2, q3]

    got1 = collect("gather1_", crossed)
    far2 = send("own_outer2", after(outer1, ahead), to_next_chip_sibling)
    hop_far2 = send("wide_outer2", far2, to_sibling_next_wide)
    got0 = collect("gather0_", after(jnp.concatenate([back, ahead], axis=0), *got1))

    def merge1_kernel(edge, usual, q0, q1, q2, q3, out):
        @pl.when(edge[0] == 1)
        def _():
            for place, source in enumerate((q0, q1, q2, q3)):
                low = place * quarter
                out[low : low + quarter, :] = source[quarter:, :]
                out[rows + low : rows + low + quarter, :] = source[:quarter, :]

        @pl.when(edge[0] == 0)
        def _():
            out[...] = usual[...]

    hop1 = call("merge1", merge1_kernel, blocks(2), (at_edge,), (pair1, *got1))
    hop_sib1 = send("sibling_hop1", hop1, to_sibling)
    sums = terms("terms_hop1", [(hop1, [4, 5])], [(far2, [11])], sums)
    got0 = [after(got0[0], far2, *sums), *got0[1:]]

    def merge0_kernel(edge, usual, q0, q1, q2, q3, out, keys):
        @pl.when(edge[0] == 1)
        def _():
            for place, source in enumerate((q0, q1, q2, q3)):
                low = place * quarter
                out[low : low + quarter, :] = source[:quarter, :]
                keys[low : low + quarter, :] = source[quarter : 2 * quarter, :]
                out[rows + low : rows + low + quarter, :] = source[2 * quarter :, :]

        @pl.when(edge[0] == 0)
        def _():
            out[...] = usual[...]
            keys[...] = usual[rows:, :]

    hop0, hop_outer0 = call(
        "merge0", merge0_kernel, [blocks(2), blocks(1)], (at_edge,), (pair0, *got0)
    )
    hop_sib0 = send("sibling_hop0", hop0, to_sibling)
    sums = terms("terms_hop0", [(hop_outer0, [7]), (hop0, [6])], [(after(hop_sib1, hop_far2), [12, 13])], sums)

    def last_kernel(c, e, s, out, ff, kf, hs0, hf2, near_in, far_in, image_grad, caption_grad):
        farthest = jnp.where(e[0] == 1, hs0[rows:, :], hf2[...])
        far = s[0] * add_terms(
            far_in[...], out[...], ff[:, :1], kf, s[0],
            [(hs0[:rows, :], 14, False), (farthest, 15, False)],
        )
        near = s[0] * near_in[...]

        @pl.when(c[0] == 1)
        def _():
            image_grad[...] = near
            caption_grad[...] = far

        @pl.when(c[0] == 0)
        def _():
            image_grad[...] = far
            caption_grad[...] = near

    image_grad, caption_grad = call(
        "terms_last", last_kernel, [total, total], (core_flag, sibling_at_edge, scale),
        (outer, far_factor, key_factors, hop_sib0, hop_far2, *sums),
    )
    return image_grad, caption_grad


def solution(mesh):
    in_specs = (P(("blk", "wide"), None), P(("blk", "wide"), None), P(), P(), P())
    out_specs = (P(("blk", "wide"), None), P(("blk", "wide"), None))
    return jax.shard_map(
        on_device, mesh=mesh, in_specs=in_specs, out_specs=out_specs, check_vma=False
    )
```

```python
import jax
import jax.numpy as jnp
from jax import lax
from jax.experimental import pallas as pl
from jax.experimental.pallas import tpu as pltpu
from jax.sharding import PartitionSpec as P

AXES = ("blk", "wide")


def coordinates(blk, wide):
    return wide // 8, (wide // 4) % 2, wide % 4, blk // 2, blk % 2


def device_id(x, half, y, z, core):
    return ((z % 8) * 2 + core) * 32 + ((x % 4) * 2 + half) * 4 + y


def pairs(target):
    found = []
    for blk in range(16):
        for wide in range(32):
            x, half, y, z, core = coordinates(blk, wide)
            sign = 1 if core == 1 else -1
            mirrored = y if core == 1 else 3 - y
            there = target(x, half, mirrored, z, core, sign)
            if there is not None:
                x2, half2, mirrored2, z2, core2 = there
                y2 = mirrored2 if core == 1 else 3 - mirrored2
                found.append((blk * 32 + wide, device_id(x2, half2, y2, z2, core2)))
    return found


def crossing(x, half, sign):
    if sign == 1:
        return (x, 1) if half == 0 else (x + 1, 0)
    return (x, 0) if half == 1 else (x - 1, 1)


def to_sibling(x, h, m, z, c, s):
    return x, h, m, z, 1 - c


def to_previous_chip_sibling(x, h, m, z, c, s):
    return x, h, m, z - s, 1 - c


def to_next_chip_sibling(x, h, m, z, c, s):
    return x, h, m, z + s, 1 - c


def to_next_chip(x, h, m, z, c, s):
    return x, h, m, z + s, c


def to_previous_chip(x, h, m, z, c, s):
    return x, h, m, z - s, c


def to_next_wide(x, h, m, z, c, s):
    return (x, h, m + 1, z, c) if m < 3 else None


def to_sibling_next_wide(x, h, m, z, c, s):
    return (x, h, m - 1, z, c) if m > 0 else None


def across(x, h, m, z, c, s):
    x2, h2 = crossing(x, h, s)
    return x2, h2, m, z + s, c


def line_to_line(here, there):
    return lambda x, h, m, z, c, s: (x, h, there, z, c) if m == here else None


def send(name, x, target):
    with jax.named_scope(name):
        return lax.ppermute(x, AXES, pairs(target))


def scalars():
    return pl.BlockSpec(memory_space=pltpu.SMEM)


def whole():
    return pl.BlockSpec(memory_space=pltpu.VMEM)


def call(name, kernel, out_shape, smem, vmem, weight=1):
    many = isinstance(out_shape, (list, tuple))
    outs = [whole() for _ in out_shape] if many else whole()
    with jax.named_scope(name):
        return pl.pallas_call(
            kernel,
            out_shape=out_shape,
            in_specs=[scalars() for _ in smem] + [whole() for _ in vmem],
            out_specs=outs,
            cost_estimate=pl.CostEstimate(
                flops=weight * 1000, bytes_accessed=1000, transcendentals=0
            ),
            compiler_params=pltpu.CompilerParams(vmem_limit_bytes=16 * 1024 * 1024),
        )(*smem, *vmem)


def term(query, query_factor, keys, key_factor, scale, own=False):
    logits = lax.dot_general(
        query, keys, (((1,), (1,)), ((), ())), preferred_element_type=jnp.float32
    )
    weights = jnp.exp(logits * scale - 5.0) * (query_factor + key_factor)
    if own:
        rows = lax.broadcasted_iota(jnp.int32, weights.shape, 0)
        cols = lax.broadcasted_iota(jnp.int32, weights.shape, 1)
        weights = weights - jnp.where(rows == cols, 1.0, 0.0)
    return jnp.dot(weights.astype(jnp.bfloat16), keys, preferred_element_type=jnp.float32)


def add_terms(total, query, query_factor, key_factors, scale, items):
    for keys, row, own in items:
        part = term(query, query_factor, keys, key_factors[row : row + 1, :], scale, own)
        total = part if total is None else total + part
    return total


def cut_kernel(inner, outer, *outs):
    quarter = inner.shape[0] // 4
    for step in range(4):
        low = quarter * step
        outs[step][:quarter, :] = inner[low : low + quarter, :]
        outs[step][quarter:, :] = outer[low : low + quarter, :]


def on_device(images, captions, logit_scale, row_lse, col_lse):
    rows, width = images.shape
    quarter = rows // 4
    half = jnp.bfloat16
    blk = lax.axis_index("blk")
    wide = lax.axis_index("wide")
    core = blk % 2
    sign = 2 * core - 1
    y = wide % 4
    mirrored = jnp.where(core == 1, y, 3 - y)
    carries_captions = core == 1
    at_edge = jnp.where(mirrored == 0, 1, 0).astype(jnp.int32).reshape(1)
    sibling_at_edge = jnp.where(mirrored == 3, 1, 0).astype(jnp.int32).reshape(1)
    core_flag = core.astype(jnp.int32).reshape(1)
    scale = logit_scale.reshape(1)

    def blocks(count):
        return jax.ShapeDtypeStruct((count * rows, width), half)

    outer = jnp.where(carries_captions, captions, images)
    other = jnp.where(carries_captions, images, captions)

    def after(value, *others):
        return lax.optimization_barrier((value, *others))[0]

    inner = send("swap", other, to_sibling)
    outer1 = send("own_outer1", outer, to_next_chip)
    inner1 = send("own_inner1", other, to_previous_chip_sibling)

    strip = jax.ShapeDtypeStruct((2 * quarter, width), half)
    cuts = call("cut", cut_kernel, [strip] * 4, (), (inner, outer))
    spread0 = send("spread0", cuts[0], line_to_line(3, 0))
    spread1 = send("spread1", cuts[1], line_to_line(3, 2))
    spread2 = send("spread2", cuts[2], line_to_line(3, 1))
    held = jnp.where(
        mirrored == 0,
        spread0,
        jnp.where(mirrored == 2, spread1, jnp.where(mirrored == 1, spread2, cuts[3])),
    )
    crossed = send("cross", held, across)
    pair0 = send(
        "wide_pair0", jnp.concatenate([after(inner, held), outer], axis=0), to_next_wide
    )
    batch = row_lse.shape[0]

    def part(carried, b, w):
        start = ((b % 16) * 32 + (w % 32)) * rows
        from_rows = lax.dynamic_slice_in_dim(row_lse, start, rows)
        from_cols = lax.dynamic_slice_in_dim(col_lse, start, rows)
        return jnp.where(carries_captions == carried, from_cols, from_rows)

    def factor(values):
        return 0.5 * jnp.exp(5.0 - values)

    pal = blk + 1 - 2 * core
    near_w, far_w = wide - sign, wide + sign
    own_outer = part(True, blk, wide)
    own_other = part(False, blk, wide)
    key_factors = factor(
        jnp.stack(
            [
                own_outer,
                part(True, pal, wide),
                part(True, blk - 2 * sign, wide),
                part(True, pal - 2 * sign, wide),
                part(True, blk - 2 * sign, near_w),
                part(True, pal - 2 * sign, near_w),
                part(True, pal, near_w),
                part(True, blk, near_w),
                own_other,
                part(False, pal + 2 * sign, wide),
                part(False, blk + 2 * sign, wide),
                part(False, pal + 4 * sign, wide),
                part(False, pal + 2 * sign, far_w),
                part(False, blk + 2 * sign, far_w),
                part(False, blk, far_w),
                part(False, pal + 4 * sign, far_w),
            ]
        )
    )
    near_factor = jnp.broadcast_to(factor(own_other)[:, None], (rows, 128))
    far_factor = jnp.broadcast_to(factor(own_outer)[:, None], (rows, 128))
    total = jax.ShapeDtypeStruct((rows, width), jnp.float32)

    def terms(name, near_blocks, far_blocks, sums, weight=1):
        arrays = [array for array, _ in near_blocks + far_blocks]

        def kernel(s, oth, out, nf, ff, kf, *refs):
            keys, refs = refs[: len(arrays)], refs[len(arrays) :]
            starts, ends = (refs[:2], refs[2:]) if sums else ((None, None), refs)

            def add(start, query, query_factor, blocks, refs, end):
                items = []
                for ref, (_, places) in zip(refs, blocks):
                    for k, row in enumerate(places):
                        items.append((ref[k * rows : (k + 1) * rows, :], row, row in (0, 8)))
                before = None if start is None else start[...]
                end[...] = add_terms(before, query[...], query_factor[:, :1], kf, s[0], items)

            add(starts[0], oth, nf, near_blocks, keys[: len(near_blocks)], ends[0])
            add(starts[1], out, ff, far_blocks, keys[len(near_blocks) :], ends[1])

        return call(
            name, kernel, [total, total], (scale,),
            (other, outer, near_factor, far_factor, key_factors, *arrays, *(sums or ())), weight,
        )

    sums = terms("terms_own0", [(outer, [0]), (inner, [1]), (after(outer1, held), [2])], [(other, [8])], None, 100_000_000)
    own1 = jnp.concatenate([outer1, after(inner1, *sums)], axis=0)
    sib1 = send("sibling1", own1, to_sibling)
    pair1 = send("wide_pair1", own1, to_next_wide)
    sums = terms("terms_own1", [(inner1, [3])], [(sib1, [9, 10])], sums)
    crossed = after(crossed, pair0, pair1, *sums)

    back = send("cross_back", crossed, to_previous_chip)
    ahead = send("cross_ahead", crossed[quarter:], to_next_chip)

    def collect(name, mine):
        q1 = send(name + "1", mine, line_to_line(2, 0))
        q2 = send(name + "2", mine, line_to_line(1, 0))
        q3 = send(name + "3", mine, line_to_line(3, 0))
        return [mine, q1, q2, q3]

    got1 = collect("gather1_", crossed)
    far2 = send("own_outer2", after(outer1, ahead), to_next_chip_sibling)
    hop_far2 = send("wide_outer2", far2, to_sibling_next_wide)
    got0 = collect("gather0_", after(jnp.concatenate([back, ahead], axis=0), *got1))

    def merge1_kernel(edge, usual, q0, q1, q2, q3, out):
        @pl.when(edge[0] == 1)
        def _():
            for place, source in enumerate((q0, q1, q2, q3)):
                low = place * quarter
                out[low : low + quarter, :] = source[quarter:, :]
                out[rows + low : rows + low + quarter, :] = source[:quarter, :]

        @pl.when(edge[0] == 0)
        def _():
            out[...] = usual[...]

    hop1 = call("merge1", merge1_kernel, blocks(2), (at_edge,), (pair1, *got1))
    hop_sib1 = send("sibling_hop1", hop1, to_sibling)
    sums = terms("terms_hop1", [(hop1, [4, 5])], [(far2, [11])], sums)
    got0 = [after(got0[0], far2, *sums), *got0[1:]]

    def merge0_kernel(edge, usual, q0, q1, q2, q3, inner0, outer0, farthest):
        @pl.when(edge[0] == 1)
        def _():
            for place, source in enumerate((q0, q1, q2, q3)):
                low = place * quarter
                inner0[low : low + quarter, :] = source[:quarter, :]
                outer0[low : low + quarter, :] = source[quarter : 2 * quarter, :]
                farthest[low : low + quarter, :] = source[2 * quarter :, :]

        @pl.when(edge[0] == 0)
        def _():
            inner0[...] = usual[:rows, :]
            outer0[...] = usual[rows:, :]
            farthest[...] = usual[rows:, :]

    hop_inner0, hop_outer0, hop_outer2 = call(
        "merge0", merge0_kernel, [blocks(1)] * 3, (at_edge,), (pair0, *got0)
    )
    hop_sib0 = send("sibling_hop0", hop_inner0, to_sibling)
    hop_sib2 = send("sibling_hop2", hop_outer2, to_sibling)
    sums = terms(
        "terms_hop0", [(hop_outer0, [7]), (hop_inner0, [6])],
        [(after(hop_sib1, hop_far2), [12, 13])], sums,
    )

    def last_kernel(c, e, s, out, ff, kf, hs0, hs2, hf2, near_in, far_in, image_grad, caption_grad):
        farthest = jnp.where(e[0] == 1, hs2[...], hf2[...])
        far = s[0] * add_terms(
            far_in[...], out[...], ff[:, :1], kf, s[0],
            [(hs0[...], 14, False), (farthest, 15, False)],
        )
        near = s[0] * near_in[...]

        @pl.when(c[0] == 1)
        def _():
            image_grad[...] = near
            caption_grad[...] = far

        @pl.when(c[0] == 0)
        def _():
            image_grad[...] = far
            caption_grad[...] = near

    image_grad, caption_grad = call(
        "terms_last", last_kernel, [total, total], (core_flag, sibling_at_edge, scale),
        (outer, far_factor, key_factors, hop_sib0, hop_sib2, hop_far2, *sums),
    )
    return image_grad, caption_grad


def solution(mesh):
    in_specs = (P(("blk", "wide"), None), P(("blk", "wide"), None), P(), P(), P())
    out_specs = (P(("blk", "wide"), None), P(("blk", "wide"), None))
    return jax.shard_map(
        on_device, mesh=mesh, in_specs=in_specs, out_specs=out_specs, check_vma=False
    )
```

```python
import jax
import jax.numpy as jnp
from jax import lax
from jax.experimental import pallas as pl
from jax.experimental.pallas import tpu as pltpu
from jax.sharding import PartitionSpec as P

AXES = ("blk", "wide")


def coordinates(blk, wide):
    return wide // 8, (wide // 4) % 2, wide % 4, blk // 2, blk % 2


def device_id(x, half, y, z, core):
    return ((z % 8) * 2 + core) * 32 + ((x % 4) * 2 + half) * 4 + y


def pairs(target):
    found = []
    for blk in range(16):
        for wide in range(32):
            x, half, y, z, core = coordinates(blk, wide)
            sign = 1 if core == 1 else -1
            mirrored = y if core == 1 else 3 - y
            there = target(x, half, mirrored, z, core, sign)
            if there is not None:
                x2, half2, mirrored2, z2, core2 = there
                y2 = mirrored2 if core == 1 else 3 - mirrored2
                found.append((blk * 32 + wide, device_id(x2, half2, y2, z2, core2)))
    return found


def crossing(x, half, sign):
    if sign == 1:
        return (x, 1) if half == 0 else (x + 1, 0)
    return (x, 0) if half == 1 else (x - 1, 1)


def to_sibling(x, h, m, z, c, s):
    return x, h, m, z, 1 - c


def to_previous_chip_sibling(x, h, m, z, c, s):
    return x, h, m, z - s, 1 - c


def to_next_chip_sibling(x, h, m, z, c, s):
    return x, h, m, z + s, 1 - c


def to_next_chip(x, h, m, z, c, s):
    return x, h, m, z + s, c


def to_previous_chip(x, h, m, z, c, s):
    return x, h, m, z - s, c


def to_next_wide(x, h, m, z, c, s):
    return (x, h, m + 1, z, c) if m < 3 else None


def to_sibling_next_wide(x, h, m, z, c, s):
    return (x, h, m - 1, z, c) if m > 0 else None


def across(x, h, m, z, c, s):
    x2, h2 = crossing(x, h, s)
    return x2, h2, m, z + s, c


def line_to_line(here, there):
    return lambda x, h, m, z, c, s: (x, h, there, z, c) if m == here else None


def send(name, x, target):
    with jax.named_scope(name):
        return lax.ppermute(x, AXES, pairs(target))


def scalars():
    return pl.BlockSpec(memory_space=pltpu.SMEM)


def whole():
    return pl.BlockSpec(memory_space=pltpu.VMEM)


def call(name, kernel, out_shape, smem, vmem, weight=1):
    many = isinstance(out_shape, (list, tuple))
    outs = [whole() for _ in out_shape] if many else whole()
    with jax.named_scope(name):
        return pl.pallas_call(
            kernel,
            out_shape=out_shape,
            in_specs=[scalars() for _ in smem] + [whole() for _ in vmem],
            out_specs=outs,
            cost_estimate=pl.CostEstimate(
                flops=weight * 1000, bytes_accessed=1000, transcendentals=0
            ),
            compiler_params=pltpu.CompilerParams(vmem_limit_bytes=16 * 1024 * 1024),
        )(*smem, *vmem)


def term(query, query_factor, keys, key_factor, scale, own=False):
    logits = lax.dot_general(
        query, keys, (((1,), (1,)), ((), ())), preferred_element_type=jnp.float32
    )
    weights = jnp.exp(logits * scale - 5.0) * (query_factor + key_factor)
    if own:
        rows = lax.broadcasted_iota(jnp.int32, weights.shape, 0)
        cols = lax.broadcasted_iota(jnp.int32, weights.shape, 1)
        weights = weights - jnp.where(rows == cols, 1.0, 0.0)
    return jnp.dot(weights.astype(jnp.bfloat16), keys, preferred_element_type=jnp.float32)


def add_terms(total, query, query_factor, key_factors, scale, items):
    for keys, row, own in items:
        part = term(query, query_factor, keys, key_factors[row : row + 1, :], scale, own)
        total = part if total is None else total + part
    return total


def cut_kernel(inner, outer, *outs):
    quarter = inner.shape[0] // 4
    for step in range(4):
        low = quarter * step
        outs[step][:quarter, :] = inner[low : low + quarter, :]
        outs[step][quarter:, :] = outer[low : low + quarter, :]


def on_device(images, captions, logit_scale, row_lse, col_lse):
    rows, width = images.shape
    quarter = rows // 4
    half = jnp.bfloat16
    blk = lax.axis_index("blk")
    wide = lax.axis_index("wide")
    core = blk % 2
    sign = 2 * core - 1
    y = wide % 4
    mirrored = jnp.where(core == 1, y, 3 - y)
    carries_captions = core == 1
    at_edge = jnp.where(mirrored == 0, 1, 0).astype(jnp.int32).reshape(1)
    sibling_at_edge = jnp.where(mirrored == 3, 1, 0).astype(jnp.int32).reshape(1)
    core_flag = core.astype(jnp.int32).reshape(1)
    scale = logit_scale.reshape(1)

    def blocks(count):
        return jax.ShapeDtypeStruct((count * rows, width), half)

    outer = jnp.where(carries_captions, captions, images)
    other = jnp.where(carries_captions, images, captions)

    def after(value, *others):
        return lax.optimization_barrier((value, *others))[0]

    inner = send("swap", other, to_sibling)
    outer1 = send("own_outer1", outer, to_next_chip)
    inner1 = send("own_inner1", other, to_previous_chip_sibling)

    strip = jax.ShapeDtypeStruct((2 * quarter, width), half)
    cuts = call("cut", cut_kernel, [strip] * 4, (), (inner, outer))
    spread0 = send("spread0", cuts[0], line_to_line(3, 0))
    spread1 = send("spread1", cuts[1], line_to_line(3, 2))
    spread2 = send("spread2", cuts[2], line_to_line(3, 1))
    held = jnp.where(
        mirrored == 0,
        spread0,
        jnp.where(mirrored == 2, spread1, jnp.where(mirrored == 1, spread2, cuts[3])),
    )
    crossed = send("cross", held, across)
    early = send(
        "wide_early", jnp.concatenate([after(inner, held), outer, outer1, inner1], axis=0), to_next_wide
    )
    batch = row_lse.shape[0]

    def part(carried, b, w):
        start = ((b % 16) * 32 + (w % 32)) * rows
        from_rows = lax.dynamic_slice_in_dim(row_lse, start, rows)
        from_cols = lax.dynamic_slice_in_dim(col_lse, start, rows)
        return jnp.where(carries_captions == carried, from_cols, from_rows)

    def factor(values):
        return 0.5 * jnp.exp(5.0 - values)

    pal = blk + 1 - 2 * core
    near_w, far_w = wide - sign, wide + sign
    own_outer = part(True, blk, wide)
    own_other = part(False, blk, wide)
    key_factors = factor(
        jnp.stack(
            [
                own_outer,
                part(True, pal, wide),
                part(True, blk - 2 * sign, wide),
                part(True, pal - 2 * sign, wide),
                part(True, blk - 2 * sign, near_w),
                part(True, pal - 2 * sign, near_w),
                part(True, pal, near_w),
                part(True, blk, near_w),
                own_other,
                part(False, pal + 2 * sign, wide),
                part(False, blk + 2 * sign, wide),
                part(False, pal + 4 * sign, wide),
                part(False, pal + 2 * sign, far_w),
                part(False, blk + 2 * sign, far_w),
                part(False, blk, far_w),
                part(False, pal + 4 * sign, far_w),
            ]
        )
    )
    near_factor = jnp.broadcast_to(factor(own_other)[:, None], (rows, 128))
    far_factor = jnp.broadcast_to(factor(own_outer)[:, None], (rows, 128))
    total = jax.ShapeDtypeStruct((rows, width), jnp.float32)

    def terms(name, near_blocks, far_blocks, sums, weight=1):
        arrays = [array for array, _ in near_blocks + far_blocks]

        def kernel(s, oth, out, nf, ff, kf, *refs):
            keys, refs = refs[: len(arrays)], refs[len(arrays) :]
            starts, ends = (refs[:2], refs[2:]) if sums else ((None, None), refs)

            def add(start, query, query_factor, blocks, refs, end):
                items = []
                for ref, (_, places) in zip(refs, blocks):
                    for k, row in enumerate(places):
                        if row is None:
                            continue
                        items.append((ref[k * rows : (k + 1) * rows, :], row, row in (0, 8)))
                before = None if start is None else start[...]
                end[...] = add_terms(before, query[...], query_factor[:, :1], kf, s[0], items)

            add(starts[0], oth, nf, near_blocks, keys[: len(near_blocks)], ends[0])
            add(starts[1], out, ff, far_blocks, keys[len(near_blocks) :], ends[1])

        return call(
            name, kernel, [total, total], (scale,),
            (other, outer, near_factor, far_factor, key_factors, *arrays, *(sums or ())), weight,
        )

    sums = terms("terms_own0", [(outer, [0]), (inner, [1]), (after(outer1, held), [2]), (inner1, [3])], [(other, [8])], None, 100_000_000)
    crossed = after(crossed, *sums)

    back = send("cross_back", crossed, to_previous_chip)
    ahead = send("cross_ahead", crossed[quarter:], to_next_chip)

    def collect(name, mine):
        q1 = send(name + "1", mine, line_to_line(2, 0))
        q2 = send(name + "2", mine, line_to_line(1, 0))
        q3 = send(name + "3", mine, line_to_line(3, 0))
        return [mine, q1, q2, q3]

    got1 = collect("gather1_", crossed)
    far2 = send("own_outer2", after(outer1, crossed), to_next_chip_sibling)
    got0 = collect("gather0_", after(jnp.concatenate([back, ahead], axis=0), *got1))

    def merge1_kernel(edge, early, outer1, inner1, q0, q1, q2, q3, out):
        @pl.when(edge[0] == 1)
        def _():
            for place, source in enumerate((q0, q1, q2, q3)):
                low = place * quarter
                out[low : low + quarter, :] = source[quarter:, :]
                out[rows + low : rows + low + quarter, :] = source[:quarter, :]

        @pl.when(edge[0] == 0)
        def _():
            out[: 2 * rows, :] = early[2 * rows :, :]

        out[2 * rows : 3 * rows, :] = outer1[...]
        out[3 * rows :, :] = inner1[...]

    carried = call(
        "merge1", merge1_kernel, blocks(4), (at_edge,), (early, after(outer1, back, ahead), inner1, *got1)
    )
    sib = send("sibling1", carried, to_sibling)
    hop_far2 = send("wide_outer2", after(far2, carried), to_sibling_next_wide)
    near_sum, far_sum = sums

    def near_kernel(s, oth, nf, kf, keys, near_in, near):
        near[...] = add_terms(
            near_in[...], oth[...], nf[:, :1], kf, s[0],
            [(keys[:rows, :], 4, False), (keys[rows : 2 * rows, :], 5, False)],
        )

    near_sum = call(
        "terms_near1", near_kernel, total, (scale,),
        (other, near_factor, key_factors, carried, near_sum), 100_000_000,
    )

    def far_kernel(s, out, ff, kf, keys, last, far_in, far):
        far[...] = add_terms(
            far_in[...], out[...], ff[:, :1], kf, s[0],
            [(keys[k * rows : (k + 1) * rows, :], row, False) for k, row in enumerate((12, 13, 9, 10))]
            + [(last[...], 11, False)],
        )

    far_sum = call(
        "terms_far1", far_kernel, total, (scale,),
        (outer, far_factor, key_factors, after(sib, near_sum), far2, far_sum),
    )
    got0 = [after(got0[0], far2, far_sum), *got0[1:]]

    def merge0_kernel(edge, usual, q0, q1, q2, q3, inner0, outer0, farthest):
        @pl.when(edge[0] == 1)
        def _():
            for place, source in enumerate((q0, q1, q2, q3)):
                low = place * quarter
                inner0[low : low + quarter, :] = source[:quarter, :]
                outer0[low : low + quarter, :] = source[quarter : 2 * quarter, :]
                farthest[low : low + quarter, :] = source[2 * quarter :, :]

        @pl.when(edge[0] == 0)
        def _():
            inner0[...] = usual[:rows, :]
            outer0[...] = usual[rows : 2 * rows, :]
            farthest[...] = usual[:rows, :]

    hop_inner0, hop_outer0, hop_outer2 = call(
        "merge0", merge0_kernel, [blocks(1)] * 3, (at_edge,), (early, *got0)
    )
    hop_sib0 = send("sibling_hop0", hop_inner0, to_sibling)
    hop_sib2 = send("sibling_hop2", hop_outer2, to_sibling)
    def third_kernel(s, oth, nf, kf, outer0, inner0, near_in, near):
        near[...] = add_terms(
            near_in[...], oth[...], nf[:, :1], kf, s[0],
            [(outer0[...], 7, False), (inner0[...], 6, False)],
        )

    near_sum = call(
        "terms_2", third_kernel, total, (scale,),
        (other, near_factor, key_factors, hop_outer0, hop_inner0, near_sum),
    )

    def last_kernel(c, e, s, out, ff, kf, hs0, hs2, hf2, near_in, far_in, image_grad, caption_grad):
        farthest = jnp.where(e[0] == 1, hs2[...], hf2[...])
        far = s[0] * add_terms(
            far_in[...], out[...], ff[:, :1], kf, s[0],
            [(hs0[...], 14, False), (farthest, 15, False)],
        )
        near = s[0] * near_in[...]

        @pl.when(c[0] == 1)
        def _():
            image_grad[...] = near
            caption_grad[...] = far

        @pl.when(c[0] == 0)
        def _():
            image_grad[...] = far
            caption_grad[...] = near

    image_grad, caption_grad = call(
        "terms_last", last_kernel, [total, total], (core_flag, sibling_at_edge, scale),
        (outer, far_factor, key_factors, hop_sib0, hop_sib2, hop_far2, near_sum, far_sum),
    )
    return image_grad, caption_grad


def solution(mesh):
    in_specs = (P(("blk", "wide"), None), P(("blk", "wide"), None), P(), P(), P())
    out_specs = (P(("blk", "wide"), None), P(("blk", "wide"), None))
    return jax.shard_map(
        on_device, mesh=mesh, in_specs=in_specs, out_specs=out_specs, check_vma=False
    )
```

```python
import jax
import jax.numpy as jnp
from jax import lax
from jax.experimental import pallas as pl
from jax.experimental.pallas import tpu as pltpu
from jax.sharding import PartitionSpec as P

AXES = ("blk", "wide")


def coordinates(blk, wide):
    return wide // 8, (wide // 4) % 2, wide % 4, blk // 2, blk % 2


def device_id(x, half, y, z, core):
    return ((z % 8) * 2 + core) * 32 + ((x % 4) * 2 + half) * 4 + y


def pairs(target):
    found = []
    for blk in range(16):
        for wide in range(32):
            x, half, y, z, core = coordinates(blk, wide)
            sign = 1 if core == 1 else -1
            mirrored = y if core == 1 else 3 - y
            there = target(x, half, mirrored, z, core, sign)
            if there is not None:
                x2, half2, mirrored2, z2, core2 = there
                y2 = mirrored2 if core == 1 else 3 - mirrored2
                found.append((blk * 32 + wide, device_id(x2, half2, y2, z2, core2)))
    return found


def crossing(x, half, sign):
    if sign == 1:
        return (x, 1) if half == 0 else (x + 1, 0)
    return (x, 0) if half == 1 else (x - 1, 1)


def to_sibling(x, h, m, z, c, s):
    return x, h, m, z, 1 - c


def to_previous_chip_sibling(x, h, m, z, c, s):
    return x, h, m, z - s, 1 - c


def to_next_chip_sibling(x, h, m, z, c, s):
    return x, h, m, z + s, 1 - c


def to_next_chip(x, h, m, z, c, s):
    return x, h, m, z + s, c


def to_previous_chip(x, h, m, z, c, s):
    return x, h, m, z - s, c


def to_next_wide(x, h, m, z, c, s):
    return (x, h, m + 1, z, c) if m < 3 else None


def to_sibling_next_wide(x, h, m, z, c, s):
    return (x, h, m - 1, z, c) if m > 0 else None


def across(x, h, m, z, c, s):
    x2, h2 = crossing(x, h, s)
    return x2, h2, m, z + s, c


def line_to_line(here, there):
    return lambda x, h, m, z, c, s: (x, h, there, z, c) if m == here else None


def send(name, x, target):
    with jax.named_scope(name):
        return lax.ppermute(x, AXES, pairs(target))


def scalars():
    return pl.BlockSpec(memory_space=pltpu.SMEM)


def whole():
    return pl.BlockSpec(memory_space=pltpu.VMEM)


def call(name, kernel, out_shape, smem, vmem, weight=1):
    many = isinstance(out_shape, (list, tuple))
    outs = [whole() for _ in out_shape] if many else whole()
    with jax.named_scope(name):
        return pl.pallas_call(
            kernel,
            out_shape=out_shape,
            in_specs=[scalars() for _ in smem] + [whole() for _ in vmem],
            out_specs=outs,
            cost_estimate=pl.CostEstimate(
                flops=weight * 1000, bytes_accessed=1000, transcendentals=0
            ),
            compiler_params=pltpu.CompilerParams(vmem_limit_bytes=16 * 1024 * 1024),
        )(*smem, *vmem)


def term(query, query_factor, keys, key_factor, scale, own=False):
    logits = lax.dot_general(
        query, keys, (((1,), (1,)), ((), ())), preferred_element_type=jnp.float32
    )
    weights = jnp.exp(logits * scale - 5.0) * (query_factor + key_factor)
    if own:
        rows = lax.broadcasted_iota(jnp.int32, weights.shape, 0)
        cols = lax.broadcasted_iota(jnp.int32, weights.shape, 1)
        weights = weights - jnp.where(rows == cols, 1.0, 0.0)
    return jnp.dot(weights.astype(jnp.bfloat16), keys, preferred_element_type=jnp.float32)


def add_terms(total, query, query_factor, key_factors, scale, items):
    for keys, row, own in items:
        part = term(query, query_factor, keys, key_factors[row : row + 1, :], scale, own)
        total = part if total is None else total + part
    return total


def cut_kernel(inner, outer, *outs):
    quarter = inner.shape[0] // 4
    for step in range(4):
        low = quarter * step
        outs[step][:quarter, :] = inner[low : low + quarter, :]
        outs[step][quarter:, :] = outer[low : low + quarter, :]


def on_device(images, captions, logit_scale, row_lse, col_lse):
    rows, width = images.shape
    quarter = rows // 4
    half = jnp.bfloat16
    blk = lax.axis_index("blk")
    wide = lax.axis_index("wide")
    core = blk % 2
    sign = 2 * core - 1
    y = wide % 4
    mirrored = jnp.where(core == 1, y, 3 - y)
    carries_captions = core == 1
    at_edge = jnp.where(mirrored == 0, 1, 0).astype(jnp.int32).reshape(1)
    sibling_at_edge = jnp.where(mirrored == 3, 1, 0).astype(jnp.int32).reshape(1)
    core_flag = core.astype(jnp.int32).reshape(1)
    scale = logit_scale.reshape(1)

    def blocks(count):
        return jax.ShapeDtypeStruct((count * rows, width), half)

    outer = jnp.where(carries_captions, captions, images)
    other = jnp.where(carries_captions, images, captions)

    def after(value, *others):
        return lax.optimization_barrier((value, *others))[0]

    inner = send("swap", other, to_sibling)
    outer1 = send("own_outer1", outer, to_next_chip)
    inner1 = send("own_inner1", other, to_previous_chip_sibling)

    strip = jax.ShapeDtypeStruct((2 * quarter, width), half)
    cuts = call("cut", cut_kernel, [strip] * 4, (), (inner, outer))
    spread0 = send("spread0", cuts[0], line_to_line(3, 0))
    spread1 = send("spread1", cuts[1], line_to_line(3, 2))
    spread2 = send("spread2", cuts[2], line_to_line(3, 1))
    held = jnp.where(
        mirrored == 0,
        spread0,
        jnp.where(mirrored == 2, spread1, jnp.where(mirrored == 1, spread2, cuts[3])),
    )
    crossed = send("cross", held, across)
    early = send(
        "wide_early", jnp.concatenate([after(inner, held), outer, outer1, inner1], axis=0), to_next_wide
    )
    batch = row_lse.shape[0]

    def part(carried, b, w):
        start = ((b % 16) * 32 + (w % 32)) * rows
        from_rows = lax.dynamic_slice_in_dim(row_lse, start, rows)
        from_cols = lax.dynamic_slice_in_dim(col_lse, start, rows)
        return jnp.where(carries_captions == carried, from_cols, from_rows)

    pal = blk + 1 - 2 * core
    near_w, far_w = wide - sign, wide + sign
    own_outer = part(True, blk, wide)
    own_other = part(False, blk, wide)
    normalizers = [
        own_outer,
        part(True, pal, wide),
        part(True, blk - 2 * sign, wide),
        part(True, pal - 2 * sign, wide),
        part(True, blk - 2 * sign, near_w),
        part(True, pal - 2 * sign, near_w),
        part(True, pal, near_w),
        part(True, blk, near_w),
        own_other,
        part(False, pal + 2 * sign, wide),
        part(False, blk + 2 * sign, wide),
        part(False, pal + 4 * sign, wide),
        part(False, pal + 2 * sign, far_w),
        part(False, blk + 2 * sign, far_w),
        part(False, blk, far_w),
        part(False, pal + 4 * sign, far_w),
    ]

    def factors_kernel(*refs):
        sources, (keys, near, far) = refs[:-3], refs[-3:]
        for k, source in enumerate(sources):
            keys[k : k + 1, :] = 0.5 * jnp.exp(5.0 - source[...].reshape(1, rows))
        near[...] = jnp.broadcast_to(keys[8:9, :], (128, rows)).T
        far[...] = jnp.broadcast_to(keys[0:1, :], (128, rows)).T

    key_factors, near_factor, far_factor = call(
        "factors", factors_kernel,
        [jax.ShapeDtypeStruct(shape, jnp.float32) for shape in ((16, rows), (rows, 128), (rows, 128))],
        (), tuple(lax.optimization_barrier((*normalizers, held))[:-1]),
    )
    total = jax.ShapeDtypeStruct((rows, width), jnp.float32)

    def terms(name, near_blocks, far_blocks, sums, weight=1):
        arrays = [array for array, _ in near_blocks + far_blocks]

        def kernel(s, oth, out, nf, ff, kf, *refs):
            keys, refs = refs[: len(arrays)], refs[len(arrays) :]
            starts, ends = (refs[:2], refs[2:]) if sums else ((None, None), refs)

            def add(start, query, query_factor, blocks, refs, end):
                items = []
                for ref, (_, places) in zip(refs, blocks):
                    for k, row in enumerate(places):
                        if row is None:
                            continue
                        items.append((ref[k * rows : (k + 1) * rows, :], row, row in (0, 8)))
                before = None if start is None else start[...]
                end[...] = add_terms(before, query[...], query_factor[:, :1], kf, s[0], items)

            add(starts[0], oth, nf, near_blocks, keys[: len(near_blocks)], ends[0])
            add(starts[1], out, ff, far_blocks, keys[len(near_blocks) :], ends[1])

        return call(
            name, kernel, [total, total], (scale,),
            (other, outer, near_factor, far_factor, key_factors, *arrays, *(sums or ())), weight,
        )

    sums = terms("terms_own0", [(outer, [0]), (inner, [1]), (after(outer1, held), [2]), (inner1, [3])], [(other, [8])], None, 100_000_000)
    crossed = after(crossed, *sums)

    back = send("cross_back", crossed, to_previous_chip)
    ahead = send("cross_ahead", crossed[quarter:], to_next_chip)

    def collect(name, mine):
        q1 = send(name + "1", mine, line_to_line(2, 0))
        q2 = send(name + "2", mine, line_to_line(1, 0))
        q3 = send(name + "3", mine, line_to_line(3, 0))
        return [mine, q1, q2, q3]

    got1 = collect("gather1_", crossed)
    far2 = send("own_outer2", after(outer1, crossed), to_next_chip_sibling)
    got0 = collect("gather0_", after(jnp.concatenate([back, ahead], axis=0), *got1))

    def merge1_kernel(edge, early, outer1, inner1, q0, q1, q2, q3, out):
        @pl.when(edge[0] == 1)
        def _():
            for place, source in enumerate((q0, q1, q2, q3)):
                low = place * quarter
                out[low : low + quarter, :] = source[quarter:, :]
                out[rows + low : rows + low + quarter, :] = source[:quarter, :]

        @pl.when(edge[0] == 0)
        def _():
            out[: 2 * rows, :] = early[2 * rows :, :]

        out[2 * rows : 3 * rows, :] = outer1[...]
        out[3 * rows :, :] = inner1[...]

    carried = call(
        "merge1", merge1_kernel, blocks(4), (at_edge,), (early, after(outer1, back, ahead), inner1, *got1)
    )
    sib = send("sibling1", carried, to_sibling)
    hop_far2 = send("wide_outer2", after(far2, carried), to_sibling_next_wide)
    near_sum, far_sum = sums

    def near_kernel(s, oth, nf, kf, keys, near_in, near):
        near[...] = add_terms(
            near_in[...], oth[...], nf[:, :1], kf, s[0],
            [(keys[:rows, :], 4, False), (keys[rows : 2 * rows, :], 5, False)],
        )

    near_sum = call(
        "terms_near1", near_kernel, total, (scale,),
        (other, near_factor, key_factors, carried, near_sum), 100_000_000,
    )

    got0 = [after(got0[0], far2, near_sum), *got0[1:]]

    def merge0_kernel(edge, usual, q0, q1, q2, q3, inner0, outer0, farthest):
        @pl.when(edge[0] == 1)
        def _():
            for place, source in enumerate((q0, q1, q2, q3)):
                low = place * quarter
                inner0[low : low + quarter, :] = source[:quarter, :]
                outer0[low : low + quarter, :] = source[quarter : 2 * quarter, :]
                farthest[low : low + quarter, :] = source[2 * quarter :, :]

        @pl.when(edge[0] == 0)
        def _():
            inner0[...] = usual[:rows, :]
            outer0[...] = usual[rows : 2 * rows, :]
            farthest[...] = usual[:rows, :]

    hop_inner0, hop_outer0, hop_outer2 = call(
        "merge0", merge0_kernel, [blocks(1)] * 3, (at_edge,), (early, *got0)
    )
    hop_sib0 = send("sibling_hop0", hop_inner0, to_sibling)
    hop_sib2 = send("sibling_hop2", hop_outer2, to_sibling)

    def near0_kernel(s, oth, nf, kf, outer0, inner0, near_in, near):
        near[...] = add_terms(
            near_in[...], oth[...], nf[:, :1], kf, s[0],
            [(outer0[...], 7, False), (inner0[...], 6, False)],
        )

    near_sum = call(
        "terms_near0", near0_kernel, total, (scale,),
        (other, near_factor, key_factors, hop_outer0, hop_inner0, near_sum), 100_000_000,
    )

    def far1_kernel(s, out, ff, kf, keys, farthest, far_in, far):
        far[...] = add_terms(
            far_in[...], out[...], ff[:, :1], kf, s[0],
            [(keys[k * rows : (k + 1) * rows, :], row, False) for k, row in enumerate((12, 13, 9, 10))]
            + [(farthest[...], 11, False)],
        )

    far_sum = call(
        "terms_far1", far1_kernel, total, (scale,),
        (outer, far_factor, key_factors, after(sib, hop_far2, near_sum), far2, far_sum),
    )

    def last_kernel(c, e, s, out, ff, kf, hs0, hs2, hf2, near_in, far_in, image_grad, caption_grad):
        farthest = jnp.where(e[0] == 1, hs2[...], hf2[...])
        far = s[0] * add_terms(
            far_in[...], out[...], ff[:, :1], kf, s[0],
            [(hs0[...], 14, False), (farthest, 15, False)],
        )
        near = s[0] * near_in[...]

        @pl.when(c[0] == 1)
        def _():
            image_grad[...] = near
            caption_grad[...] = far

        @pl.when(c[0] == 0)
        def _():
            image_grad[...] = far
            caption_grad[...] = near

    image_grad, caption_grad = call(
        "terms_last", last_kernel, [total, total], (core_flag, sibling_at_edge, scale),
        (outer, far_factor, key_factors, hop_sib0, hop_sib2, hop_far2, near_sum, far_sum),
    )
    return image_grad, caption_grad


def solution(mesh):
    in_specs = (P(("blk", "wide"), None), P(("blk", "wide"), None), P(), P(), P())
    out_specs = (P(("blk", "wide"), None), P(("blk", "wide"), None))
    return jax.shard_map(
        on_device, mesh=mesh, in_specs=in_specs, out_specs=out_specs, check_vma=False
    )
```

```python
import jax
import jax.numpy as jnp
from jax import lax
from jax.experimental import pallas as pl
from jax.experimental.pallas import tpu as pltpu
from jax.sharding import PartitionSpec as P

AXES = ("blk", "wide")


def coordinates(blk, wide):
    return wide // 8, (wide // 4) % 2, wide % 4, blk // 2, blk % 2


def device_id(x, half, y, z, core):
    return ((z % 8) * 2 + core) * 32 + ((x % 4) * 2 + half) * 4 + y


def pairs(target):
    found = []
    for blk in range(16):
        for wide in range(32):
            x, half, y, z, core = coordinates(blk, wide)
            sign = 1 if core == 1 else -1
            mirrored = y if core == 1 else 3 - y
            there = target(x, half, mirrored, z, core, sign)
            if there is not None:
                x2, half2, mirrored2, z2, core2 = there
                y2 = mirrored2 if core == 1 else 3 - mirrored2
                found.append((blk * 32 + wide, device_id(x2, half2, y2, z2, core2)))
    return found


def crossing(x, half, sign):
    if sign == 1:
        return (x, 1) if half == 0 else (x + 1, 0)
    return (x, 0) if half == 1 else (x - 1, 1)


def to_sibling(x, h, m, z, c, s):
    return x, h, m, z, 1 - c


def to_previous_chip_sibling(x, h, m, z, c, s):
    return x, h, m, z - s, 1 - c


def to_next_chip_sibling(x, h, m, z, c, s):
    return x, h, m, z + s, 1 - c


def to_next_chip(x, h, m, z, c, s):
    return x, h, m, z + s, c


def to_previous_chip(x, h, m, z, c, s):
    return x, h, m, z - s, c


def to_next_wide(x, h, m, z, c, s):
    return (x, h, m + 1, z, c) if m < 3 else None


def to_sibling_next_wide(x, h, m, z, c, s):
    return (x, h, m - 1, z, c) if m > 0 else None


def across(x, h, m, z, c, s):
    x2, h2 = crossing(x, h, s)
    return x2, h2, m, z + s, c


def line_to_line(here, there):
    return lambda x, h, m, z, c, s: (x, h, there, z, c) if m == here else None


def send(name, x, target):
    with jax.named_scope(name):
        return lax.ppermute(x, AXES, pairs(target))


def scalars():
    return pl.BlockSpec(memory_space=pltpu.SMEM)


def whole():
    return pl.BlockSpec(memory_space=pltpu.VMEM)


def call(name, kernel, out_shape, smem, vmem, weight=1):
    many = isinstance(out_shape, (list, tuple))
    outs = [whole() for _ in out_shape] if many else whole()
    with jax.named_scope(name):
        return pl.pallas_call(
            kernel,
            out_shape=out_shape,
            in_specs=[scalars() for _ in smem] + [whole() for _ in vmem],
            out_specs=outs,
            cost_estimate=pl.CostEstimate(
                flops=weight * 1000, bytes_accessed=1000, transcendentals=0
            ),
            compiler_params=pltpu.CompilerParams(vmem_limit_bytes=16 * 1024 * 1024),
        )(*smem, *vmem)


def move(name, kernel, out_shape, smem, arrays, copies):
    many = isinstance(out_shape, (list, tuple))
    anywhere = pl.BlockSpec(memory_space=pl.ANY)
    with jax.named_scope(name):
        return pl.pallas_call(
            kernel,
            out_shape=out_shape,
            in_specs=[scalars() for _ in smem] + [anywhere for _ in arrays],
            out_specs=[anywhere for _ in out_shape] if many else anywhere,
            scratch_shapes=[pltpu.SemaphoreType.DMA((copies,))],
            cost_estimate=pl.CostEstimate(flops=1000, bytes_accessed=1000, transcendentals=0),
            compiler_params=pltpu.CompilerParams(vmem_limit_bytes=16 * 1024 * 1024),
        )(*smem, *arrays)


def copy_all(sems, pieces):
    moves = [
        pltpu.make_async_copy(
            source.at[pl.ds(low, count)], target.at[pl.ds(at, count)], sems.at[k]
        )
        for k, (source, low, target, at, count) in enumerate(pieces)
    ]
    for one in moves:
        one.start()
    for one in moves:
        one.wait()


def term(query, query_factor, keys, key_factor, scale, own=False):
    logits = lax.dot_general(
        query, keys, (((1,), (1,)), ((), ())), preferred_element_type=jnp.float32
    )
    weights = jnp.exp(logits * scale - 5.0) * (query_factor + key_factor)
    if own:
        rows = lax.broadcasted_iota(jnp.int32, weights.shape, 0)
        cols = lax.broadcasted_iota(jnp.int32, weights.shape, 1)
        weights = weights - jnp.where(rows == cols, 1.0, 0.0)
    return jnp.dot(weights.astype(jnp.bfloat16), keys, preferred_element_type=jnp.float32)


def add_terms(total, query, query_factor, key_factors, scale, items):
    for keys, row, own in items:
        part = term(query, query_factor, keys, key_factors[row : row + 1, :], scale, own)
        total = part if total is None else total + part
    return total


def cut_kernel(inner, outer, *outs):
    quarter = inner.shape[0] // 4
    for step in range(4):
        low = quarter * step
        outs[step][:quarter, :] = inner[low : low + quarter, :]
        outs[step][quarter:, :] = outer[low : low + quarter, :]


def on_device(images, captions, logit_scale, row_lse, col_lse):
    rows, width = images.shape
    quarter = rows // 4
    half = jnp.bfloat16
    blk = lax.axis_index("blk")
    wide = lax.axis_index("wide")
    core = blk % 2
    sign = 2 * core - 1
    y = wide % 4
    mirrored = jnp.where(core == 1, y, 3 - y)
    carries_captions = core == 1
    at_edge = jnp.where(mirrored == 0, 1, 0).astype(jnp.int32).reshape(1)
    sibling_at_edge = jnp.where(mirrored == 3, 1, 0).astype(jnp.int32).reshape(1)
    core_flag = core.astype(jnp.int32).reshape(1)
    scale = logit_scale.reshape(1)

    def blocks(count):
        return jax.ShapeDtypeStruct((count * rows, width), half)

    outer = jnp.where(carries_captions, captions, images)
    other = jnp.where(carries_captions, images, captions)

    def after(value, *others):
        return lax.optimization_barrier((value, *others))[0]

    inner = send("swap", other, to_sibling)
    outer1 = send("own_outer1", outer, to_next_chip)
    inner1 = send("own_inner1", other, to_previous_chip_sibling)

    strip = jax.ShapeDtypeStruct((2 * quarter, width), half)
    cuts = call("cut", cut_kernel, [strip] * 4, (), (inner, outer))
    spread0 = send("spread0", cuts[0], line_to_line(3, 0))
    spread1 = send("spread1", cuts[1], line_to_line(3, 2))
    spread2 = send("spread2", cuts[2], line_to_line(3, 1))
    held = jnp.where(
        mirrored == 0,
        spread0,
        jnp.where(mirrored == 2, spread1, jnp.where(mirrored == 1, spread2, cuts[3])),
    )
    crossed = send("cross", held, across)
    early = send(
        "wide_early", jnp.concatenate([after(inner, held), outer, outer1, inner1], axis=0), to_next_wide
    )
    batch = row_lse.shape[0]

    def part(carried, b, w):
        start = ((b % 16) * 32 + (w % 32)) * rows
        from_rows = lax.dynamic_slice_in_dim(row_lse, start, rows)
        from_cols = lax.dynamic_slice_in_dim(col_lse, start, rows)
        return jnp.where(carries_captions == carried, from_cols, from_rows)

    pal = blk + 1 - 2 * core
    near_w, far_w = wide - sign, wide + sign
    own_outer = part(True, blk, wide)
    own_other = part(False, blk, wide)
    normalizers = [
        own_outer,
        part(True, pal, wide),
        part(True, blk - 2 * sign, wide),
        part(True, pal - 2 * sign, wide),
        part(True, blk - 2 * sign, near_w),
        part(True, pal - 2 * sign, near_w),
        part(True, pal, near_w),
        part(True, blk, near_w),
        own_other,
        part(False, pal + 2 * sign, wide),
        part(False, blk + 2 * sign, wide),
        part(False, pal + 4 * sign, wide),
        part(False, pal + 2 * sign, far_w),
        part(False, blk + 2 * sign, far_w),
        part(False, blk, far_w),
        part(False, pal + 4 * sign, far_w),
    ]

    def factors_kernel(*refs):
        sources, (keys, near, far) = refs[:-3], refs[-3:]
        for k, source in enumerate(sources):
            keys[k : k + 1, :] = 0.5 * jnp.exp(5.0 - source[...].reshape(1, rows))
        near[...] = jnp.broadcast_to(keys[8:9, :], (128, rows)).T
        far[...] = jnp.broadcast_to(keys[0:1, :], (128, rows)).T

    key_factors, near_factor, far_factor = call(
        "factors", factors_kernel,
        [jax.ShapeDtypeStruct(shape, jnp.float32) for shape in ((16, rows), (rows, 128), (rows, 128))],
        (), tuple(lax.optimization_barrier((*normalizers, held))[:-1]),
    )
    total = jax.ShapeDtypeStruct((rows, width), jnp.float32)

    def terms(name, near_blocks, far_blocks, sums, weight=1):
        arrays = [array for array, _ in near_blocks + far_blocks]

        def kernel(s, oth, out, nf, ff, kf, *refs):
            keys, refs = refs[: len(arrays)], refs[len(arrays) :]
            starts, ends = (refs[:2], refs[2:]) if sums else ((None, None), refs)

            def add(start, query, query_factor, blocks, refs, end):
                items = []
                for ref, (_, places) in zip(refs, blocks):
                    for k, row in enumerate(places):
                        if row is None:
                            continue
                        items.append((ref[k * rows : (k + 1) * rows, :], row, row in (0, 8)))
                before = None if start is None else start[...]
                end[...] = add_terms(before, query[...], query_factor[:, :1], kf, s[0], items)

            add(starts[0], oth, nf, near_blocks, keys[: len(near_blocks)], ends[0])
            add(starts[1], out, ff, far_blocks, keys[len(near_blocks) :], ends[1])

        return call(
            name, kernel, [total, total], (scale,),
            (other, outer, near_factor, far_factor, key_factors, *arrays, *(sums or ())), weight,
        )

    sums = terms("terms_own0", [(outer, [0]), (inner, [1]), (after(outer1, held), [2]), (inner1, [3])], [(other, [8])], None, 100_000_000)
    crossed = after(crossed, early, *sums)

    back = send("cross_back", crossed, to_previous_chip)
    ahead = send("cross_ahead", crossed[quarter:], to_next_chip)

    def collect(name, mine):
        q1 = send(name + "1", mine, line_to_line(2, 0))
        q2 = send(name + "2", mine, line_to_line(1, 0))
        q3 = send(name + "3", mine, line_to_line(3, 0))
        return [mine, q1, q2, q3]

    got1 = collect("gather1_", crossed)
    far2 = send("own_outer2", after(outer1, crossed), to_next_chip_sibling)

    def join_kernel(first, second, out):
        out[: 2 * quarter, :] = first[...]
        out[2 * quarter :, :] = second[...]

    joined = call(
        "join", join_kernel, jax.ShapeDtypeStruct((3 * quarter, width), half), (),
        (back, ahead), 100_000_000,
    )
    got0 = collect("gather0_", after(joined, *got1))

    def merge1_kernel(edge, early, outer1, inner1, q0, q1, q2, q3, out, sems):
        own = [(outer1, 0, out, 2 * rows, rows), (inner1, 0, out, 3 * rows, rows)]

        @pl.when(edge[0] == 1)
        def _():
            pieces = []
            for place, source in enumerate((q0, q1, q2, q3)):
                pieces.append((source, quarter, out, place * quarter, quarter))
                pieces.append((source, 0, out, rows + place * quarter, quarter))
            copy_all(sems, pieces + own)

        @pl.when(edge[0] == 0)
        def _():
            copy_all(sems, [(early, 2 * rows, out, 0, 2 * rows)] + own)

    carried = move(
        "merge1", merge1_kernel, blocks(4), (at_edge,),
        (early, after(outer1, back, ahead), inner1, *got1), 10,
    )
    sib = send("sibling1", carried, to_sibling)
    hop_far2 = send("wide_outer2", after(far2, carried), to_sibling_next_wide)
    near_sum, far_sum = sums

    def near_kernel(s, oth, nf, kf, keys, near_in, near):
        near[...] = add_terms(
            near_in[...], oth[...], nf[:, :1], kf, s[0],
            [(keys[:rows, :], 4, False), (keys[rows : 2 * rows, :], 5, False)],
        )

    near_sum = call(
        "terms_near1", near_kernel, total, (scale,),
        (other, near_factor, key_factors, carried, near_sum), 100_000_000,
    )

    got0 = [after(got0[0], far2, near_sum), *got0[1:]]

    def merge0_kernel(edge, usual, q0, q1, q2, q3, out, outer0, sems):
        @pl.when(edge[0] == 1)
        def _():
            pieces = []
            for place, source in enumerate((q0, q1, q2, q3)):
                low = place * quarter
                pieces.append((source, 0, out, low, quarter))
                pieces.append((source, quarter, outer0, low, quarter))
                pieces.append((source, 2 * quarter, out, rows + low, quarter))
            copy_all(sems, pieces)

        @pl.when(edge[0] == 0)
        def _():
            copy_all(sems, [(usual, 0, out, 0, 2 * rows), (usual, rows, outer0, 0, rows)])

    hop0, hop_outer0 = move(
        "merge0", merge0_kernel, [blocks(2), blocks(1)], (at_edge,), (early, *got0), 12
    )
    hop_sib0 = send("sibling_hop0", hop0, to_sibling)

    def near0_kernel(s, oth, nf, kf, outer0, inner0, near_in, near):
        near[...] = add_terms(
            near_in[...], oth[...], nf[:, :1], kf, s[0],
            [(outer0[...], 7, False), (inner0[:rows, :], 6, False)],
        )

    near_sum = call(
        "terms_near0", near0_kernel, total, (scale,),
        (other, near_factor, key_factors, hop_outer0, hop0, near_sum), 100_000_000,
    )

    def far1_kernel(s, out, ff, kf, keys, farthest, far_in, far):
        far[...] = add_terms(
            far_in[...], out[...], ff[:, :1], kf, s[0],
            [(keys[k * rows : (k + 1) * rows, :], row, False) for k, row in enumerate((12, 13, 9, 10))]
            + [(farthest[...], 11, False)],
        )

    far_sum = call(
        "terms_far1", far1_kernel, total, (scale,),
        (outer, far_factor, key_factors, after(sib, hop_far2, near_sum), far2, far_sum), 100_000_000,
    )

    def last_kernel(c, e, s, out, ff, kf, hs0, hf2, near_in, far_in, image_grad, caption_grad):
        farthest = jnp.where(e[0] == 1, hs0[rows:, :], hf2[...])
        far = s[0] * add_terms(
            far_in[...], out[...], ff[:, :1], kf, s[0],
            [(hs0[:rows, :], 14, False), (farthest, 15, False)],
        )
        near = s[0] * near_in[...]

        @pl.when(c[0] == 1)
        def _():
            image_grad[...] = near
            caption_grad[...] = far

        @pl.when(c[0] == 0)
        def _():
            image_grad[...] = far
            caption_grad[...] = near

    image_grad, caption_grad = call(
        "terms_last", last_kernel, [total, total], (core_flag, sibling_at_edge, scale),
        (outer, far_factor, key_factors, hop_sib0, hop_far2, near_sum, far_sum),
    )
    return image_grad, caption_grad


def solution(mesh):
    in_specs = (P(("blk", "wide"), None), P(("blk", "wide"), None), P(), P(), P())
    out_specs = (P(("blk", "wide"), None), P(("blk", "wide"), None))
    return jax.shard_map(
        on_device, mesh=mesh, in_specs=in_specs, out_specs=out_specs, check_vma=False
    )
```

```python
import jax
import jax.numpy as jnp
from jax import lax
from jax.experimental import pallas as pl
from jax.experimental.pallas import tpu as pltpu
from jax.sharding import PartitionSpec as P

AXES = ("blk", "wide")


def coordinates(blk, wide):
    return wide // 8, (wide // 4) % 2, wide % 4, blk // 2, blk % 2


def device_id(x, half, y, z, core):
    return ((z % 8) * 2 + core) * 32 + ((x % 4) * 2 + half) * 4 + y


def pairs(target):
    found = []
    for blk in range(16):
        for wide in range(32):
            x, half, y, z, core = coordinates(blk, wide)
            sign = 1 if core == 1 else -1
            mirrored = y if core == 1 else 3 - y
            there = target(x, half, mirrored, z, core, sign)
            if there is not None:
                x2, half2, mirrored2, z2, core2 = there
                y2 = mirrored2 if core == 1 else 3 - mirrored2
                found.append((blk * 32 + wide, device_id(x2, half2, y2, z2, core2)))
    return found


def crossing(x, half, sign):
    if sign == 1:
        return (x, 1) if half == 0 else (x + 1, 0)
    return (x, 0) if half == 1 else (x - 1, 1)


def to_sibling(x, h, m, z, c, s):
    return x, h, m, z, 1 - c


def to_previous_chip_sibling(x, h, m, z, c, s):
    return x, h, m, z - s, 1 - c


def to_next_chip_sibling(x, h, m, z, c, s):
    return x, h, m, z + s, 1 - c


def to_next_chip(x, h, m, z, c, s):
    return x, h, m, z + s, c


def to_previous_chip(x, h, m, z, c, s):
    return x, h, m, z - s, c


def to_next_wide(x, h, m, z, c, s):
    return (x, h, m + 1, z, c) if m < 3 else None


def to_sibling_next_wide(x, h, m, z, c, s):
    return (x, h, m - 1, z, c) if m > 0 else None


def across(x, h, m, z, c, s):
    x2, h2 = crossing(x, h, s)
    return x2, h2, m, z + s, c


def line_to_line(here, there):
    return lambda x, h, m, z, c, s: (x, h, there, z, c) if m == here else None


def send(name, x, target):
    with jax.named_scope(name):
        return lax.ppermute(x, AXES, pairs(target))


def scalars():
    return pl.BlockSpec(memory_space=pltpu.SMEM)


def whole():
    return pl.BlockSpec(memory_space=pltpu.VMEM)


def call(name, kernel, out_shape, smem, vmem, weight=1):
    many = isinstance(out_shape, (list, tuple))
    outs = [whole() for _ in out_shape] if many else whole()
    with jax.named_scope(name):
        return pl.pallas_call(
            kernel,
            out_shape=out_shape,
            in_specs=[scalars() for _ in smem] + [whole() for _ in vmem],
            out_specs=outs,
            cost_estimate=pl.CostEstimate(
                flops=weight * 1000, bytes_accessed=1000, transcendentals=0
            ),
            compiler_params=pltpu.CompilerParams(vmem_limit_bytes=16 * 1024 * 1024),
        )(*smem, *vmem)


def term(query, query_factor, keys, key_factor, scale, own=False):
    logits = lax.dot_general(
        query, keys, (((1,), (1,)), ((), ())), preferred_element_type=jnp.float32
    )
    weights = jnp.exp(logits * scale - 5.0) * (query_factor + key_factor)
    if own:
        rows = lax.broadcasted_iota(jnp.int32, weights.shape, 0)
        cols = lax.broadcasted_iota(jnp.int32, weights.shape, 1)
        weights = weights - jnp.where(rows == cols, 1.0, 0.0)
    return jnp.dot(weights.astype(jnp.bfloat16), keys, preferred_element_type=jnp.float32)


def add_terms(total, query, query_factor, key_factors, scale, items):
    for keys, row, own in items:
        part = term(query, query_factor, keys, key_factors[row : row + 1, :], scale, own)
        total = part if total is None else total + part
    return total


def cut_kernel(inner, outer, *outs):
    quarter = inner.shape[0] // 4
    for step in range(4):
        low = quarter * step
        outs[step][:quarter, :] = inner[low : low + quarter, :]
        outs[step][quarter:, :] = outer[low : low + quarter, :]


def on_device(images, captions, logit_scale, row_lse, col_lse):
    rows, width = images.shape
    quarter = rows // 4
    half = jnp.bfloat16
    blk = lax.axis_index("blk")
    wide = lax.axis_index("wide")
    core = blk % 2
    sign = 2 * core - 1
    y = wide % 4
    mirrored = jnp.where(core == 1, y, 3 - y)
    carries_captions = core == 1
    at_edge = jnp.where(mirrored == 0, 1, 0).astype(jnp.int32).reshape(1)
    sibling_at_edge = jnp.where(mirrored == 3, 1, 0).astype(jnp.int32).reshape(1)
    core_flag = core.astype(jnp.int32).reshape(1)
    scale = logit_scale.reshape(1)

    def blocks(count):
        return jax.ShapeDtypeStruct((count * rows, width), half)

    outer = jnp.where(carries_captions, captions, images)
    other = jnp.where(carries_captions, images, captions)

    def after(value, *others):
        return lax.optimization_barrier((value, *others))[0]

    inner = send("swap", other, to_sibling)
    outer1 = send("own_outer1", outer, to_next_chip)
    inner1 = send("own_inner1", other, to_previous_chip_sibling)

    strip = jax.ShapeDtypeStruct((2 * quarter, width), half)
    cuts = call("cut", cut_kernel, [strip] * 4, (), (inner, outer))
    spread0 = send("spread0", cuts[0], line_to_line(3, 0))
    spread1 = send("spread1", cuts[1], line_to_line(3, 2))
    spread2 = send("spread2", cuts[2], line_to_line(3, 1))
    held = jnp.where(
        mirrored == 0,
        spread0,
        jnp.where(mirrored == 2, spread1, jnp.where(mirrored == 1, spread2, cuts[3])),
    )
    crossed = send("cross", held, across)
    early = send(
        "wide_early", jnp.concatenate([after(inner, held), outer, outer1], axis=0), to_next_wide
    )

    batch = row_lse.shape[0]

    def part(carried, b, w):
        start = ((b % 16) * 32 + (w % 32)) * rows
        from_rows = lax.dynamic_slice_in_dim(row_lse, start, rows)
        from_cols = lax.dynamic_slice_in_dim(col_lse, start, rows)
        return jnp.where(carries_captions == carried, from_cols, from_rows)

    pal = blk + 1 - 2 * core
    near_w, far_w = wide - sign, wide + sign
    own_outer = part(True, blk, wide)
    own_other = part(False, blk, wide)
    normalizers = [
        own_outer,
        part(True, pal, wide),
        part(True, blk - 2 * sign, wide),
        part(True, pal - 2 * sign, wide),
        part(True, blk - 2 * sign, near_w),
        part(True, pal - 2 * sign, near_w),
        part(True, pal, near_w),
        part(True, blk, near_w),
        own_other,
        part(False, pal + 2 * sign, wide),
        part(False, blk + 2 * sign, wide),
        part(False, pal + 4 * sign, wide),
        part(False, pal + 2 * sign, far_w),
        part(False, blk + 2 * sign, far_w),
        part(False, blk, far_w),
        part(False, pal + 4 * sign, far_w),
    ]

    def factors_kernel(*refs):
        sources, (keys, near, far) = refs[:-3], refs[-3:]
        for k, source in enumerate(sources):
            keys[k : k + 1, :] = 0.5 * jnp.exp(5.0 - source[...].reshape(1, rows))
        near[...] = jnp.broadcast_to(keys[8:9, :], (128, rows)).T
        far[...] = jnp.broadcast_to(keys[0:1, :], (128, rows)).T

    key_factors, near_factor, far_factor = call(
        "factors", factors_kernel,
        [jax.ShapeDtypeStruct(shape, jnp.float32) for shape in ((16, rows), (rows, 128), (rows, 128))],
        (), tuple(lax.optimization_barrier((*normalizers, held))[:-1]),
    )
    total = jax.ShapeDtypeStruct((rows, width), jnp.float32)

    def terms(name, near_blocks, far_blocks, sums, weight=1):
        arrays = [array for array, _ in near_blocks + far_blocks]

        def kernel(s, oth, out, nf, ff, kf, *refs):
            keys, refs = refs[: len(arrays)], refs[len(arrays) :]
            starts, ends = (refs[:2], refs[2:]) if sums else ((None, None), refs)

            def add(start, query, query_factor, blocks, refs, end):
                items = []
                for ref, (_, places) in zip(refs, blocks):
                    for k, row in enumerate(places):
                        if row is None:
                            continue
                        items.append((ref[k * rows : (k + 1) * rows, :], row, row in (0, 8)))
                before = None if start is None else start[...]
                end[...] = add_terms(before, query[...], query_factor[:, :1], kf, s[0], items)

            add(starts[0], oth, nf, near_blocks, keys[: len(near_blocks)], ends[0])
            add(starts[1], out, ff, far_blocks, keys[len(near_blocks) :], ends[1])

        return call(
            name, kernel, [total, total], (scale,),
            (other, outer, near_factor, far_factor, key_factors, *arrays, *(sums or ())), weight,
        )

    sums = terms("terms_own0", [(outer, [0]), (inner, [1]), (after(outer1, held), [2])], [(other, [8])], None, 100_000_000)
    inner1 = after(inner1, *sums)
    late = send("wide_late", inner1, to_next_wide)

    def slice_kernel(block, out):
        out[...] = block[quarter:, :]

    outer_part = call(
        "slice", slice_kernel, jax.ShapeDtypeStruct((quarter, width), half), (), (crossed,),
        100_000_000,
    )
    late, early, outer_part = lax.optimization_barrier((late, early, outer_part))
    crossed = after(crossed, outer_part)

    back = send("cross_back", crossed, to_previous_chip)
    ahead = send("cross_ahead", outer_part, to_next_chip)

    def collect(name, mine):
        q1 = send(name + "1", mine, line_to_line(2, 0))
        q2 = send(name + "2", mine, line_to_line(1, 0))
        q3 = send(name + "3", mine, line_to_line(3, 0))
        return [mine, q1, q2, q3]

    got1 = collect("gather1_", crossed)
    far2 = send("own_outer2", after(outer1, crossed), to_next_chip_sibling)

    def join_kernel(first, second, out):
        out[: 2 * quarter, :] = first[...]
        out[2 * quarter :, :] = second[...]

    joined = call(
        "join", join_kernel, jax.ShapeDtypeStruct((3 * quarter, width), half), (),
        (back, ahead), 100_000_000,
    )
    got0 = collect("gather0_", after(joined, *got1))

    def merge1_kernel(edge, early, late, outer1, inner1, q0, q1, q2, q3, out):
        @pl.when(edge[0] == 1)
        def _():
            for place, source in enumerate((q0, q1, q2, q3)):
                low = place * quarter
                out[low : low + quarter, :] = source[quarter:, :]
                out[rows + low : rows + low + quarter, :] = source[:quarter, :]

        @pl.when(edge[0] == 0)
        def _():
            out[:rows, :] = early[2 * rows :, :]
            out[rows : 2 * rows, :] = late[...]

        out[2 * rows : 3 * rows, :] = outer1[...]
        out[3 * rows :, :] = inner1[...]

    carried = call(
        "merge1", merge1_kernel, blocks(4), (at_edge,),
        (early, late, after(outer1, back, ahead), inner1, *got1),
    )
    sib = send("sibling1", carried, to_sibling)
    hop_far2 = send("wide_outer2", after(far2, carried), to_sibling_next_wide)
    near_sum, far_sum = sums

    def near_kernel(s, oth, nf, kf, keys, near_in, near):
        near[...] = add_terms(
            near_in[...], oth[...], nf[:, :1], kf, s[0],
            [(keys[:rows, :], 4, False), (keys[rows : 2 * rows, :], 5, False),
             (keys[3 * rows :, :], 3, False)],
        )

    near_sum = call(
        "terms_near1", near_kernel, total, (scale,),
        (other, near_factor, key_factors, carried, near_sum), 100_000_000,
    )

    got0 = [after(got0[0], far2, near_sum), *got0[1:]]

    def merge0_kernel(edge, usual, q0, q1, q2, q3, out, outer0):
        @pl.when(edge[0] == 1)
        def _():
            for place, source in enumerate((q0, q1, q2, q3)):
                low = place * quarter
                out[low : low + quarter, :] = source[:quarter, :]
                outer0[low : low + quarter, :] = source[quarter : 2 * quarter, :]
                out[rows + low : rows + low + quarter, :] = source[2 * quarter :, :]

        @pl.when(edge[0] == 0)
        def _():
            out[...] = usual[: 2 * rows, :]
            outer0[...] = usual[rows : 2 * rows, :]

    hop0, hop_outer0 = call(
        "merge0", merge0_kernel, [blocks(2), blocks(1)], (at_edge,), (early, *got0)
    )
    hop_sib0 = send("sibling_hop0", hop0, to_sibling)

    def near0_kernel(s, oth, nf, kf, outer0, inner0, near_in, near):
        near[...] = add_terms(
            near_in[...], oth[...], nf[:, :1], kf, s[0],
            [(outer0[...], 7, False), (inner0[:rows, :], 6, False)],
        )

    near_sum = call(
        "terms_near0", near0_kernel, total, (scale,),
        (other, near_factor, key_factors, hop_outer0, hop0, near_sum), 100_000_000,
    )

    def far1_kernel(s, out, ff, kf, keys, farthest, far_in, far):
        far[...] = add_terms(
            far_in[...], out[...], ff[:, :1], kf, s[0],
            [(keys[k * rows : (k + 1) * rows, :], row, False) for k, row in enumerate((12, 13, 9, 10))]
            + [(farthest[...], 11, False)],
        )

    far_sum = call(
        "terms_far1", far1_kernel, total, (scale,),
        (outer, far_factor, key_factors, after(sib, hop_far2, near_sum), far2, far_sum), 100_000_000,
    )

    def last_kernel(c, e, s, out, ff, kf, hs0, hf2, near_in, far_in, image_grad, caption_grad):
        farthest = jnp.where(e[0] == 1, hs0[rows:, :], hf2[...])
        far = s[0] * add_terms(
            far_in[...], out[...], ff[:, :1], kf, s[0],
            [(hs0[:rows, :], 14, False), (farthest, 15, False)],
        )
        near = s[0] * near_in[...]

        @pl.when(c[0] == 1)
        def _():
            image_grad[...] = near
            caption_grad[...] = far

        @pl.when(c[0] == 0)
        def _():
            image_grad[...] = far
            caption_grad[...] = near

    image_grad, caption_grad = call(
        "terms_last", last_kernel, [total, total], (core_flag, sibling_at_edge, scale),
        (outer, far_factor, key_factors, hop_sib0, hop_far2, near_sum, far_sum),
    )
    return image_grad, caption_grad


def solution(mesh):
    in_specs = (P(("blk", "wide"), None), P(("blk", "wide"), None), P(), P(), P())
    out_specs = (P(("blk", "wide"), None), P(("blk", "wide"), None))
    return jax.shard_map(
        on_device, mesh=mesh, in_specs=in_specs, out_specs=out_specs, check_vma=False
    )
```

```python
import jax
import jax.numpy as jnp
from jax import lax
from jax.experimental import pallas as pl
from jax.experimental.pallas import tpu as pltpu
from jax.sharding import PartitionSpec as P

AXES = ("blk", "wide")
LOG2E = 1.4426950408889634


def coordinates(blk, wide):
    return wide // 8, (wide // 4) % 2, wide % 4, blk // 2, blk % 2


def device_id(x, half, y, z, core):
    return ((z % 8) * 2 + core) * 32 + ((x % 4) * 2 + half) * 4 + y


def pairs(target):
    found = []
    for blk in range(16):
        for wide in range(32):
            x, half, y, z, core = coordinates(blk, wide)
            sign = 1 if core == 1 else -1
            mirrored = y if core == 1 else 3 - y
            there = target(x, half, mirrored, z, core, sign)
            if there is not None:
                x2, half2, mirrored2, z2, core2 = there
                y2 = mirrored2 if core == 1 else 3 - mirrored2
                found.append((blk * 32 + wide, device_id(x2, half2, y2, z2, core2)))
    return found


def crossing(x, half, sign):
    if sign == 1:
        return (x, 1) if half == 0 else (x + 1, 0)
    return (x, 0) if half == 1 else (x - 1, 1)


def to_sibling(x, h, m, z, c, s):
    return x, h, m, z, 1 - c


def to_previous_chip_sibling(x, h, m, z, c, s):
    return x, h, m, z - s, 1 - c


def to_next_chip_sibling(x, h, m, z, c, s):
    return x, h, m, z + s, 1 - c


def to_next_chip(x, h, m, z, c, s):
    return x, h, m, z + s, c


def to_previous_chip(x, h, m, z, c, s):
    return x, h, m, z - s, c


def to_next_wide(x, h, m, z, c, s):
    return (x, h, m + 1, z, c) if m < 3 else None


def to_sibling_next_wide(x, h, m, z, c, s):
    return (x, h, m - 1, z, c) if m > 0 else None


def across(x, h, m, z, c, s):
    x2, h2 = crossing(x, h, s)
    return x2, h2, m, z + s, c


def line_to_line(here, there):
    return lambda x, h, m, z, c, s: (x, h, there, z, c) if m == here else None


def send(name, x, target):
    with jax.named_scope(name):
        return lax.ppermute(x, AXES, pairs(target))


def scalars():
    return pl.BlockSpec(memory_space=pltpu.SMEM)


def whole():
    return pl.BlockSpec(memory_space=pltpu.VMEM)


def call(name, kernel, out_shape, smem, vmem, weight=1):
    many = isinstance(out_shape, (list, tuple))
    outs = [whole() for _ in out_shape] if many else whole()
    with jax.named_scope(name):
        return pl.pallas_call(
            kernel,
            out_shape=out_shape,
            in_specs=[scalars() for _ in smem] + [whole() for _ in vmem],
            out_specs=outs,
            cost_estimate=pl.CostEstimate(
                flops=weight * 1000, bytes_accessed=1000, transcendentals=0
            ),
            compiler_params=pltpu.CompilerParams(vmem_limit_bytes=16 * 1024 * 1024),
        )(*smem, *vmem)


def assemble(name, kernel, out_shape, smem, arrays, copies):
    many = isinstance(out_shape, (list, tuple))
    with jax.named_scope(name):
        return pl.pallas_call(
            kernel,
            out_shape=out_shape,
            in_specs=[scalars() for _ in smem] + [pl.BlockSpec(memory_space=pl.ANY) for _ in arrays],
            out_specs=[whole() for _ in out_shape] if many else whole(),
            scratch_shapes=[pltpu.SemaphoreType.DMA((copies,))],
            cost_estimate=pl.CostEstimate(flops=1000, bytes_accessed=1000, transcendentals=0),
            compiler_params=pltpu.CompilerParams(vmem_limit_bytes=16 * 1024 * 1024),
        )(*smem, *arrays)


def copy_all(sems, pieces):
    moves = [
        pltpu.make_async_copy(
            source.at[pl.ds(low, count)], target.at[pl.ds(at, count)], sems.at[k]
        )
        for k, (source, low, target, at, count) in enumerate(pieces)
    ]
    for one in moves:
        one.start()
    for one in moves:
        one.wait()


def term(query, query_factor, keys, key_factor, scale, own=False):
    logits = lax.dot_general(
        query, keys, (((1,), (1,)), ((), ())), preferred_element_type=jnp.float32
    )
    weights = jnp.exp2(logits * (scale * LOG2E) - 5.0 * LOG2E) * (query_factor + key_factor)
    if own:
        rows = lax.broadcasted_iota(jnp.int32, weights.shape, 0)
        cols = lax.broadcasted_iota(jnp.int32, weights.shape, 1)
        weights = weights - jnp.where(rows == cols, 1.0, 0.0)
    return jnp.dot(weights.astype(jnp.bfloat16), keys, preferred_element_type=jnp.float32)


def add_terms(total, query, query_factor, key_factors, scale, items):
    for keys, row, own in items:
        part = term(query, query_factor, keys, key_factors[row : row + 1, :], scale, own)
        total = part if total is None else total + part
    return total


def cut_kernel(inner, outer, *outs):
    quarter = inner.shape[0] // 4
    for step in range(4):
        low = quarter * step
        outs[step][:quarter, :] = inner[low : low + quarter, :]
        outs[step][quarter:, :] = outer[low : low + quarter, :]


def on_device(images, captions, logit_scale, row_lse, col_lse):
    rows, width = images.shape
    quarter = rows // 4
    half = jnp.bfloat16
    blk = lax.axis_index("blk")
    wide = lax.axis_index("wide")
    core = blk % 2
    sign = 2 * core - 1
    y = wide % 4
    mirrored = jnp.where(core == 1, y, 3 - y)
    carries_captions = core == 1
    at_edge = jnp.where(mirrored == 0, 1, 0).astype(jnp.int32).reshape(1)
    sibling_at_edge = jnp.where(mirrored == 3, 1, 0).astype(jnp.int32).reshape(1)
    core_flag = core.astype(jnp.int32).reshape(1)
    scale = logit_scale.reshape(1)

    def blocks(count):
        return jax.ShapeDtypeStruct((count * rows, width), half)

    outer = jnp.where(carries_captions, captions, images)
    other = jnp.where(carries_captions, images, captions)

    def after(value, *others):
        return lax.optimization_barrier((value, *others))[0]

    inner = send("swap", other, to_sibling)
    outer1 = send("own_outer1", outer, to_next_chip)
    inner1 = send("own_inner1", other, to_previous_chip_sibling)

    strip = jax.ShapeDtypeStruct((2 * quarter, width), half)
    cuts = call("cut", cut_kernel, [strip] * 4, (), (inner, outer))
    spread0 = send("spread0", cuts[0], line_to_line(3, 0))
    spread1 = send("spread1", cuts[1], line_to_line(3, 2))
    spread2 = send("spread2", cuts[2], line_to_line(3, 1))
    held = jnp.where(
        mirrored == 0,
        spread0,
        jnp.where(mirrored == 2, spread1, jnp.where(mirrored == 1, spread2, cuts[3])),
    )
    crossed = send("cross", held, across)
    early = send(
        "wide_early", jnp.concatenate([after(inner, held), outer, outer1], axis=0), to_next_wide
    )

    batch = row_lse.shape[0]

    def part(carried, b, w):
        start = ((b % 16) * 32 + (w % 32)) * rows
        from_rows = lax.dynamic_slice_in_dim(row_lse, start, rows)
        from_cols = lax.dynamic_slice_in_dim(col_lse, start, rows)
        return jnp.where(carries_captions == carried, from_cols, from_rows)

    pal = blk + 1 - 2 * core
    near_w, far_w = wide - sign, wide + sign
    own_outer = part(True, blk, wide)
    own_other = part(False, blk, wide)
    normalizers = [
        own_outer,
        part(True, pal, wide),
        part(True, blk - 2 * sign, wide),
        part(True, pal - 2 * sign, wide),
        part(True, blk - 2 * sign, near_w),
        part(True, pal - 2 * sign, near_w),
        part(True, pal, near_w),
        part(True, blk, near_w),
        own_other,
        part(False, pal + 2 * sign, wide),
        part(False, blk + 2 * sign, wide),
        part(False, pal + 4 * sign, wide),
        part(False, pal + 2 * sign, far_w),
        part(False, blk + 2 * sign, far_w),
        part(False, blk, far_w),
        part(False, pal + 4 * sign, far_w),
    ]

    def factors_kernel(*refs):
        sources, (keys, near, far) = refs[:-3], refs[-3:]
        for k, source in enumerate(sources):
            keys[k : k + 1, :] = 0.5 * jnp.exp(5.0 - source[...].reshape(1, rows))
        near[...] = jnp.broadcast_to(keys[8:9, :], (128, rows)).T
        far[...] = jnp.broadcast_to(keys[0:1, :], (128, rows)).T

    key_factors, near_factor, far_factor = call(
        "factors", factors_kernel,
        [jax.ShapeDtypeStruct(shape, jnp.float32) for shape in ((16, rows), (rows, 128), (rows, 128))],
        (), tuple(lax.optimization_barrier((*normalizers, held))[:-1]),
    )
    total = jax.ShapeDtypeStruct((rows, width), jnp.float32)

    def terms(name, near_blocks, far_blocks, sums, weight=1):
        arrays = [array for array, _ in near_blocks + far_blocks]

        def kernel(s, oth, out, nf, ff, kf, *refs):
            keys, refs = refs[: len(arrays)], refs[len(arrays) :]
            starts, ends = (refs[:2], refs[2:]) if sums else ((None, None), refs)

            def add(start, query, query_factor, blocks, refs, end):
                items = []
                for ref, (_, places) in zip(refs, blocks):
                    for k, row in enumerate(places):
                        if row is None:
                            continue
                        items.append((ref[k * rows : (k + 1) * rows, :], row, row in (0, 8)))
                before = None if start is None else start[...]
                end[...] = add_terms(before, query[...], query_factor[:, :1], kf, s[0], items)

            add(starts[0], oth, nf, near_blocks, keys[: len(near_blocks)], ends[0])
            add(starts[1], out, ff, far_blocks, keys[len(near_blocks) :], ends[1])

        return call(
            name, kernel, [total, total], (scale,),
            (other, outer, near_factor, far_factor, key_factors, *arrays, *(sums or ())), weight,
        )

    sums = terms("terms_own0", [(outer, [0]), (inner, [1]), (after(outer1, held), [2])], [(other, [8])], None, 100_000_000)
    inner1 = after(inner1, *sums)
    late = send("wide_late", inner1, to_next_wide)

    def slice_kernel(block, out):
        out[...] = block[quarter:, :]

    outer_part = call(
        "slice", slice_kernel, jax.ShapeDtypeStruct((quarter, width), half), (), (crossed,),
        100_000_000,
    )
    back = send("cross_back", after(crossed, outer_part), to_previous_chip)
    ahead = send("cross_ahead", outer_part, to_next_chip)
    late, early, _ = lax.optimization_barrier((late, early, outer_part))
    crossed = after(crossed, late, early)

    def collect(name, mine):
        q1 = send(name + "1", mine, line_to_line(2, 0))
        q2 = send(name + "2", mine, line_to_line(1, 0))
        q3 = send(name + "3", mine, line_to_line(3, 0))
        return [mine, q1, q2, q3]

    got1 = collect("gather1_", crossed)
    far2 = send("own_outer2", after(outer1, crossed), to_next_chip_sibling)

    def join_kernel(first, second, out):
        out[: 2 * quarter, :] = first[...]
        out[2 * quarter :, :] = second[...]

    joined = call(
        "join", join_kernel, jax.ShapeDtypeStruct((3 * quarter, width), half), (),
        (back, ahead), 100_000_000,
    )
    got0 = collect("gather0_", after(joined, *got1))

    def merge1_kernel(edge, early, late, outer1, inner1, q0, q1, q2, q3, out, sems):
        own = [(outer1, 0, out, 2 * rows, rows), (inner1, 0, out, 3 * rows, rows)]

        @pl.when(edge[0] == 1)
        def _():
            pieces = []
            for place, source in enumerate((q0, q1, q2, q3)):
                pieces.append((source, quarter, out, place * quarter, quarter))
                pieces.append((source, 0, out, rows + place * quarter, quarter))
            copy_all(sems, pieces + own)

        @pl.when(edge[0] == 0)
        def _():
            copy_all(sems, [(early, 2 * rows, out, 0, rows), (late, 0, out, rows, rows)] + own)

    carried = assemble(
        "merge1", merge1_kernel, blocks(4), (at_edge,),
        (early, late, after(outer1, back, ahead), inner1, *got1), 10,
    )
    sib = send("sibling1", carried, to_sibling)
    hop_far2 = send("wide_outer2", after(far2, carried), to_sibling_next_wide)
    near_sum, far_sum = sums

    def near_kernel(s, oth, nf, kf, keys, near_in, near):
        near[...] = add_terms(
            near_in[...], oth[...], nf[:, :1], kf, s[0],
            [(keys[:rows, :], 4, False), (keys[rows : 2 * rows, :], 5, False),
             (keys[3 * rows :, :], 3, False)],
        )

    near_sum = call(
        "terms_near1", near_kernel, total, (scale,),
        (other, near_factor, key_factors, carried, near_sum), 100_000_000,
    )

    got0 = [after(got0[0], far2, near_sum), *got0[1:]]

    def merge0_kernel(edge, usual, q0, q1, q2, q3, out, outer0, sems):
        @pl.when(edge[0] == 1)
        def _():
            pieces = []
            for place, source in enumerate((q0, q1, q2, q3)):
                low = place * quarter
                pieces.append((source, 0, out, low, quarter))
                pieces.append((source, quarter, outer0, low, quarter))
                pieces.append((source, 2 * quarter, out, rows + low, quarter))
            copy_all(sems, pieces)

        @pl.when(edge[0] == 0)
        def _():
            copy_all(sems, [(usual, 0, out, 0, 2 * rows), (usual, rows, outer0, 0, rows)])

    hop0, hop_outer0 = assemble(
        "merge0", merge0_kernel, [blocks(2), blocks(1)], (at_edge,), (early, *got0), 12
    )
    hop_sib0 = send("sibling_hop0", hop0, to_sibling)

    anywhere = pl.BlockSpec(memory_space=pl.ANY)

    def near0_kernel(c, s, oth, nf, kf, outer0, inner0, near_in, image_grad, caption_grad, held_sum, sem):
        held_sum[...] = s[0] * add_terms(
            near_in[...], oth[...], nf[:, :1], kf, s[0],
            [(outer0[...], 7, False), (inner0[:rows, :], 6, False)],
        )

        @pl.when(c[0] == 1)
        def _():
            one = pltpu.make_async_copy(held_sum, image_grad, sem)
            one.start()
            one.wait()

        @pl.when(c[0] == 0)
        def _():
            one = pltpu.make_async_copy(held_sum, caption_grad, sem)
            one.start()
            one.wait()

    with jax.named_scope("terms_near0"):
        half_done = pl.pallas_call(
            near0_kernel,
            out_shape=[total, total],
            in_specs=[scalars()] * 2 + [whole()] * 6,
            out_specs=[anywhere] * 2,
            scratch_shapes=[pltpu.VMEM((rows, width), jnp.float32), pltpu.SemaphoreType.DMA],
            cost_estimate=pl.CostEstimate(
                flops=100_000_000_000, bytes_accessed=1000, transcendentals=0
            ),
            compiler_params=pltpu.CompilerParams(vmem_limit_bytes=16 * 1024 * 1024),
        )(core_flag, scale, other, near_factor, key_factors, hop_outer0, hop0, near_sum)

    def far1_kernel(s, out, ff, kf, keys, farthest, far_in, far):
        far[...] = add_terms(
            far_in[...], out[...], ff[:, :1], kf, s[0],
            [(keys[k * rows : (k + 1) * rows, :], row, False) for k, row in enumerate((12, 13, 9, 10))]
            + [(farthest[...], 11, False)],
        )

    far_sum = call(
        "terms_far1", far1_kernel, total, (scale,),
        (outer, far_factor, key_factors, after(sib, hop_far2, *half_done), far2, far_sum), 100_000_000,
    )

    def last_kernel(
        c, e, s, out, ff, kf, hs0, hf2, far_in, _i, _c, image_grad, caption_grad, held_sum, sem
    ):
        farthest = jnp.where(e[0] == 1, hs0[rows:, :], hf2[...])
        held_sum[...] = s[0] * add_terms(
            far_in[...], out[...], ff[:, :1], kf, s[0],
            [(hs0[:rows, :], 14, False), (farthest, 15, False)],
        )

        @pl.when(c[0] == 1)
        def _():
            one = pltpu.make_async_copy(held_sum, caption_grad, sem)
            one.start()
            one.wait()

        @pl.when(c[0] == 0)
        def _():
            one = pltpu.make_async_copy(held_sum, image_grad, sem)
            one.start()
            one.wait()

    with jax.named_scope("terms_last"):
        image_grad, caption_grad = pl.pallas_call(
            last_kernel,
            out_shape=[total, total],
            in_specs=[scalars()] * 3 + [whole()] * 6 + [anywhere] * 2,
            out_specs=[anywhere] * 2,
            scratch_shapes=[pltpu.VMEM((rows, width), jnp.float32), pltpu.SemaphoreType.DMA],
            input_output_aliases={9: 0, 10: 1},
            cost_estimate=pl.CostEstimate(flops=1000, bytes_accessed=1000, transcendentals=0),
            compiler_params=pltpu.CompilerParams(vmem_limit_bytes=16 * 1024 * 1024),
        )(
            core_flag, sibling_at_edge, scale,
            outer, far_factor, key_factors, hop_sib0, hop_far2, far_sum, *half_done,
        )
    return image_grad, caption_grad


def solution(mesh):
    in_specs = (P(("blk", "wide"), None), P(("blk", "wide"), None), P(), P(), P())
    out_specs = (P(("blk", "wide"), None), P(("blk", "wide"), None))
    return jax.shard_map(
        on_device, mesh=mesh, in_specs=in_specs, out_specs=out_specs, check_vma=False
    )
```

```python
import jax
import jax.numpy as jnp
from jax import lax
from jax.experimental import pallas as pl
from jax.experimental.pallas import tpu as pltpu
from jax.sharding import PartitionSpec as P

AXES = ("blk", "wide")
LOG2E = 1.4426950408889634


def coordinates(blk, wide):
    return wide // 8, (wide // 4) % 2, wide % 4, blk // 2, blk % 2


def device_id(x, half, y, z, core):
    return ((z % 8) * 2 + core) * 32 + ((x % 4) * 2 + half) * 4 + y


def pairs(target):
    found = []
    for blk in range(16):
        for wide in range(32):
            x, half, y, z, core = coordinates(blk, wide)
            sign = 1 if core == 1 else -1
            mirrored = y if core == 1 else 3 - y
            there = target(x, half, mirrored, z, core, sign)
            if there is not None:
                x2, half2, mirrored2, z2, core2 = there
                y2 = mirrored2 if core == 1 else 3 - mirrored2
                found.append((blk * 32 + wide, device_id(x2, half2, y2, z2, core2)))
    return found


def crossing(x, half, sign):
    if sign == 1:
        return (x, 1) if half == 0 else (x + 1, 0)
    return (x, 0) if half == 1 else (x - 1, 1)


def to_sibling(x, h, m, z, c, s):
    return x, h, m, z, 1 - c


def to_previous_chip_sibling(x, h, m, z, c, s):
    return x, h, m, z - s, 1 - c


def to_next_chip_sibling(x, h, m, z, c, s):
    return x, h, m, z + s, 1 - c


def to_next_chip(x, h, m, z, c, s):
    return x, h, m, z + s, c


def to_previous_chip(x, h, m, z, c, s):
    return x, h, m, z - s, c


def to_next_wide(x, h, m, z, c, s):
    return (x, h, m + 1, z, c) if m < 3 else None


def to_sibling_next_wide(x, h, m, z, c, s):
    return (x, h, m - 1, z, c) if m > 0 else None


def across(x, h, m, z, c, s):
    x2, h2 = crossing(x, h, s)
    return x2, h2, m, z + s, c


def line_to_line(here, there):
    return lambda x, h, m, z, c, s: (x, h, there, z, c) if m == here else None


def send(name, x, target):
    with jax.named_scope(name):
        return lax.ppermute(x, AXES, pairs(target))


def scalars():
    return pl.BlockSpec(memory_space=pltpu.SMEM)


def whole():
    return pl.BlockSpec(memory_space=pltpu.VMEM)


def call(name, kernel, out_shape, smem, vmem, weight=1):
    many = isinstance(out_shape, (list, tuple))
    outs = [whole() for _ in out_shape] if many else whole()
    with jax.named_scope(name):
        return pl.pallas_call(
            kernel,
            out_shape=out_shape,
            in_specs=[scalars() for _ in smem] + [whole() for _ in vmem],
            out_specs=outs,
            cost_estimate=pl.CostEstimate(
                flops=weight * 1000, bytes_accessed=1000, transcendentals=0
            ),
            compiler_params=pltpu.CompilerParams(vmem_limit_bytes=16 * 1024 * 1024),
        )(*smem, *vmem)


def assemble(name, kernel, out_shape, smem, arrays, copies):
    many = isinstance(out_shape, (list, tuple))
    with jax.named_scope(name):
        return pl.pallas_call(
            kernel,
            out_shape=out_shape,
            in_specs=[scalars() for _ in smem] + [pl.BlockSpec(memory_space=pl.ANY) for _ in arrays],
            out_specs=[whole() for _ in out_shape] if many else whole(),
            scratch_shapes=[pltpu.SemaphoreType.DMA((copies,))],
            cost_estimate=pl.CostEstimate(flops=1000, bytes_accessed=1000, transcendentals=0),
            compiler_params=pltpu.CompilerParams(vmem_limit_bytes=16 * 1024 * 1024),
        )(*smem, *arrays)


def copy_all(sems, pieces):
    moves = [
        pltpu.make_async_copy(
            source.at[pl.ds(low, count)], target.at[pl.ds(at, count)], sems.at[k]
        )
        for k, (source, low, target, at, count) in enumerate(pieces)
    ]
    for one in moves:
        one.start()
    for one in moves:
        one.wait()


def term(query, query_factor, keys, key_factor, scale, own=False):
    logits = lax.dot_general(
        query, keys, (((1,), (1,)), ((), ())), preferred_element_type=jnp.float32
    )
    weights = jnp.exp2(logits * (scale * LOG2E) - 5.0 * LOG2E) * (query_factor + key_factor)
    if own:
        rows = lax.broadcasted_iota(jnp.int32, weights.shape, 0)
        cols = lax.broadcasted_iota(jnp.int32, weights.shape, 1)
        weights = weights - jnp.where(rows == cols, 1.0, 0.0)
    return jnp.dot(weights.astype(jnp.bfloat16), keys, preferred_element_type=jnp.float32)


def add_terms(total, query, query_factor, key_factors, scale, items):
    rows = query.shape[0]
    for keys, place, own in items:
        chosen = key_factors[:, place * rows : place * rows + keys.shape[0]]
        part = term(query, query_factor, keys, chosen, scale, own)
        total = part if total is None else total + part
    return total


def cut_kernel(inner, outer, *outs):
    quarter = inner.shape[0] // 4
    for step in range(4):
        low = quarter * step
        outs[step][:quarter, :] = inner[low : low + quarter, :]
        outs[step][quarter:, :] = outer[low : low + quarter, :]


def on_device(images, captions, logit_scale, row_lse, col_lse):
    rows, width = images.shape
    quarter = rows // 4
    half = jnp.bfloat16
    blk = lax.axis_index("blk")
    wide = lax.axis_index("wide")
    core = blk % 2
    sign = 2 * core - 1
    y = wide % 4
    mirrored = jnp.where(core == 1, y, 3 - y)
    carries_captions = core == 1
    at_edge = jnp.where(mirrored == 0, 1, 0).astype(jnp.int32).reshape(1)
    sibling_at_edge = jnp.where(mirrored == 3, 1, 0).astype(jnp.int32).reshape(1)
    core_flag = core.astype(jnp.int32).reshape(1)
    scale = logit_scale.reshape(1)

    def blocks(count):
        return jax.ShapeDtypeStruct((count * rows, width), half)

    outer = jnp.where(carries_captions, captions, images)
    other = jnp.where(carries_captions, images, captions)

    def after(value, *others):
        return lax.optimization_barrier((value, *others))[0]

    inner = send("swap", other, to_sibling)
    outer1 = send("own_outer1", outer, to_next_chip)
    inner1 = send("own_inner1", other, to_previous_chip_sibling)

    strip = jax.ShapeDtypeStruct((2 * quarter, width), half)
    cuts = call("cut", cut_kernel, [strip] * 4, (), (inner, outer))
    spread0 = send("spread0", cuts[0], line_to_line(3, 0))
    spread1 = send("spread1", cuts[1], line_to_line(3, 2))
    spread2 = send("spread2", cuts[2], line_to_line(3, 1))
    held = jnp.where(
        mirrored == 0,
        spread0,
        jnp.where(mirrored == 2, spread1, jnp.where(mirrored == 1, spread2, cuts[3])),
    )
    crossed = send("cross", held, across)
    early = send(
        "wide_early", jnp.concatenate([after(inner, held), outer, outer1], axis=0), to_next_wide
    )

    batch = row_lse.shape[0]

    def part(carried, b, w):
        start = ((b % 16) * 32 + (w % 32)) * rows
        from_rows = lax.dynamic_slice_in_dim(row_lse, start, rows)
        from_cols = lax.dynamic_slice_in_dim(col_lse, start, rows)
        return jnp.where(carries_captions == carried, from_cols, from_rows)

    pal = blk + 1 - 2 * core
    near_w, far_w = wide - sign, wide + sign
    own_outer = part(True, blk, wide)
    own_other = part(False, blk, wide)
    normalizers = [
        own_outer,
        part(True, pal, wide),
        part(True, blk - 2 * sign, wide),
        part(True, pal - 2 * sign, wide),
        part(True, blk - 2 * sign, near_w),
        part(True, pal - 2 * sign, near_w),
        part(True, pal, near_w),
        part(True, blk, near_w),
        own_other,
        part(False, pal + 2 * sign, wide),
        part(False, blk + 2 * sign, wide),
        part(False, pal + 4 * sign, wide),
        part(False, pal + 2 * sign, far_w),
        part(False, blk + 2 * sign, far_w),
        part(False, blk, far_w),
        part(False, pal + 4 * sign, far_w),
    ]

    def factors_kernel(*refs):
        sources, (keys, near, far) = refs[:-3], refs[-3:]
        for k, source in enumerate(sources):
            keys[:, k * rows : (k + 1) * rows] = 0.5 * jnp.exp(5.0 - source[...].reshape(1, rows))
        near[...] = jnp.broadcast_to(keys[:, 8 * rows : 9 * rows], (128, rows)).T
        far[...] = jnp.broadcast_to(keys[:, :rows], (128, rows)).T

    key_factors, near_factor, far_factor = call(
        "factors", factors_kernel,
        [jax.ShapeDtypeStruct(shape, jnp.float32) for shape in ((1, 16 * rows), (rows, 128), (rows, 128))],
        (), tuple(lax.optimization_barrier((*normalizers, held))[:-1]),
    )
    total = jax.ShapeDtypeStruct((rows, width), jnp.float32)

    def terms(name, near_blocks, far_blocks, sums, weight=1):
        arrays = [array for array, _ in near_blocks + far_blocks]

        def kernel(s, oth, out, nf, ff, kf, *refs):
            keys, refs = refs[: len(arrays)], refs[len(arrays) :]
            starts, ends = (refs[:2], refs[2:]) if sums else ((None, None), refs)

            def add(start, query, query_factor, blocks, refs, end):
                items = []
                for ref, (_, places) in zip(refs, blocks):
                    for k, row in enumerate(places):
                        if row is None:
                            continue
                        items.append((ref[k * rows : (k + 1) * rows, :], row, row in (0, 8)))
                before = None if start is None else start[...]
                end[...] = add_terms(before, query[...], query_factor[:, :1], kf, s[0], items)

            add(starts[0], oth, nf, near_blocks, keys[: len(near_blocks)], ends[0])
            add(starts[1], out, ff, far_blocks, keys[len(near_blocks) :], ends[1])

        return call(
            name, kernel, [total, total], (scale,),
            (other, outer, near_factor, far_factor, key_factors, *arrays, *(sums or ())), weight,
        )

    sums = terms("terms_own0", [(outer, [0]), (inner, [1]), (after(outer1, held), [2])], [(other, [8])], None, 100_000_000)
    inner1 = after(inner1, *sums)
    late = send("wide_late", inner1, to_next_wide)

    def slice_kernel(block, out):
        out[...] = block[quarter:, :]

    outer_part = call(
        "slice", slice_kernel, jax.ShapeDtypeStruct((quarter, width), half), (), (after(crossed, *sums),),
        100_000_000,
    )
    back = send("cross_back", after(crossed, outer_part), to_previous_chip)
    ahead = send("cross_ahead", outer_part, to_next_chip)
    early, _ = lax.optimization_barrier((early, outer_part))
    crossed = after(crossed, early)

    def collect(name, mine):
        q1 = send(name + "1", mine, line_to_line(2, 0))
        q2 = send(name + "2", mine, line_to_line(1, 0))
        q3 = send(name + "3", mine, line_to_line(3, 0))
        return [mine, q1, q2, q3]

    got1 = collect("gather1_", crossed)
    far2 = send("own_outer2", after(outer1, crossed), to_next_chip_sibling)

    def join_kernel(first, second, out):
        out[: 2 * quarter, :] = first[...]
        out[2 * quarter :, :] = second[...]

    joined = call(
        "join", join_kernel, jax.ShapeDtypeStruct((3 * quarter, width), half), (),
        (back, ahead), 100_000_000,
    )
    got0 = collect("gather0_", after(joined, *got1))

    def merge1_kernel(edge, early, late, outer1, inner1, q0, q1, q2, q3, out, sems):
        own = [(outer1, 0, out, 2 * rows, rows), (inner1, 0, out, 3 * rows, rows)]

        @pl.when(edge[0] == 1)
        def _():
            pieces = []
            for place, source in enumerate((q0, q1, q2, q3)):
                pieces.append((source, quarter, out, place * quarter, quarter))
                pieces.append((source, 0, out, rows + place * quarter, quarter))
            copy_all(sems, pieces + own)

        @pl.when(edge[0] == 0)
        def _():
            copy_all(sems, [(early, 2 * rows, out, 0, rows), (late, 0, out, rows, rows)] + own)

    carried = assemble(
        "merge1", merge1_kernel, blocks(4), (at_edge,),
        (early, late, after(outer1, back, ahead), inner1, *got1), 10,
    )
    sib = send("sibling1", carried, to_sibling)
    hop_far2 = send("wide_outer2", after(far2, carried), to_sibling_next_wide)
    near_sum, far_sum = sums

    def near_kernel(s, oth, nf, kf, keys, near_in, near):
        near[...] = add_terms(
            near_in[...], oth[...], nf[:, :1], kf, s[0],
            [(keys[: 2 * rows, :], 4, False), (keys[3 * rows :, :], 3, False)],
        )

    near_sum = call(
        "terms_near1", near_kernel, total, (scale,),
        (other, near_factor, key_factors, carried, near_sum), 100_000_000,
    )

    got0 = [after(got0[0], far2, near_sum), *got0[1:]]

    def merge0_kernel(edge, usual, q0, q1, q2, q3, out, outer0, sems):
        @pl.when(edge[0] == 1)
        def _():
            pieces = []
            for place, source in enumerate((q0, q1, q2, q3)):
                low = place * quarter
                pieces.append((source, 0, out, low, quarter))
                pieces.append((source, quarter, outer0, low, quarter))
                pieces.append((source, 2 * quarter, out, rows + low, quarter))
            copy_all(sems, pieces)

        @pl.when(edge[0] == 0)
        def _():
            copy_all(sems, [(usual, 0, out, 0, 2 * rows), (usual, rows, outer0, 0, rows)])

    hop0, hop_outer0 = assemble(
        "merge0", merge0_kernel, [blocks(2), blocks(1)], (at_edge,), (early, *got0), 12
    )
    hop_sib0 = send("sibling_hop0", hop0, to_sibling)

    anywhere = pl.BlockSpec(memory_space=pl.ANY)

    def near0_kernel(c, s, oth, nf, kf, outer0, inner0, near_in, image_grad, caption_grad, held_sum, sem):
        held_sum[...] = s[0] * add_terms(
            near_in[...], oth[...], nf[:, :1], kf, s[0],
            [(jnp.concatenate([inner0[:rows, :], outer0[...]], axis=0), 6, False)],
        )

        @pl.when(c[0] == 1)
        def _():
            one = pltpu.make_async_copy(held_sum, image_grad, sem)
            one.start()
            one.wait()

        @pl.when(c[0] == 0)
        def _():
            one = pltpu.make_async_copy(held_sum, caption_grad, sem)
            one.start()
            one.wait()

    with jax.named_scope("terms_near0"):
        half_done = pl.pallas_call(
            near0_kernel,
            out_shape=[total, total],
            in_specs=[scalars()] * 2 + [whole()] * 6,
            out_specs=[anywhere] * 2,
            scratch_shapes=[pltpu.VMEM((rows, width), jnp.float32), pltpu.SemaphoreType.DMA],
            cost_estimate=pl.CostEstimate(
                flops=100_000_000_000, bytes_accessed=1000, transcendentals=0
            ),
            compiler_params=pltpu.CompilerParams(vmem_limit_bytes=16 * 1024 * 1024),
        )(core_flag, scale, other, near_factor, key_factors, hop_outer0, hop0, near_sum)

    def far1_kernel(s, out, ff, kf, keys, farthest, far_in, far):
        far[...] = add_terms(
            far_in[...], out[...], ff[:, :1], kf, s[0],
            [(keys[: 2 * rows, :], 12, False), (keys[2 * rows :, :], 9, False),
             (farthest[...], 11, False)],
        )

    far_sum = call(
        "terms_far1", far1_kernel, total, (scale,),
        (outer, far_factor, key_factors, after(sib, hop_far2, *half_done), far2, far_sum), 100_000_000,
    )

    def last_kernel(
        c, e, s, out, ff, kf, hs0, hf2, far_in, _i, _c, image_grad, caption_grad, held_sum, sem
    ):
        farthest = jnp.where(e[0] == 1, hs0[rows:, :], hf2[...])
        held_sum[...] = s[0] * add_terms(
            far_in[...], out[...], ff[:, :1], kf, s[0],
            [(jnp.concatenate([hs0[:rows, :], farthest], axis=0), 14, False)],
        )

        @pl.when(c[0] == 1)
        def _():
            one = pltpu.make_async_copy(held_sum, caption_grad, sem)
            one.start()
            one.wait()

        @pl.when(c[0] == 0)
        def _():
            one = pltpu.make_async_copy(held_sum, image_grad, sem)
            one.start()
            one.wait()

    with jax.named_scope("terms_last"):
        image_grad, caption_grad = pl.pallas_call(
            last_kernel,
            out_shape=[total, total],
            in_specs=[scalars()] * 3 + [whole()] * 6 + [anywhere] * 2,
            out_specs=[anywhere] * 2,
            scratch_shapes=[pltpu.VMEM((rows, width), jnp.float32), pltpu.SemaphoreType.DMA],
            input_output_aliases={9: 0, 10: 1},
            cost_estimate=pl.CostEstimate(flops=1000, bytes_accessed=1000, transcendentals=0),
            compiler_params=pltpu.CompilerParams(vmem_limit_bytes=16 * 1024 * 1024),
        )(
            core_flag, sibling_at_edge, scale,
            outer, far_factor, key_factors, hop_sib0, hop_far2, far_sum, *half_done,
        )
    return image_grad, caption_grad


def solution(mesh):
    in_specs = (P(("blk", "wide"), None), P(("blk", "wide"), None), P(), P(), P())
    out_specs = (P(("blk", "wide"), None), P(("blk", "wide"), None))
    return jax.shard_map(
        on_device, mesh=mesh, in_specs=in_specs, out_specs=out_specs, check_vma=False
    )
```

```python
import jax
import jax.numpy as jnp
from jax import lax
from jax.experimental import pallas as pl
from jax.experimental.pallas import tpu as pltpu
from jax.sharding import PartitionSpec as P

AXES = ("blk", "wide")
LOG2E = 1.4426950408889634


def coordinates(blk, wide):
    return wide // 8, (wide // 4) % 2, wide % 4, blk // 2, blk % 2


def device_id(x, half, y, z, core):
    return ((z % 8) * 2 + core) * 32 + ((x % 4) * 2 + half) * 4 + y


def pairs(target):
    found = []
    for blk in range(16):
        for wide in range(32):
            x, half, y, z, core = coordinates(blk, wide)
            sign = 1 if core == 1 else -1
            mirrored = y if core == 1 else 3 - y
            there = target(x, half, mirrored, z, core, sign)
            if there is not None:
                x2, half2, mirrored2, z2, core2 = there
                y2 = mirrored2 if core == 1 else 3 - mirrored2
                found.append((blk * 32 + wide, device_id(x2, half2, y2, z2, core2)))
    return found


def crossing(x, half, sign):
    if sign == 1:
        return (x, 1) if half == 0 else (x + 1, 0)
    return (x, 0) if half == 1 else (x - 1, 1)


def to_sibling(x, h, m, z, c, s):
    return x, h, m, z, 1 - c


def to_previous_chip_sibling(x, h, m, z, c, s):
    return x, h, m, z - s, 1 - c


def to_next_chip_sibling(x, h, m, z, c, s):
    return x, h, m, z + s, 1 - c


def to_next_chip(x, h, m, z, c, s):
    return x, h, m, z + s, c


def to_previous_chip(x, h, m, z, c, s):
    return x, h, m, z - s, c


def to_next_wide(x, h, m, z, c, s):
    return (x, h, m + 1, z, c) if m < 3 else None


def farthest_route(x, h, m, z, c, s):
    return (x, h, m - 1, z, c) if m > 0 else (x, h, m, z + s, 1 - c)


def edge_to_previous_chip(x, h, m, z, c, s):
    return (x, h, m, z - s, c) if m == 0 else None


def across(x, h, m, z, c, s):
    x2, h2 = crossing(x, h, s)
    return x2, h2, m, z + s, c


def line_to_line(here, there):
    return lambda x, h, m, z, c, s: (x, h, there, z, c) if m == here else None


def send(name, x, target):
    with jax.named_scope(name):
        return lax.ppermute(x, AXES, pairs(target))


def scalars():
    return pl.BlockSpec(memory_space=pltpu.SMEM)


def whole():
    return pl.BlockSpec(memory_space=pltpu.VMEM)


def call(name, kernel, out_shape, smem, vmem, weight=1):
    many = isinstance(out_shape, (list, tuple))
    outs = [whole() for _ in out_shape] if many else whole()
    with jax.named_scope(name):
        return pl.pallas_call(
            kernel,
            out_shape=out_shape,
            in_specs=[scalars() for _ in smem] + [whole() for _ in vmem],
            out_specs=outs,
            cost_estimate=pl.CostEstimate(
                flops=weight * 1000, bytes_accessed=1000, transcendentals=0
            ),
            compiler_params=pltpu.CompilerParams(vmem_limit_bytes=16 * 1024 * 1024),
        )(*smem, *vmem)


def assemble(name, kernel, out_shape, smem, arrays, copies):
    many = isinstance(out_shape, (list, tuple))
    with jax.named_scope(name):
        return pl.pallas_call(
            kernel,
            out_shape=out_shape,
            in_specs=[scalars() for _ in smem] + [pl.BlockSpec(memory_space=pl.ANY) for _ in arrays],
            out_specs=[whole() for _ in out_shape] if many else whole(),
            scratch_shapes=[pltpu.SemaphoreType.DMA((copies,))],
            cost_estimate=pl.CostEstimate(flops=1000, bytes_accessed=1000, transcendentals=0),
            compiler_params=pltpu.CompilerParams(vmem_limit_bytes=16 * 1024 * 1024),
        )(*smem, *arrays)


def copy_all(sems, pieces):
    moves = [
        pltpu.make_async_copy(
            source.at[pl.ds(low, count)], target.at[pl.ds(at, count)], sems.at[k]
        )
        for k, (source, low, target, at, count) in enumerate(pieces)
    ]
    for one in moves:
        one.start()
    for one in moves:
        one.wait()


def term(query, query_factor, keys, key_factor, scale, own=False):
    logits = lax.dot_general(
        query, keys, (((1,), (1,)), ((), ())), preferred_element_type=jnp.float32
    )
    weights = jnp.exp2(logits * (scale * LOG2E) - 5.0 * LOG2E) * (query_factor + key_factor)
    if own:
        rows = lax.broadcasted_iota(jnp.int32, weights.shape, 0)
        cols = lax.broadcasted_iota(jnp.int32, weights.shape, 1)
        weights = weights - jnp.where(rows == cols, 1.0, 0.0)
    return jnp.dot(weights.astype(jnp.bfloat16), keys, preferred_element_type=jnp.float32)


def add_terms(total, query, query_factor, key_factors, scale, items):
    rows = query.shape[0]
    for keys, place, own in items:
        chosen = key_factors[:, place * rows : place * rows + keys.shape[0]]
        part = term(query, query_factor, keys, chosen, scale, own)
        total = part if total is None else total + part
    return total


def cut_kernel(inner, outer, *outs):
    quarter = inner.shape[0] // 4
    for step in range(4):
        low = quarter * step
        outs[step][:quarter, :] = inner[low : low + quarter, :]
        outs[step][quarter:, :] = outer[low : low + quarter, :]


def on_device(images, captions, logit_scale, row_lse, col_lse):
    rows, width = images.shape
    quarter = rows // 4
    half = jnp.bfloat16
    blk = lax.axis_index("blk")
    wide = lax.axis_index("wide")
    core = blk % 2
    sign = 2 * core - 1
    y = wide % 4
    mirrored = jnp.where(core == 1, y, 3 - y)
    carries_captions = core == 1
    at_edge = jnp.where(mirrored == 0, 1, 0).astype(jnp.int32).reshape(1)
    core_flag = core.astype(jnp.int32).reshape(1)
    scale = logit_scale.reshape(1)

    def blocks(count):
        return jax.ShapeDtypeStruct((count * rows, width), half)

    outer = jnp.where(carries_captions, captions, images)
    other = jnp.where(carries_captions, images, captions)

    def after(value, *others):
        return lax.optimization_barrier((value, *others))[0]

    inner = send("swap", other, to_sibling)
    outer1 = send("own_outer1", outer, to_next_chip)
    inner1 = send("own_inner1", other, to_previous_chip_sibling)

    strip = jax.ShapeDtypeStruct((2 * quarter, width), half)
    cuts = call("cut", cut_kernel, [strip] * 4, (), (inner, outer))
    spread0 = send("spread0", cuts[0], line_to_line(3, 0))
    spread1 = send("spread1", cuts[1], line_to_line(3, 2))
    spread2 = send("spread2", cuts[2], line_to_line(3, 1))
    held = jnp.where(
        mirrored == 0,
        spread0,
        jnp.where(mirrored == 2, spread1, jnp.where(mirrored == 1, spread2, cuts[3])),
    )
    crossed = send("cross", held, across)
    early = send(
        "wide_early", jnp.concatenate([after(inner, held), outer, outer1], axis=0), to_next_wide
    )

    batch = row_lse.shape[0]

    def part(carried, b, w):
        start = ((b % 16) * 32 + (w % 32)) * rows
        from_rows = lax.dynamic_slice_in_dim(row_lse, start, rows)
        from_cols = lax.dynamic_slice_in_dim(col_lse, start, rows)
        return jnp.where(carries_captions == carried, from_cols, from_rows)

    pal = blk + 1 - 2 * core
    near_w, far_w = wide - sign, wide + sign
    own_outer = part(True, blk, wide)
    own_other = part(False, blk, wide)
    normalizers = [
        own_outer,
        part(True, pal, wide),
        part(True, blk - 2 * sign, wide),
        part(True, pal - 2 * sign, wide),
        part(True, blk - 2 * sign, near_w),
        part(True, pal - 2 * sign, near_w),
        part(True, pal, near_w),
        part(True, blk, near_w),
        own_other,
        part(False, pal + 2 * sign, wide),
        part(False, blk + 2 * sign, wide),
        part(False, pal + 4 * sign, wide),
        part(False, pal + 2 * sign, far_w),
        part(False, blk + 2 * sign, far_w),
        part(False, blk, far_w),
        part(False, pal + 4 * sign, far_w),
    ]

    def factors_kernel(*refs):
        sources, (keys, near, far) = refs[:-3], refs[-3:]
        for k, source in enumerate(sources):
            keys[:, k * rows : (k + 1) * rows] = 0.5 * jnp.exp(5.0 - source[...].reshape(1, rows))
        near[...] = jnp.broadcast_to(keys[:, 8 * rows : 9 * rows], (128, rows)).T
        far[...] = jnp.broadcast_to(keys[:, :rows], (128, rows)).T

    key_factors, near_factor, far_factor = call(
        "factors", factors_kernel,
        [jax.ShapeDtypeStruct(shape, jnp.float32) for shape in ((1, 16 * rows), (rows, 128), (rows, 128))],
        (), tuple(lax.optimization_barrier((*normalizers, held))[:-1]),
    )
    total = jax.ShapeDtypeStruct((rows, width), jnp.float32)

    def terms(name, near_blocks, far_blocks, sums, weight=1):
        arrays = [array for array, _ in near_blocks + far_blocks]

        def kernel(s, oth, out, nf, ff, kf, *refs):
            keys, refs = refs[: len(arrays)], refs[len(arrays) :]
            starts, ends = (refs[:2], refs[2:]) if sums else ((None, None), refs)

            def add(start, query, query_factor, blocks, refs, end):
                items = []
                for ref, (_, places) in zip(refs, blocks):
                    for k, row in enumerate(places):
                        if row is None:
                            continue
                        items.append((ref[k * rows : (k + 1) * rows, :], row, row in (0, 8)))
                before = None if start is None else start[...]
                end[...] = add_terms(before, query[...], query_factor[:, :1], kf, s[0], items)

            add(starts[0], oth, nf, near_blocks, keys[: len(near_blocks)], ends[0])
            add(starts[1], out, ff, far_blocks, keys[len(near_blocks) :], ends[1])

        return call(
            name, kernel, [total, total], (scale,),
            (other, outer, near_factor, far_factor, key_factors, *arrays, *(sums or ())), weight,
        )

    sums = terms("terms_own0", [(outer, [0]), (inner, [1]), (after(outer1, held), [2])], [(other, [8])], None, 100_000_000)
    def copy_kernel(block, out):
        out[...] = block[...]

    crossed = call(
        "crossed", copy_kernel, strip, (), (after(crossed, *sums),), 100_000_000
    )
    early, _ = lax.optimization_barrier((early, crossed))
    crossed = after(crossed, early)
    got = [
        crossed,
        send("gather1", crossed, line_to_line(2, 0)),
        send("gather2", crossed, line_to_line(1, 0)),
        send("gather3", crossed, line_to_line(3, 0)),
    ]
    inner1 = after(inner1, crossed)
    late = send("wide_late", inner1, to_next_wide)
    far2 = send("own_outer2", after(outer1, crossed), to_next_chip_sibling)
    near_sum, far_sum = sums

    def own1_kernel(s, oth, nf, kf, keys, near_in, near):
        near[...] = add_terms(
            near_in[...], oth[...], nf[:, :1], kf, s[0], [(keys[...], 3, False)]
        )

    near_sum = call(
        "terms_own1", own1_kernel, total, (scale,),
        (other, near_factor, key_factors, after(inner1, *got), near_sum), 100_000_000,
    )

    def merge_kernel(edge, early, late, q0, q1, q2, q3, out, sems):
        @pl.when(edge[0] == 1)
        def _():
            pieces = []
            for place, source in enumerate((q0, q1, q2, q3)):
                pieces.append((source, quarter, out, place * quarter, quarter))
                pieces.append((source, 0, out, rows + place * quarter, quarter))
            copy_all(sems, pieces)

        @pl.when(edge[0] == 0)
        def _():
            copy_all(sems, [(early, 2 * rows, out, 0, rows), (late, 0, out, rows, rows)])

    hop1 = assemble(
        "merge", merge_kernel, blocks(2), (at_edge,), (early, after(late, near_sum), *got), 8
    )
    back = send("edge_back", hop1, edge_to_previous_chip)
    sib1 = send("sibling_own1", jnp.concatenate([outer1, inner1], axis=0), to_sibling)
    is_edge = mirrored == 0
    hop_far2 = send("farthest", jnp.where(is_edge, hop1[:rows], far2), farthest_route)

    def near1_kernel(s, oth, nf, kf, keys, near_in, near):
        near[...] = add_terms(
            near_in[...], oth[...], nf[:, :1], kf, s[0], [(keys[...], 4, False)]
        )

    near_sum = call(
        "terms_near1", near1_kernel, total, (scale,),
        (other, near_factor, key_factors, after(hop1, far2), near_sum),
    )
    hop_sib1 = send("sibling_hop1", hop1, to_sibling)

    def far1_kernel(s, out, ff, kf, own, farthest, far_in, far):
        far[...] = add_terms(
            far_in[...], out[...], ff[:, :1], kf, s[0],
            [(own[...], 9, False), (farthest[...], 11, False)],
        )

    far_sum = call(
        "terms_far1", far1_kernel, total, (scale,),
        (outer, far_factor, key_factors, after(sib1, near_sum), far2, far_sum), 50_000_000,
    )

    def far2_kernel(s, out, ff, kf, hop, far_in, far):
        far[...] = add_terms(
            far_in[...], out[...], ff[:, :1], kf, s[0], [(hop[...], 12, False)]
        )

    far_sum = call(
        "terms_far2", far2_kernel, total, (scale,),
        (outer, far_factor, key_factors, hop_sib1, far_sum),
    )
    back = after(back, far_sum)
    hop_inner0 = jnp.where(is_edge, back[rows:], early[:rows])
    hop_sib0 = send("sibling_hop0", hop_inner0, to_sibling)
    anywhere = pl.BlockSpec(memory_space=pl.ANY)

    def near0_kernel(
        c, e, s, oth, nf, kf, inner0, back, early, near_in, image_grad, caption_grad, held_sum, sem
    ):
        outer0 = jnp.where(e[0] == 1, back[:rows, :], early[rows : 2 * rows, :])
        held_sum[...] = s[0] * add_terms(
            near_in[...], oth[...], nf[:, :1], kf, s[0],
            [(jnp.concatenate([inner0[...], outer0], axis=0), 6, False)],
        )

        @pl.when(c[0] == 1)
        def _():
            one = pltpu.make_async_copy(held_sum, image_grad, sem)
            one.start()
            one.wait()

        @pl.when(c[0] == 0)
        def _():
            one = pltpu.make_async_copy(held_sum, caption_grad, sem)
            one.start()
            one.wait()

    with jax.named_scope("terms_near0"):
        half_done = pl.pallas_call(
            near0_kernel,
            out_shape=[total, total],
            in_specs=[scalars()] * 3 + [whole()] * 7,
            out_specs=[anywhere] * 2,
            scratch_shapes=[pltpu.VMEM((rows, width), jnp.float32), pltpu.SemaphoreType.DMA],
            cost_estimate=pl.CostEstimate(
                flops=100_000_000_000, bytes_accessed=1000, transcendentals=0
            ),
            compiler_params=pltpu.CompilerParams(vmem_limit_bytes=16 * 1024 * 1024),
        )(
            core_flag, at_edge, scale,
            other, near_factor, key_factors, hop_inner0, back, early, near_sum,
        )

    def last_kernel(
        c, s, out, ff, kf, hs0, hf2, far_in, _i, _c, image_grad, caption_grad, held_sum, sem
    ):
        held_sum[...] = s[0] * add_terms(
            far_in[...], out[...], ff[:, :1], kf, s[0],
            [(jnp.concatenate([hs0[...], hf2[...]], axis=0), 14, False)],
        )

        @pl.when(c[0] == 1)
        def _():
            one = pltpu.make_async_copy(held_sum, caption_grad, sem)
            one.start()
            one.wait()

        @pl.when(c[0] == 0)
        def _():
            one = pltpu.make_async_copy(held_sum, image_grad, sem)
            one.start()
            one.wait()

    with jax.named_scope("terms_last"):
        image_grad, caption_grad = pl.pallas_call(
            last_kernel,
            out_shape=[total, total],
            in_specs=[scalars()] * 2 + [whole()] * 6 + [anywhere] * 2,
            out_specs=[anywhere] * 2,
            scratch_shapes=[pltpu.VMEM((rows, width), jnp.float32), pltpu.SemaphoreType.DMA],
            input_output_aliases={8: 0, 9: 1},
            cost_estimate=pl.CostEstimate(flops=1000, bytes_accessed=1000, transcendentals=0),
            compiler_params=pltpu.CompilerParams(vmem_limit_bytes=16 * 1024 * 1024),
        )(
            core_flag, scale,
            outer, far_factor, key_factors, hop_sib0, hop_far2, far_sum, *half_done,
        )
    return image_grad, caption_grad


def solution(mesh):
    in_specs = (P(("blk", "wide"), None), P(("blk", "wide"), None), P(), P(), P())
    out_specs = (P(("blk", "wide"), None), P(("blk", "wide"), None))
    return jax.shard_map(
        on_device, mesh=mesh, in_specs=in_specs, out_specs=out_specs, check_vma=False
    )
```

```python
import jax
import jax.numpy as jnp
from jax import lax
from jax.experimental import pallas as pl
from jax.experimental.pallas import tpu as pltpu
from jax.sharding import PartitionSpec as P

AXES = ("blk", "wide")
LOG2E = 1.4426950408889634


def coordinates(blk, wide):
    return wide // 8, (wide // 4) % 2, wide % 4, blk // 2, blk % 2


def device_id(x, half, y, z, core):
    return ((z % 8) * 2 + core) * 32 + ((x % 4) * 2 + half) * 4 + y


def pairs(target):
    found = []
    for blk in range(16):
        for wide in range(32):
            x, half, y, z, core = coordinates(blk, wide)
            sign = 1 if core == 1 else -1
            mirrored = y if core == 1 else 3 - y
            there = target(x, half, mirrored, z, core, sign)
            if there is not None:
                x2, half2, mirrored2, z2, core2 = there
                y2 = mirrored2 if core == 1 else 3 - mirrored2
                found.append((blk * 32 + wide, device_id(x2, half2, y2, z2, core2)))
    return found


def crossing(x, half, sign):
    if sign == 1:
        return (x, 1) if half == 0 else (x + 1, 0)
    return (x, 0) if half == 1 else (x - 1, 1)


def to_sibling(x, h, m, z, c, s):
    return x, h, m, z, 1 - c


def to_previous_chip_sibling(x, h, m, z, c, s):
    return x, h, m, z - s, 1 - c


def to_next_chip_sibling(x, h, m, z, c, s):
    return x, h, m, z + s, 1 - c


def to_next_chip(x, h, m, z, c, s):
    return x, h, m, z + s, c


def to_previous_chip(x, h, m, z, c, s):
    return x, h, m, z - s, c


def to_next_wide(x, h, m, z, c, s):
    return (x, h, m + 1, z, c) if m < 3 else None


def farthest_route(x, h, m, z, c, s):
    return (x, h, m - 1, z, c) if m > 0 else (x, h, m, z + s, 1 - c)


def edge_to_previous_chip(x, h, m, z, c, s):
    return (x, h, m, z - s, c) if m == 0 else None


def across(x, h, m, z, c, s):
    x2, h2 = crossing(x, h, s)
    return x2, h2, m, z + s, c


def line_to_line(here, there):
    return lambda x, h, m, z, c, s: (x, h, there, z, c) if m == here else None


def send(name, x, target):
    with jax.named_scope(name):
        return lax.ppermute(x, AXES, pairs(target))


def scalars():
    return pl.BlockSpec(memory_space=pltpu.SMEM)


def whole():
    return pl.BlockSpec(memory_space=pltpu.VMEM)


def call(name, kernel, out_shape, smem, vmem, weight=1):
    many = isinstance(out_shape, (list, tuple))
    outs = [whole() for _ in out_shape] if many else whole()
    with jax.named_scope(name):
        return pl.pallas_call(
            kernel,
            out_shape=out_shape,
            in_specs=[scalars() for _ in smem] + [whole() for _ in vmem],
            out_specs=outs,
            cost_estimate=pl.CostEstimate(
                flops=weight * 1000, bytes_accessed=1000, transcendentals=0
            ),
            compiler_params=pltpu.CompilerParams(vmem_limit_bytes=16 * 1024 * 1024),
        )(*smem, *vmem)


def assemble(name, kernel, out_shape, smem, arrays, copies):
    many = isinstance(out_shape, (list, tuple))
    with jax.named_scope(name):
        return pl.pallas_call(
            kernel,
            out_shape=out_shape,
            in_specs=[scalars() for _ in smem] + [pl.BlockSpec(memory_space=pl.ANY) for _ in arrays],
            out_specs=[whole() for _ in out_shape] if many else whole(),
            scratch_shapes=[pltpu.SemaphoreType.DMA((copies,))],
            cost_estimate=pl.CostEstimate(flops=1000, bytes_accessed=1000, transcendentals=0),
            compiler_params=pltpu.CompilerParams(vmem_limit_bytes=16 * 1024 * 1024),
        )(*smem, *arrays)


def copy_all(sems, pieces):
    moves = [
        pltpu.make_async_copy(
            source.at[pl.ds(low, count)], target.at[pl.ds(at, count)], sems.at[k]
        )
        for k, (source, low, target, at, count) in enumerate(pieces)
    ]
    for one in moves:
        one.start()
    for one in moves:
        one.wait()


def term(query, query_factor, keys, key_factor, scale, own=False):
    logits = lax.dot_general(
        query, keys, (((1,), (1,)), ((), ())), preferred_element_type=jnp.float32
    )
    weights = jnp.exp2(logits * (scale * LOG2E) - 5.0 * LOG2E) * (query_factor + key_factor)
    if own:
        rows = lax.broadcasted_iota(jnp.int32, weights.shape, 0)
        cols = lax.broadcasted_iota(jnp.int32, weights.shape, 1)
        weights = weights - jnp.where(rows == cols, 1.0, 0.0)
    return jnp.dot(weights.astype(jnp.bfloat16), keys, preferred_element_type=jnp.float32)


def add_terms(total, query, query_factor, key_factors, scale, items):
    rows = query.shape[0]
    for keys, place, own in items:
        chosen = key_factors[:, place * rows : place * rows + keys.shape[0]]
        part = term(query, query_factor, keys, chosen, scale, own)
        total = part if total is None else total + part
    return total


def cut_kernel(inner, outer, *outs):
    quarter = inner.shape[0] // 4
    for step in range(4):
        low = quarter * step
        outs[step][:quarter, :] = inner[low : low + quarter, :]
        outs[step][quarter:, :] = outer[low : low + quarter, :]


def on_device(images, captions, logit_scale, row_lse, col_lse):
    rows, width = images.shape
    quarter = rows // 4
    half = jnp.bfloat16
    blk = lax.axis_index("blk")
    wide = lax.axis_index("wide")
    core = blk % 2
    sign = 2 * core - 1
    y = wide % 4
    mirrored = jnp.where(core == 1, y, 3 - y)
    carries_captions = core == 1
    at_edge = jnp.where(mirrored == 0, 1, 0).astype(jnp.int32).reshape(1)
    core_flag = core.astype(jnp.int32).reshape(1)
    scale = logit_scale.reshape(1)

    def blocks(count):
        return jax.ShapeDtypeStruct((count * rows, width), half)

    outer = jnp.where(carries_captions, captions, images)
    other = jnp.where(carries_captions, images, captions)

    def after(value, *others):
        return lax.optimization_barrier((value, *others))[0]

    inner = send("swap", other, to_sibling)
    outer1 = send("own_outer1", outer, to_next_chip)
    inner1 = send("own_inner1", other, to_previous_chip_sibling)

    strip = jax.ShapeDtypeStruct((2 * quarter, width), half)
    cuts = call("cut", cut_kernel, [strip] * 4, (), (inner, outer))
    spread0 = send("spread0", cuts[0], line_to_line(3, 0))
    spread1 = send("spread1", cuts[1], line_to_line(3, 2))
    spread2 = send("spread2", cuts[2], line_to_line(3, 1))
    held = jnp.where(
        mirrored == 0,
        spread0,
        jnp.where(mirrored == 2, spread1, jnp.where(mirrored == 1, spread2, cuts[3])),
    )
    crossed = send("cross", held, across)
    early = send(
        "wide_early", jnp.concatenate([after(inner, held), outer, outer1], axis=0), to_next_wide
    )

    batch = row_lse.shape[0]

    def part(carried, b, w):
        start = ((b % 16) * 32 + (w % 32)) * rows
        from_rows = lax.dynamic_slice_in_dim(row_lse, start, rows)
        from_cols = lax.dynamic_slice_in_dim(col_lse, start, rows)
        return jnp.where(carries_captions == carried, from_cols, from_rows)

    pal = blk + 1 - 2 * core
    near_w, far_w = wide - sign, wide + sign
    own_outer = part(True, blk, wide)
    own_other = part(False, blk, wide)
    normalizers = [
        own_outer,
        part(True, pal, wide),
        part(True, blk - 2 * sign, wide),
        part(True, pal - 2 * sign, wide),
        part(True, blk - 2 * sign, near_w),
        part(True, pal - 2 * sign, near_w),
        part(True, pal, near_w),
        part(True, blk, near_w),
        own_other,
        part(False, pal + 2 * sign, wide),
        part(False, blk + 2 * sign, wide),
        part(False, pal + 4 * sign, wide),
        part(False, pal + 2 * sign, far_w),
        part(False, blk + 2 * sign, far_w),
        part(False, blk, far_w),
        part(False, pal + 4 * sign, far_w),
    ]

    def factors_kernel(*refs):
        sources, (keys, near, far) = refs[:-3], refs[-3:]
        for k, source in enumerate(sources):
            keys[:, k * rows : (k + 1) * rows] = 0.5 * jnp.exp(5.0 - source[...].reshape(1, rows))
        near[...] = jnp.broadcast_to(keys[:, 8 * rows : 9 * rows], (128, rows)).T
        far[...] = jnp.broadcast_to(keys[:, :rows], (128, rows)).T

    key_factors, near_factor, far_factor = call(
        "factors", factors_kernel,
        [jax.ShapeDtypeStruct(shape, jnp.float32) for shape in ((1, 16 * rows), (rows, 128), (rows, 128))],
        (), tuple(lax.optimization_barrier((*normalizers, held))[:-1]),
    )
    total = jax.ShapeDtypeStruct((rows, width), jnp.float32)

    def terms(name, near_blocks, far_blocks, sums, weight=1):
        arrays = [array for array, _ in near_blocks + far_blocks]

        def kernel(s, oth, out, nf, ff, kf, *refs):
            keys, refs = refs[: len(arrays)], refs[len(arrays) :]
            starts, ends = (refs[:2], refs[2:]) if sums else ((None, None), refs)

            def add(start, query, query_factor, blocks, refs, end):
                items = []
                for ref, (_, places) in zip(refs, blocks):
                    for k, row in enumerate(places):
                        if row is None:
                            continue
                        items.append((ref[k * rows : (k + 1) * rows, :], row, row in (0, 8)))
                before = None if start is None else start[...]
                end[...] = add_terms(before, query[...], query_factor[:, :1], kf, s[0], items)

            add(starts[0], oth, nf, near_blocks, keys[: len(near_blocks)], ends[0])
            add(starts[1], out, ff, far_blocks, keys[len(near_blocks) :], ends[1])

        return call(
            name, kernel, [total, total], (scale,),
            (other, outer, near_factor, far_factor, key_factors, *arrays, *(sums or ())), weight,
        )

    sums = terms("terms_own0", [(outer, [0]), (inner, [1]), (after(outer1, held), [2])], [(other, [8])], None, 100_000_000)
    def copy_kernel(block, out):
        out[...] = block[...]

    crossed = call(
        "crossed", copy_kernel, strip, (), (after(crossed, *sums),), 100_000_000
    )
    early, _ = lax.optimization_barrier((early, crossed))
    crossed = after(crossed, early)
    got = [
        crossed,
        send("gather1", crossed, line_to_line(2, 0)),
        send("gather2", crossed, line_to_line(1, 0)),
        send("gather3", crossed, line_to_line(3, 0)),
    ]

    def gather_kernel(q0, q1, q2, q3, out, sems):
        pieces = []
        for place, source in enumerate((q0, q1, q2, q3)):
            pieces.append((source, quarter, out, place * quarter, quarter))
            pieces.append((source, 0, out, rows + place * quarter, quarter))
        copy_all(sems, pieces)

    whole_blocks = assemble("whole_blocks", gather_kernel, blocks(2), (), tuple(got), 8)
    back = send("edge_back", whole_blocks, edge_to_previous_chip)
    inner1 = after(inner1, crossed)
    late = send("wide_late", inner1, to_next_wide)
    far2 = send("own_outer2", after(outer1, crossed), to_next_chip_sibling)
    near_sum, far_sum = sums

    def own1_kernel(s, oth, nf, kf, keys, near_in, near):
        near[...] = add_terms(
            near_in[...], oth[...], nf[:, :1], kf, s[0], [(keys[...], 3, False)]
        )

    near_sum = call(
        "terms_own1", own1_kernel, total, (scale,),
        (other, near_factor, key_factors, after(inner1, whole_blocks), near_sum), 100_000_000,
    )

    def merge_kernel(edge, early, late, gathered, out, sems):
        @pl.when(edge[0] == 1)
        def _():
            copy_all(sems, [(gathered, 0, out, 0, 2 * rows)])

        @pl.when(edge[0] == 0)
        def _():
            copy_all(sems, [(early, 2 * rows, out, 0, rows), (late, 0, out, rows, rows)])

    hop1 = assemble(
        "merge", merge_kernel, blocks(2), (at_edge,),
        (early, after(late, near_sum), whole_blocks), 2,
    )
    hop_sib1 = send("sibling_hop1", hop1, to_sibling)
    sib1 = send(
        "sibling_own1", jnp.concatenate([outer1, inner1], axis=0), to_sibling
    )
    is_edge = mirrored == 0

    def near1_kernel(s, oth, nf, kf, keys, near_in, near):
        near[...] = add_terms(
            near_in[...], oth[...], nf[:, :1], kf, s[0], [(keys[...], 4, False)]
        )

    near_sum = call(
        "terms_near1", near1_kernel, total, (scale,),
        (other, near_factor, key_factors, after(hop1, far2), near_sum),
    )
    hop_sib1 = send("sibling_hop1", hop1, to_sibling)

    def far1_kernel(s, out, ff, kf, own, farthest, far_in, far):
        far[...] = add_terms(
            far_in[...], out[...], ff[:, :1], kf, s[0],
            [(own[...], 9, False), (farthest[...], 11, False)],
        )

    far_sum = call(
        "terms_far1", far1_kernel, total, (scale,),
        (outer, far_factor, key_factors, after(sib1, near_sum), far2, far_sum), 50_000_000,
    )

    hop_far2 = send(
        "farthest", jnp.where(is_edge, hop1[:rows], after(far2, far_sum)), farthest_route
    )

    def far2_kernel(s, out, ff, kf, hop, far_in, far):
        far[...] = add_terms(
            far_in[...], out[...], ff[:, :1], kf, s[0], [(hop[...], 12, False)]
        )

    far_sum = call(
        "terms_far2", far2_kernel, total, (scale,),
        (outer, far_factor, key_factors, hop_sib1, far_sum),
    )
    back = after(back, far_sum)
    hop_inner0 = jnp.where(is_edge, back[rows:], early[:rows])
    hop_sib0 = send("sibling_hop0", hop_inner0, to_sibling)
    anywhere = pl.BlockSpec(memory_space=pl.ANY)

    def near0_kernel(
        c, e, s, oth, nf, kf, inner0, back, early, near_in, image_grad, caption_grad, held_sum, sem
    ):
        outer0 = jnp.where(e[0] == 1, back[:rows, :], early[rows : 2 * rows, :])
        held_sum[...] = s[0] * add_terms(
            near_in[...], oth[...], nf[:, :1], kf, s[0],
            [(jnp.concatenate([inner0[...], outer0], axis=0), 6, False)],
        )

        @pl.when(c[0] == 1)
        def _():
            one = pltpu.make_async_copy(held_sum, image_grad, sem)
            one.start()
            one.wait()

        @pl.when(c[0] == 0)
        def _():
            one = pltpu.make_async_copy(held_sum, caption_grad, sem)
            one.start()
            one.wait()

    with jax.named_scope("terms_near0"):
        half_done = pl.pallas_call(
            near0_kernel,
            out_shape=[total, total],
            in_specs=[scalars()] * 3 + [whole()] * 7,
            out_specs=[anywhere] * 2,
            scratch_shapes=[pltpu.VMEM((rows, width), jnp.float32), pltpu.SemaphoreType.DMA],
            cost_estimate=pl.CostEstimate(
                flops=100_000_000_000, bytes_accessed=1000, transcendentals=0
            ),
            compiler_params=pltpu.CompilerParams(vmem_limit_bytes=16 * 1024 * 1024),
        )(
            core_flag, at_edge, scale,
            other, near_factor, key_factors, hop_inner0, back, early, near_sum,
        )

    def last_kernel(
        c, s, out, ff, kf, hs0, hf2, far_in, _i, _c, image_grad, caption_grad, held_sum, sem
    ):
        held_sum[...] = s[0] * add_terms(
            far_in[...], out[...], ff[:, :1], kf, s[0],
            [(jnp.concatenate([hs0[...], hf2[...]], axis=0), 14, False)],
        )

        @pl.when(c[0] == 1)
        def _():
            one = pltpu.make_async_copy(held_sum, caption_grad, sem)
            one.start()
            one.wait()

        @pl.when(c[0] == 0)
        def _():
            one = pltpu.make_async_copy(held_sum, image_grad, sem)
            one.start()
            one.wait()

    with jax.named_scope("terms_last"):
        image_grad, caption_grad = pl.pallas_call(
            last_kernel,
            out_shape=[total, total],
            in_specs=[scalars()] * 2 + [whole()] * 6 + [anywhere] * 2,
            out_specs=[anywhere] * 2,
            scratch_shapes=[pltpu.VMEM((rows, width), jnp.float32), pltpu.SemaphoreType.DMA],
            input_output_aliases={8: 0, 9: 1},
            cost_estimate=pl.CostEstimate(flops=1000, bytes_accessed=1000, transcendentals=0),
            compiler_params=pltpu.CompilerParams(vmem_limit_bytes=16 * 1024 * 1024),
        )(
            core_flag, scale,
            outer, far_factor, key_factors, hop_sib0, hop_far2, far_sum, *half_done,
        )
    return image_grad, caption_grad


def solution(mesh):
    in_specs = (P(("blk", "wide"), None), P(("blk", "wide"), None), P(), P(), P())
    out_specs = (P(("blk", "wide"), None), P(("blk", "wide"), None))
    return jax.shard_map(
        on_device, mesh=mesh, in_specs=in_specs, out_specs=out_specs, check_vma=False
    )
```

```python
import jax
import jax.numpy as jnp
from jax import lax
from jax.experimental import pallas as pl
from jax.experimental.pallas import tpu as pltpu
from jax.sharding import PartitionSpec as P

AXES = ("blk", "wide")
LOG2E = 1.4426950408889634


def coordinates(blk, wide):
    return wide // 8, (wide // 4) % 2, wide % 4, blk // 2, blk % 2


def device_id(x, half, y, z, core):
    return ((z % 8) * 2 + core) * 32 + ((x % 4) * 2 + half) * 4 + y


def pairs(target):
    found = []
    for blk in range(16):
        for wide in range(32):
            x, half, y, z, core = coordinates(blk, wide)
            sign = 1 if core == 1 else -1
            mirrored = y if core == 1 else 3 - y
            there = target(x, half, mirrored, z, core, sign)
            if there is not None:
                x2, half2, mirrored2, z2, core2 = there
                y2 = mirrored2 if core == 1 else 3 - mirrored2
                found.append((blk * 32 + wide, device_id(x2, half2, y2, z2, core2)))
    return found


def crossing(x, half, sign):
    if sign == 1:
        return (x, 1) if half == 0 else (x + 1, 0)
    return (x, 0) if half == 1 else (x - 1, 1)


def to_sibling(x, h, m, z, c, s):
    return x, h, m, z, 1 - c


def to_previous_chip_sibling(x, h, m, z, c, s):
    return x, h, m, z - s, 1 - c


def to_next_chip_sibling(x, h, m, z, c, s):
    return x, h, m, z + s, 1 - c


def to_next_chip(x, h, m, z, c, s):
    return x, h, m, z + s, c


def to_previous_chip(x, h, m, z, c, s):
    return x, h, m, z - s, c


def to_next_wide(x, h, m, z, c, s):
    return (x, h, m + 1, z, c) if m < 3 else None


def farthest_route(x, h, m, z, c, s):
    return (x, h, m - 1, z, c) if m > 0 else (x, h, m, z + s, 1 - c)


def edge_to_previous_chip(x, h, m, z, c, s):
    return (x, h, m, z - s, c) if m == 0 else None


def across(x, h, m, z, c, s):
    x2, h2 = crossing(x, h, s)
    return x2, h2, m, z + s, c


def line_to_line(here, there):
    return lambda x, h, m, z, c, s: (x, h, there, z, c) if m == here else None


def send(name, x, target):
    with jax.named_scope(name):
        return lax.ppermute(x, AXES, pairs(target))


def scalars():
    return pl.BlockSpec(memory_space=pltpu.SMEM)


def whole():
    return pl.BlockSpec(memory_space=pltpu.VMEM)


def call(name, kernel, out_shape, smem, vmem, weight=1):
    many = isinstance(out_shape, (list, tuple))
    outs = [whole() for _ in out_shape] if many else whole()
    with jax.named_scope(name):
        return pl.pallas_call(
            kernel,
            out_shape=out_shape,
            in_specs=[scalars() for _ in smem] + [whole() for _ in vmem],
            out_specs=outs,
            cost_estimate=pl.CostEstimate(
                flops=weight * 1000, bytes_accessed=1000, transcendentals=0
            ),
            compiler_params=pltpu.CompilerParams(vmem_limit_bytes=16 * 1024 * 1024),
        )(*smem, *vmem)


def assemble(name, kernel, out_shape, smem, arrays, copies):
    many = isinstance(out_shape, (list, tuple))
    with jax.named_scope(name):
        return pl.pallas_call(
            kernel,
            out_shape=out_shape,
            in_specs=[scalars() for _ in smem] + [pl.BlockSpec(memory_space=pl.ANY) for _ in arrays],
            out_specs=[whole() for _ in out_shape] if many else whole(),
            scratch_shapes=[pltpu.SemaphoreType.DMA((copies,))],
            cost_estimate=pl.CostEstimate(flops=1000, bytes_accessed=1000, transcendentals=0),
            compiler_params=pltpu.CompilerParams(vmem_limit_bytes=16 * 1024 * 1024),
        )(*smem, *arrays)


def copy_all(sems, pieces):
    moves = [
        pltpu.make_async_copy(
            source.at[pl.ds(low, count)], target.at[pl.ds(at, count)], sems.at[k]
        )
        for k, (source, low, target, at, count) in enumerate(pieces)
    ]
    for one in moves:
        one.start()
    for one in moves:
        one.wait()


def term(query, query_factor, keys, key_factor, scale, own=False):
    logits = lax.dot_general(
        query, keys, (((1,), (1,)), ((), ())), preferred_element_type=jnp.float32
    )
    weights = jnp.exp2(logits * (scale * LOG2E) - 5.0 * LOG2E) * (query_factor + key_factor)
    if own:
        rows = lax.broadcasted_iota(jnp.int32, weights.shape, 0)
        cols = lax.broadcasted_iota(jnp.int32, weights.shape, 1)
        weights = weights - jnp.where(rows == cols, 1.0, 0.0)
    return jnp.dot(weights.astype(jnp.bfloat16), keys, preferred_element_type=jnp.float32)


def add_terms(total, query, query_factor, key_factors, scale, items):
    rows = query.shape[0]
    for keys, place, own in items:
        chosen = key_factors[:, place * rows : place * rows + keys.shape[0]]
        part = term(query, query_factor, keys, chosen, scale, own)
        total = part if total is None else total + part
    return total


def cut_kernel(inner, outer, *outs):
    quarter = inner.shape[0] // 4
    for step in range(4):
        low = quarter * step
        outs[step][:quarter, :] = inner[low : low + quarter, :]
        outs[step][quarter:, :] = outer[low : low + quarter, :]


def on_device(images, captions, logit_scale, row_lse, col_lse):
    rows, width = images.shape
    quarter = rows // 4
    half = jnp.bfloat16
    blk = lax.axis_index("blk")
    wide = lax.axis_index("wide")
    core = blk % 2
    sign = 2 * core - 1
    y = wide % 4
    mirrored = jnp.where(core == 1, y, 3 - y)
    carries_captions = core == 1
    at_edge = jnp.where(mirrored == 0, 1, 0).astype(jnp.int32).reshape(1)
    core_flag = core.astype(jnp.int32).reshape(1)
    scale = logit_scale.reshape(1)

    def blocks(count):
        return jax.ShapeDtypeStruct((count * rows, width), half)

    outer = jnp.where(carries_captions, captions, images)
    other = jnp.where(carries_captions, images, captions)

    def after(value, *others):
        return lax.optimization_barrier((value, *others))[0]

    inner = send("swap", other, to_sibling)
    outer1 = send("own_outer1", outer, to_next_chip)
    inner1 = send("own_inner1", other, to_previous_chip_sibling)

    strip = jax.ShapeDtypeStruct((2 * quarter, width), half)
    cuts = call("cut", cut_kernel, [strip] * 4, (), (inner, outer))
    spread0 = send("spread0", cuts[0], line_to_line(3, 0))
    spread1 = send("spread1", cuts[1], line_to_line(3, 2))
    spread2 = send("spread2", cuts[2], line_to_line(3, 1))
    held = jnp.where(
        mirrored == 0,
        spread0,
        jnp.where(mirrored == 2, spread1, jnp.where(mirrored == 1, spread2, cuts[3])),
    )
    crossed = send("cross", held, across)
    early = send(
        "wide_early", jnp.concatenate([after(inner, held), outer, outer1], axis=0), to_next_wide
    )

    batch = row_lse.shape[0]

    def part(carried, b, w):
        start = ((b % 16) * 32 + (w % 32)) * rows
        from_rows = lax.dynamic_slice_in_dim(row_lse, start, rows)
        from_cols = lax.dynamic_slice_in_dim(col_lse, start, rows)
        return jnp.where(carries_captions == carried, from_cols, from_rows)

    pal = blk + 1 - 2 * core
    near_w, far_w = wide - sign, wide + sign
    own_outer = part(True, blk, wide)
    own_other = part(False, blk, wide)
    normalizers = [
        own_outer,
        part(True, pal, wide),
        part(True, blk - 2 * sign, wide),
        part(True, pal - 2 * sign, wide),
        part(True, blk - 2 * sign, near_w),
        part(True, pal - 2 * sign, near_w),
        part(True, pal, near_w),
        part(True, blk, near_w),
        own_other,
        part(False, pal + 2 * sign, wide),
        part(False, blk + 2 * sign, wide),
        part(False, pal + 4 * sign, wide),
        part(False, pal + 2 * sign, far_w),
        part(False, blk + 2 * sign, far_w),
        part(False, blk, far_w),
        part(False, pal + 4 * sign, far_w),
    ]

    def factors_kernel(*refs):
        sources, (keys, near, far) = refs[:-3], refs[-3:]
        for k, source in enumerate(sources):
            keys[:, k * rows : (k + 1) * rows] = 0.5 * jnp.exp(5.0 - source[...].reshape(1, rows))
        near[...] = jnp.broadcast_to(keys[:, 8 * rows : 9 * rows], (128, rows)).T
        far[...] = jnp.broadcast_to(keys[:, :rows], (128, rows)).T

    key_factors, near_factor, far_factor = call(
        "factors", factors_kernel,
        [jax.ShapeDtypeStruct(shape, jnp.float32) for shape in ((1, 16 * rows), (rows, 128), (rows, 128))],
        (), tuple(lax.optimization_barrier((*normalizers, held))[:-1]),
    )
    total = jax.ShapeDtypeStruct((rows, width), jnp.float32)

    def terms(name, near_blocks, far_blocks, sums, weight=1):
        arrays = [array for array, _ in near_blocks + far_blocks]

        def kernel(s, oth, out, nf, ff, kf, *refs):
            keys, refs = refs[: len(arrays)], refs[len(arrays) :]
            starts, ends = (refs[:2], refs[2:]) if sums else ((None, None), refs)

            def add(start, query, query_factor, blocks, refs, end):
                items = []
                for ref, (_, places) in zip(refs, blocks):
                    for k, row in enumerate(places):
                        if row is None:
                            continue
                        items.append((ref[k * rows : (k + 1) * rows, :], row, row in (0, 8)))
                before = None if start is None else start[...]
                end[...] = add_terms(before, query[...], query_factor[:, :1], kf, s[0], items)

            add(starts[0], oth, nf, near_blocks, keys[: len(near_blocks)], ends[0])
            add(starts[1], out, ff, far_blocks, keys[len(near_blocks) :], ends[1])

        return call(
            name, kernel, [total, total], (scale,),
            (other, outer, near_factor, far_factor, key_factors, *arrays, *(sums or ())), weight,
        )

    sums = terms("terms_own0", [(outer, [0]), (inner, [1]), (after(outer1, held), [2])], [(other, [8])], None, 100_000_000)
    def copy_kernel(block, out):
        out[...] = block[...]

    crossed = call(
        "crossed", copy_kernel, strip, (), (after(crossed, *sums),), 100_000_000
    )
    early, _ = lax.optimization_barrier((early, crossed))
    crossed = after(crossed, early)
    got = [
        crossed,
        send("gather1", crossed, line_to_line(2, 0)),
        send("gather2", crossed, line_to_line(1, 0)),
        send("gather3", crossed, line_to_line(3, 0)),
    ]

    def gather_kernel(q0, q1, q2, q3, out, sems):
        pieces = []
        for place, source in enumerate((q0, q1, q2, q3)):
            pieces.append((source, quarter, out, place * quarter, quarter))
            pieces.append((source, 0, out, rows + place * quarter, quarter))
        copy_all(sems, pieces)

    whole_blocks = assemble("whole_blocks", gather_kernel, blocks(2), (), tuple(got), 8)
    back = send("edge_back", whole_blocks, edge_to_previous_chip)
    inner1 = after(inner1, crossed)
    late = send("wide_late", inner1, to_next_wide)
    far2 = send("own_outer2", after(outer1, crossed), to_next_chip_sibling)
    near_sum, far_sum = sums

    def own1_kernel(s, oth, nf, kf, keys, near_in, near):
        near[...] = add_terms(
            near_in[...], oth[...], nf[:, :1], kf, s[0], [(keys[...], 3, False)]
        )

    near_sum = call(
        "terms_own1", own1_kernel, total, (scale,),
        (other, near_factor, key_factors, after(inner1, whole_blocks, far2), near_sum), 100_000_000,
    )

    def merge_kernel(edge, early, late, gathered, out, sems):
        @pl.when(edge[0] == 1)
        def _():
            copy_all(sems, [(gathered, 0, out, 0, 2 * rows)])

        @pl.when(edge[0] == 0)
        def _():
            copy_all(sems, [(early, 2 * rows, out, 0, rows), (late, 0, out, rows, rows)])

    hop1 = assemble(
        "merge", merge_kernel, blocks(2), (at_edge,),
        (early, after(late, near_sum), whole_blocks), 2,
    )
    hop_sib1 = send("sibling_hop1", hop1, to_sibling)
    sib1 = send(
        "sibling_own1", jnp.concatenate([outer1, inner1], axis=0), to_sibling
    )
    is_edge = mirrored == 0

    def near1_kernel(s, oth, nf, kf, keys, near_in, near):
        near[...] = add_terms(
            near_in[...], oth[...], nf[:, :1], kf, s[0], [(keys[...], 4, False)]
        )

    near_sum = call(
        "terms_near1", near1_kernel, total, (scale,),
        (other, near_factor, key_factors, hop1, near_sum),
    )
    hop_sib1 = send("sibling_hop1", hop1, to_sibling)

    def far1_kernel(s, out, ff, kf, own, farthest, far_in, far):
        far[...] = add_terms(
            far_in[...], out[...], ff[:, :1], kf, s[0],
            [(own[...], 9, False), (farthest[...], 11, False)],
        )

    far_sum = call(
        "terms_far1", far1_kernel, total, (scale,),
        (outer, far_factor, key_factors, after(sib1, near_sum), far2, far_sum), 50_000_000,
    )

    hop_far2 = send(
        "farthest", jnp.where(is_edge, hop1[:rows], after(far2, far_sum)), farthest_route
    )

    def far2_kernel(s, out, ff, kf, hop, far_in, far):
        far[...] = add_terms(
            far_in[...], out[...], ff[:, :1], kf, s[0], [(hop[...], 12, False)]
        )

    far_sum = call(
        "terms_far2", far2_kernel, total, (scale,),
        (outer, far_factor, key_factors, hop_sib1, far_sum),
    )
    back = after(back, far_sum)
    hop_inner0 = jnp.where(is_edge, back[rows:], early[:rows])
    hop_sib0 = send("sibling_hop0", hop_inner0, to_sibling)
    anywhere = pl.BlockSpec(memory_space=pl.ANY)

    def near0_kernel(
        c, e, s, oth, nf, kf, inner0, back, early, near_in, image_grad, caption_grad, held_sum, sem
    ):
        outer0 = jnp.where(e[0] == 1, back[:rows, :], early[rows : 2 * rows, :])
        held_sum[...] = s[0] * add_terms(
            near_in[...], oth[...], nf[:, :1], kf, s[0],
            [(jnp.concatenate([inner0[...], outer0], axis=0), 6, False)],
        )

        @pl.when(c[0] == 1)
        def _():
            one = pltpu.make_async_copy(held_sum, image_grad, sem)
            one.start()
            one.wait()

        @pl.when(c[0] == 0)
        def _():
            one = pltpu.make_async_copy(held_sum, caption_grad, sem)
            one.start()
            one.wait()

    with jax.named_scope("terms_near0"):
        half_done = pl.pallas_call(
            near0_kernel,
            out_shape=[total, total],
            in_specs=[scalars()] * 3 + [whole()] * 7,
            out_specs=[anywhere] * 2,
            scratch_shapes=[pltpu.VMEM((rows, width), jnp.float32), pltpu.SemaphoreType.DMA],
            cost_estimate=pl.CostEstimate(
                flops=100_000_000_000, bytes_accessed=1000, transcendentals=0
            ),
            compiler_params=pltpu.CompilerParams(vmem_limit_bytes=16 * 1024 * 1024),
        )(
            core_flag, at_edge, scale,
            other, near_factor, key_factors, hop_inner0, back, early, near_sum,
        )

    def last_kernel(
        c, s, out, ff, kf, hs0, hf2, far_in, _i, _c, image_grad, caption_grad, held_sum, sem
    ):
        held_sum[...] = s[0] * add_terms(
            far_in[...], out[...], ff[:, :1], kf, s[0],
            [(jnp.concatenate([hs0[...], hf2[...]], axis=0), 14, False)],
        )

        @pl.when(c[0] == 1)
        def _():
            one = pltpu.make_async_copy(held_sum, caption_grad, sem)
            one.start()
            one.wait()

        @pl.when(c[0] == 0)
        def _():
            one = pltpu.make_async_copy(held_sum, image_grad, sem)
            one.start()
            one.wait()

    with jax.named_scope("terms_last"):
        image_grad, caption_grad = pl.pallas_call(
            last_kernel,
            out_shape=[total, total],
            in_specs=[scalars()] * 2 + [whole()] * 6 + [anywhere] * 2,
            out_specs=[anywhere] * 2,
            scratch_shapes=[pltpu.VMEM((rows, width), jnp.float32), pltpu.SemaphoreType.DMA],
            input_output_aliases={8: 0, 9: 1},
            cost_estimate=pl.CostEstimate(flops=1000, bytes_accessed=1000, transcendentals=0),
            compiler_params=pltpu.CompilerParams(vmem_limit_bytes=16 * 1024 * 1024),
        )(
            core_flag, scale,
            outer, far_factor, key_factors, hop_sib0, hop_far2, far_sum, *half_done,
        )
    return image_grad, caption_grad


def solution(mesh):
    in_specs = (P(("blk", "wide"), None), P(("blk", "wide"), None), P(), P(), P())
    out_specs = (P(("blk", "wide"), None), P(("blk", "wide"), None))
    return jax.shard_map(
        on_device, mesh=mesh, in_specs=in_specs, out_specs=out_specs, check_vma=False
    )
```

```python
import jax
import jax.numpy as jnp
from jax import lax
from jax.experimental import pallas as pl
from jax.experimental.pallas import tpu as pltpu
from jax.sharding import PartitionSpec as P

AXES = ("blk", "wide")
LOG2E = 1.4426950408889634


def coordinates(blk, wide):
    return wide // 8, (wide // 4) % 2, wide % 4, blk // 2, blk % 2


def device_id(x, half, y, z, core):
    return ((z % 8) * 2 + core) * 32 + ((x % 4) * 2 + half) * 4 + y


def pairs(target):
    found = []
    for blk in range(16):
        for wide in range(32):
            x, half, y, z, core = coordinates(blk, wide)
            sign = 1 if core == 1 else -1
            mirrored = y if core == 1 else 3 - y
            there = target(x, half, mirrored, z, core, sign)
            if there is not None:
                x2, half2, mirrored2, z2, core2 = there
                y2 = mirrored2 if core == 1 else 3 - mirrored2
                found.append((blk * 32 + wide, device_id(x2, half2, y2, z2, core2)))
    return found


def crossing(x, half, sign):
    if sign == 1:
        return (x, 1) if half == 0 else (x + 1, 0)
    return (x, 0) if half == 1 else (x - 1, 1)


def to_sibling(x, h, m, z, c, s):
    return x, h, m, z, 1 - c


def to_previous_chip_sibling(x, h, m, z, c, s):
    return x, h, m, z - s, 1 - c


def to_next_chip_sibling(x, h, m, z, c, s):
    return x, h, m, z + s, 1 - c


def to_next_chip(x, h, m, z, c, s):
    return x, h, m, z + s, c


def to_previous_chip(x, h, m, z, c, s):
    return x, h, m, z - s, c


def to_next_wide(x, h, m, z, c, s):
    return (x, h, m + 1, z, c) if m < 3 else None


def farthest_route(x, h, m, z, c, s):
    return (x, h, m - 1, z, c) if m > 0 else (x, h, m, z + s, 1 - c)


def edge_to_previous_chip(x, h, m, z, c, s):
    return (x, h, m, z - s, c) if m == 0 else None


def across(x, h, m, z, c, s):
    x2, h2 = crossing(x, h, s)
    return x2, h2, m, z + s, c


def line_to_line(here, there):
    return lambda x, h, m, z, c, s: (x, h, there, z, c) if m == here else None


def send(name, x, target):
    with jax.named_scope(name):
        return lax.ppermute(x, AXES, pairs(target))


def scalars():
    return pl.BlockSpec(memory_space=pltpu.SMEM)


def whole():
    return pl.BlockSpec(memory_space=pltpu.VMEM)


def call(name, kernel, out_shape, smem, vmem, weight=1):
    many = isinstance(out_shape, (list, tuple))
    outs = [whole() for _ in out_shape] if many else whole()
    with jax.named_scope(name):
        return pl.pallas_call(
            kernel,
            out_shape=out_shape,
            in_specs=[scalars() for _ in smem] + [whole() for _ in vmem],
            out_specs=outs,
            cost_estimate=pl.CostEstimate(
                flops=weight * 1000, bytes_accessed=1000, transcendentals=0
            ),
            compiler_params=pltpu.CompilerParams(vmem_limit_bytes=16 * 1024 * 1024),
        )(*smem, *vmem)


def assemble(name, kernel, out_shape, smem, arrays, copies):
    many = isinstance(out_shape, (list, tuple))
    with jax.named_scope(name):
        return pl.pallas_call(
            kernel,
            out_shape=out_shape,
            in_specs=[scalars() for _ in smem] + [pl.BlockSpec(memory_space=pl.ANY) for _ in arrays],
            out_specs=[whole() for _ in out_shape] if many else whole(),
            scratch_shapes=[pltpu.SemaphoreType.DMA((copies,))],
            cost_estimate=pl.CostEstimate(flops=1000, bytes_accessed=1000, transcendentals=0),
            compiler_params=pltpu.CompilerParams(vmem_limit_bytes=16 * 1024 * 1024),
        )(*smem, *arrays)


def copy_all(sems, pieces):
    moves = [
        pltpu.make_async_copy(
            source.at[pl.ds(low, count)], target.at[pl.ds(at, count)], sems.at[k]
        )
        for k, (source, low, target, at, count) in enumerate(pieces)
    ]
    for one in moves:
        one.start()
    for one in moves:
        one.wait()


def term(query, query_factor, keys, key_factor, scale, own=False):
    logits = lax.dot_general(
        query, keys, (((1,), (1,)), ((), ())), preferred_element_type=jnp.float32
    )
    weights = jnp.exp2(logits * (scale * LOG2E) - 5.0 * LOG2E) * (query_factor + key_factor)
    if own:
        rows = lax.broadcasted_iota(jnp.int32, weights.shape, 0)
        cols = lax.broadcasted_iota(jnp.int32, weights.shape, 1)
        weights = weights - jnp.where(rows == cols, 1.0, 0.0)
    return jnp.dot(weights.astype(jnp.bfloat16), keys, preferred_element_type=jnp.float32)


def add_terms(total, query, query_factor, key_factors, scale, items):
    rows = query.shape[0]
    for keys, place, own in items:
        chosen = key_factors[:, place * rows : place * rows + keys.shape[0]]
        part = term(query, query_factor, keys, chosen, scale, own)
        total = part if total is None else total + part
    return total


def cut_kernel(inner, outer, *outs):
    quarter = inner.shape[0] // 4
    for step in range(4):
        low = quarter * step
        outs[step][:quarter, :] = inner[low : low + quarter, :]
        outs[step][quarter:, :] = outer[low : low + quarter, :]


def on_device(images, captions, logit_scale, row_lse, col_lse):
    rows, width = images.shape
    quarter = rows // 4
    half = jnp.bfloat16
    blk = lax.axis_index("blk")
    wide = lax.axis_index("wide")
    core = blk % 2
    sign = 2 * core - 1
    y = wide % 4
    mirrored = jnp.where(core == 1, y, 3 - y)
    carries_captions = core == 1
    at_edge = jnp.where(mirrored == 0, 1, 0).astype(jnp.int32).reshape(1)
    core_flag = core.astype(jnp.int32).reshape(1)
    scale = logit_scale.reshape(1)

    def blocks(count):
        return jax.ShapeDtypeStruct((count * rows, width), half)

    outer = jnp.where(carries_captions, captions, images)
    other = jnp.where(carries_captions, images, captions)

    def after(value, *others):
        return lax.optimization_barrier((value, *others))[0]

    inner = send("swap", other, to_sibling)
    outer1 = send("own_outer1", outer, to_next_chip)
    inner1 = send("own_inner1", other, to_previous_chip_sibling)

    strip = jax.ShapeDtypeStruct((2 * quarter, width), half)
    cuts = call("cut", cut_kernel, [strip] * 4, (), (inner, outer))
    spread0 = send("spread0", cuts[0], line_to_line(3, 0))
    spread1 = send("spread1", cuts[1], line_to_line(3, 2))
    spread2 = send("spread2", cuts[2], line_to_line(3, 1))
    held = jnp.where(
        mirrored == 0,
        spread0,
        jnp.where(mirrored == 2, spread1, jnp.where(mirrored == 1, spread2, cuts[3])),
    )
    crossed = send("cross", held, across)
    early = send(
        "wide_early", jnp.concatenate([after(inner, held), outer, outer1], axis=0), to_next_wide
    )

    batch = row_lse.shape[0]

    def part(carried, b, w):
        start = ((b % 16) * 32 + (w % 32)) * rows
        from_rows = lax.dynamic_slice_in_dim(row_lse, start, rows)
        from_cols = lax.dynamic_slice_in_dim(col_lse, start, rows)
        return jnp.where(carries_captions == carried, from_cols, from_rows)

    pal = blk + 1 - 2 * core
    near_w, far_w = wide - sign, wide + sign
    own_outer = part(True, blk, wide)
    own_other = part(False, blk, wide)
    normalizers = [
        own_outer,
        part(True, pal, wide),
        part(True, blk - 2 * sign, wide),
        part(True, pal - 2 * sign, wide),
        part(True, blk - 2 * sign, near_w),
        part(True, pal - 2 * sign, near_w),
        part(True, pal, near_w),
        part(True, blk, near_w),
        own_other,
        part(False, pal + 2 * sign, wide),
        part(False, blk + 2 * sign, wide),
        part(False, pal + 4 * sign, wide),
        part(False, pal + 2 * sign, far_w),
        part(False, blk + 2 * sign, far_w),
        part(False, blk, far_w),
        part(False, pal + 4 * sign, far_w),
    ]

    def factors_kernel(*refs):
        sources, (keys, near, far) = refs[:-3], refs[-3:]
        for k, source in enumerate(sources):
            keys[:, k * rows : (k + 1) * rows] = 0.5 * jnp.exp(5.0 - source[...].reshape(1, rows))
        near[...] = jnp.broadcast_to(keys[:, 8 * rows : 9 * rows], (128, rows)).T
        far[...] = jnp.broadcast_to(keys[:, :rows], (128, rows)).T

    key_factors, near_factor, far_factor = call(
        "factors", factors_kernel,
        [jax.ShapeDtypeStruct(shape, jnp.float32) for shape in ((1, 16 * rows), (rows, 128), (rows, 128))],
        (), tuple(lax.optimization_barrier((*normalizers, held))[:-1]),
    )
    total = jax.ShapeDtypeStruct((rows, width), jnp.float32)

    def terms(name, near_blocks, far_blocks, sums, weight=1):
        arrays = [array for array, _ in near_blocks + far_blocks]

        def kernel(s, oth, out, nf, ff, kf, *refs):
            keys, refs = refs[: len(arrays)], refs[len(arrays) :]
            starts, ends = (refs[:2], refs[2:]) if sums else ((None, None), refs)

            def add(start, query, query_factor, blocks, refs, end):
                items = []
                for ref, (_, places) in zip(refs, blocks):
                    for k, row in enumerate(places):
                        if row is None:
                            continue
                        items.append((ref[k * rows : (k + 1) * rows, :], row, row in (0, 8)))
                before = None if start is None else start[...]
                end[...] = add_terms(before, query[...], query_factor[:, :1], kf, s[0], items)

            add(starts[0], oth, nf, near_blocks, keys[: len(near_blocks)], ends[0])
            add(starts[1], out, ff, far_blocks, keys[len(near_blocks) :], ends[1])

        return call(
            name, kernel, [total, total], (scale,),
            (other, outer, near_factor, far_factor, key_factors, *arrays, *(sums or ())), weight,
        )

    sums = terms("terms_own0", [(outer, [0]), (inner, [1]), (after(outer1, held), [2])], [(other, [8])], None, 100_000_000)
    def copy_kernel(block, out):
        out[...] = block[...]

    crossed = call(
        "crossed", copy_kernel, strip, (), (after(crossed, *sums),), 100_000_000
    )
    early, _ = lax.optimization_barrier((early, crossed))
    crossed = after(crossed, early)
    got = [
        crossed,
        send("gather1", crossed, line_to_line(2, 0)),
        send("gather2", crossed, line_to_line(1, 0)),
        send("gather3", crossed, line_to_line(3, 0)),
    ]

    def gather_kernel(q0, q1, q2, q3, out, sems):
        pieces = []
        for place, source in enumerate((q0, q1, q2, q3)):
            pieces.append((source, quarter, out, place * quarter, quarter))
            pieces.append((source, 0, out, rows + place * quarter, quarter))
        copy_all(sems, pieces)

    whole_blocks = assemble("whole_blocks", gather_kernel, blocks(2), (), tuple(got), 8)
    back = send("edge_back", whole_blocks, edge_to_previous_chip)
    inner1 = after(inner1, crossed)
    late = send("wide_late", inner1, to_next_wide)
    far2 = send("own_outer2", after(outer1, crossed), to_next_chip_sibling)
    near_sum, far_sum = sums

    def own1_kernel(s, oth, nf, kf, keys, near_in, near):
        near[...] = add_terms(
            near_in[...], oth[...], nf[:, :1], kf, s[0], [(keys[...], 3, False)]
        )

    near_sum = call(
        "terms_own1", own1_kernel, total, (scale,),
        (other, near_factor, key_factors, after(inner1, whole_blocks, far2), near_sum), 100_000_000,
    )

    def merge_kernel(edge, early, late, gathered, outer1, inner1, out, sems):
        own = [(outer1, 0, out, 2 * rows, rows), (inner1, 0, out, 3 * rows, rows)]

        @pl.when(edge[0] == 1)
        def _():
            copy_all(sems, own + [(gathered, 0, out, 0, 2 * rows)])

        @pl.when(edge[0] == 0)
        def _():
            copy_all(sems, own + [(early, 2 * rows, out, 0, rows), (late, 0, out, rows, rows)])

    carried = assemble(
        "merge", merge_kernel, blocks(4), (at_edge,),
        (early, after(late, near_sum), whole_blocks, outer1, inner1), 4,
    )
    sib = send("sibling1", carried, to_sibling)
    is_edge = mirrored == 0

    def near1_kernel(s, oth, nf, kf, keys, near_in, near):
        near[...] = add_terms(
            near_in[...], oth[...], nf[:, :1], kf, s[0], [(keys[: 2 * rows, :], 4, False)]
        )

    near_sum = call(
        "terms_near1", near1_kernel, total, (scale,),
        (other, near_factor, key_factors, carried, near_sum), 50_000_000,
    )
    hop_far2 = send(
        "farthest", jnp.where(is_edge, whole_blocks[:rows], after(far2, near_sum)), farthest_route
    )
    back = after(back, near_sum)
    hop_inner0 = jnp.where(is_edge, back[rows:], early[:rows])
    hop_sib0 = send("sibling_hop0", hop_inner0, to_sibling)
    anywhere = pl.BlockSpec(memory_space=pl.ANY)

    def near0_kernel(
        c, e, s, oth, nf, kf, inner0, back, early, near_in, image_grad, caption_grad, held_sum, sem
    ):
        outer0 = jnp.where(e[0] == 1, back[:rows, :], early[rows : 2 * rows, :])
        held_sum[...] = s[0] * add_terms(
            near_in[...], oth[...], nf[:, :1], kf, s[0],
            [(jnp.concatenate([inner0[...], outer0], axis=0), 6, False)],
        )

        @pl.when(c[0] == 1)
        def _():
            one = pltpu.make_async_copy(held_sum, image_grad, sem)
            one.start()
            one.wait()

        @pl.when(c[0] == 0)
        def _():
            one = pltpu.make_async_copy(held_sum, caption_grad, sem)
            one.start()
            one.wait()

    with jax.named_scope("terms_near0"):
        half_done = pl.pallas_call(
            near0_kernel,
            out_shape=[total, total],
            in_specs=[scalars()] * 3 + [whole()] * 7,
            out_specs=[anywhere] * 2,
            scratch_shapes=[pltpu.VMEM((rows, width), jnp.float32), pltpu.SemaphoreType.DMA],
            cost_estimate=pl.CostEstimate(
                flops=100_000_000_000, bytes_accessed=1000, transcendentals=0
            ),
            compiler_params=pltpu.CompilerParams(vmem_limit_bytes=16 * 1024 * 1024),
        )(
            core_flag, at_edge, scale,
            other, near_factor, key_factors, hop_inner0, back, early, near_sum,
        )

    def far1_kernel(s, out, ff, kf, keys, farthest, far_in, far):
        far[...] = add_terms(
            far_in[...], out[...], ff[:, :1], kf, s[0],
            [(keys[: 2 * rows, :], 12, False), (keys[2 * rows :, :], 9, False),
             (farthest[...], 11, False)],
        )

    far_sum = call(
        "terms_far1", far1_kernel, total, (scale,),
        (outer, far_factor, key_factors, after(sib, *half_done), far2, far_sum),
        100_000_000,
    )

    def last_kernel(
        c, s, out, ff, kf, hs0, hf2, far_in, _i, _c, image_grad, caption_grad, held_sum, sem
    ):
        held_sum[...] = s[0] * add_terms(
            far_in[...], out[...], ff[:, :1], kf, s[0],
            [(jnp.concatenate([hs0[...], hf2[...]], axis=0), 14, False)],
        )

        @pl.when(c[0] == 1)
        def _():
            one = pltpu.make_async_copy(held_sum, caption_grad, sem)
            one.start()
            one.wait()

        @pl.when(c[0] == 0)
        def _():
            one = pltpu.make_async_copy(held_sum, image_grad, sem)
            one.start()
            one.wait()

    with jax.named_scope("terms_last"):
        image_grad, caption_grad = pl.pallas_call(
            last_kernel,
            out_shape=[total, total],
            in_specs=[scalars()] * 2 + [whole()] * 6 + [anywhere] * 2,
            out_specs=[anywhere] * 2,
            scratch_shapes=[pltpu.VMEM((rows, width), jnp.float32), pltpu.SemaphoreType.DMA],
            input_output_aliases={8: 0, 9: 1},
            cost_estimate=pl.CostEstimate(flops=1000, bytes_accessed=1000, transcendentals=0),
            compiler_params=pltpu.CompilerParams(vmem_limit_bytes=16 * 1024 * 1024),
        )(
            core_flag, scale,
            outer, far_factor, key_factors, hop_sib0, hop_far2, far_sum, *half_done,
        )
    return image_grad, caption_grad


def solution(mesh):
    in_specs = (P(("blk", "wide"), None), P(("blk", "wide"), None), P(), P(), P())
    out_specs = (P(("blk", "wide"), None), P(("blk", "wide"), None))
    return jax.shard_map(
        on_device, mesh=mesh, in_specs=in_specs, out_specs=out_specs, check_vma=False
    )
```

```python
import jax
import jax.numpy as jnp
from jax import lax
from jax.experimental import pallas as pl
from jax.experimental.pallas import tpu as pltpu
from jax.sharding import PartitionSpec as P

AXES = ("blk", "wide")
LOG2E = 1.4426950408889634


def coordinates(blk, wide):
    return wide // 8, (wide // 4) % 2, wide % 4, blk // 2, blk % 2


def device_id(x, half, y, z, core):
    return ((z % 8) * 2 + core) * 32 + ((x % 4) * 2 + half) * 4 + y


def pairs(target):
    found = []
    for blk in range(16):
        for wide in range(32):
            x, half, y, z, core = coordinates(blk, wide)
            sign = 1 if core == 1 else -1
            mirrored = y if core == 1 else 3 - y
            there = target(x, half, mirrored, z, core, sign)
            if there is not None:
                x2, half2, mirrored2, z2, core2 = there
                y2 = mirrored2 if core == 1 else 3 - mirrored2
                found.append((blk * 32 + wide, device_id(x2, half2, y2, z2, core2)))
    return found


def crossing(x, half, sign):
    if sign == 1:
        return (x, 1) if half == 0 else (x + 1, 0)
    return (x, 0) if half == 1 else (x - 1, 1)


def to_sibling(x, h, m, z, c, s):
    return x, h, m, z, 1 - c


def to_previous_chip_sibling(x, h, m, z, c, s):
    return x, h, m, z - s, 1 - c


def to_next_chip_sibling(x, h, m, z, c, s):
    return x, h, m, z + s, 1 - c


def to_next_chip(x, h, m, z, c, s):
    return x, h, m, z + s, c


def to_previous_chip(x, h, m, z, c, s):
    return x, h, m, z - s, c


def to_next_wide(x, h, m, z, c, s):
    return (x, h, m + 1, z, c) if m < 3 else None


def farthest_route(x, h, m, z, c, s):
    return (x, h, m - 1, z, c) if m > 0 else (x, h, m, z + s, 1 - c)


def edge_to_previous_chip(x, h, m, z, c, s):
    return (x, h, m, z - s, c) if m == 0 else None


def across(x, h, m, z, c, s):
    x2, h2 = crossing(x, h, s)
    return x2, h2, m, z + s, c


def line_to_line(here, there):
    return lambda x, h, m, z, c, s: (x, h, there, z, c) if m == here else None


def send(name, x, target):
    with jax.named_scope(name):
        return lax.ppermute(x, AXES, pairs(target))


def scalars():
    return pl.BlockSpec(memory_space=pltpu.SMEM)


def whole():
    return pl.BlockSpec(memory_space=pltpu.VMEM)


def call(name, kernel, out_shape, smem, vmem, weight=1):
    many = isinstance(out_shape, (list, tuple))
    outs = [whole() for _ in out_shape] if many else whole()
    with jax.named_scope(name):
        return pl.pallas_call(
            kernel,
            out_shape=out_shape,
            in_specs=[scalars() for _ in smem] + [whole() for _ in vmem],
            out_specs=outs,
            cost_estimate=pl.CostEstimate(
                flops=weight * 1000, bytes_accessed=1000, transcendentals=0
            ),
            compiler_params=pltpu.CompilerParams(vmem_limit_bytes=16 * 1024 * 1024),
        )(*smem, *vmem)


def assemble(name, kernel, out_shape, smem, arrays, copies):
    many = isinstance(out_shape, (list, tuple))
    with jax.named_scope(name):
        return pl.pallas_call(
            kernel,
            out_shape=out_shape,
            in_specs=[scalars() for _ in smem] + [pl.BlockSpec(memory_space=pl.ANY) for _ in arrays],
            out_specs=[whole() for _ in out_shape] if many else whole(),
            scratch_shapes=[pltpu.SemaphoreType.DMA((copies,))],
            cost_estimate=pl.CostEstimate(flops=1000, bytes_accessed=1000, transcendentals=0),
            compiler_params=pltpu.CompilerParams(vmem_limit_bytes=16 * 1024 * 1024),
        )(*smem, *arrays)


def copy_all(sems, pieces):
    moves = [
        pltpu.make_async_copy(
            source.at[pl.ds(low, count)], target.at[pl.ds(at, count)], sems.at[k]
        )
        for k, (source, low, target, at, count) in enumerate(pieces)
    ]
    for one in moves:
        one.start()
    for one in moves:
        one.wait()


def term(query, query_factor, keys, key_factor, scale, own=False):
    logits = lax.dot_general(
        query, keys, (((1,), (1,)), ((), ())), preferred_element_type=jnp.float32
    )
    weights = jnp.exp2(logits * (scale * LOG2E) - 5.0 * LOG2E) * (query_factor + key_factor)
    if own:
        rows = lax.broadcasted_iota(jnp.int32, weights.shape, 0)
        cols = lax.broadcasted_iota(jnp.int32, weights.shape, 1)
        weights = weights - jnp.where(rows == cols, 1.0, 0.0)
    return jnp.dot(weights.astype(jnp.bfloat16), keys, preferred_element_type=jnp.float32)


def add_terms(total, query, query_factor, key_factors, scale, items):
    rows = query.shape[0]
    for keys, place, own in items:
        chosen = key_factors[:, place * rows : place * rows + keys.shape[0]]
        part = term(query, query_factor, keys, chosen, scale, own)
        total = part if total is None else total + part
    return total


def cut_kernel(inner, outer, *outs):
    quarter = inner.shape[0] // 4
    for step in range(4):
        low = quarter * step
        outs[step][:quarter, :] = inner[low : low + quarter, :]
        outs[step][quarter:, :] = outer[low : low + quarter, :]


def on_device(images, captions, logit_scale, row_lse, col_lse):
    rows, width = images.shape
    quarter = rows // 4
    half = jnp.bfloat16
    blk = lax.axis_index("blk")
    wide = lax.axis_index("wide")
    core = blk % 2
    sign = 2 * core - 1
    y = wide % 4
    mirrored = jnp.where(core == 1, y, 3 - y)
    carries_captions = core == 1
    at_edge = jnp.where(mirrored == 0, 1, 0).astype(jnp.int32).reshape(1)
    core_flag = core.astype(jnp.int32).reshape(1)
    scale = logit_scale.reshape(1)

    def blocks(count):
        return jax.ShapeDtypeStruct((count * rows, width), half)

    outer = jnp.where(carries_captions, captions, images)
    other = jnp.where(carries_captions, images, captions)

    def after(value, *others):
        return lax.optimization_barrier((value, *others))[0]

    inner = send("swap", other, to_sibling)
    outer1 = send("own_outer1", outer, to_next_chip)
    inner1 = send("own_inner1", other, to_previous_chip_sibling)

    strip = jax.ShapeDtypeStruct((2 * quarter, width), half)
    cuts = call("cut", cut_kernel, [strip] * 4, (), (inner, outer))
    spread0 = send("spread0", cuts[0], line_to_line(3, 0))
    spread1 = send("spread1", cuts[1], line_to_line(3, 2))
    spread2 = send("spread2", cuts[2], line_to_line(3, 1))
    held = jnp.where(
        mirrored == 0,
        spread0,
        jnp.where(mirrored == 2, spread1, jnp.where(mirrored == 1, spread2, cuts[3])),
    )
    crossed = send("cross", held, across)
    early = send(
        "wide_early", jnp.concatenate([after(inner, held), outer, outer1], axis=0), to_next_wide
    )

    batch = row_lse.shape[0]

    def part(carried, b, w):
        start = ((b % 16) * 32 + (w % 32)) * rows
        from_rows = lax.dynamic_slice_in_dim(row_lse, start, rows)
        from_cols = lax.dynamic_slice_in_dim(col_lse, start, rows)
        return jnp.where(carries_captions == carried, from_cols, from_rows)

    pal = blk + 1 - 2 * core
    near_w, far_w = wide - sign, wide + sign
    own_outer = part(True, blk, wide)
    own_other = part(False, blk, wide)
    normalizers = [
        own_outer,
        part(True, pal, wide),
        part(True, blk - 2 * sign, wide),
        part(True, pal - 2 * sign, wide),
        part(True, blk - 2 * sign, near_w),
        part(True, pal - 2 * sign, near_w),
        part(True, pal, near_w),
        part(True, blk, near_w),
        own_other,
        part(False, pal + 2 * sign, wide),
        part(False, blk + 2 * sign, wide),
        part(False, pal + 4 * sign, wide),
        part(False, pal + 2 * sign, far_w),
        part(False, blk + 2 * sign, far_w),
        part(False, blk, far_w),
        part(False, pal + 4 * sign, far_w),
    ]

    def factors_kernel(*refs):
        sources, (keys, near, far) = refs[:-3], refs[-3:]
        for k, source in enumerate(sources):
            keys[:, k * rows : (k + 1) * rows] = 0.5 * jnp.exp(5.0 - source[...].reshape(1, rows))
        near[...] = jnp.broadcast_to(keys[:, 8 * rows : 9 * rows], (128, rows)).T
        far[...] = jnp.broadcast_to(keys[:, :rows], (128, rows)).T

    key_factors, near_factor, far_factor = call(
        "factors", factors_kernel,
        [jax.ShapeDtypeStruct(shape, jnp.float32) for shape in ((1, 16 * rows), (rows, 128), (rows, 128))],
        (), tuple(lax.optimization_barrier((*normalizers, held))[:-1]),
    )
    total = jax.ShapeDtypeStruct((rows, width), jnp.float32)

    def terms(name, near_blocks, far_blocks, sums, weight=1):
        arrays = [array for array, _ in near_blocks + far_blocks]

        def kernel(s, oth, out, nf, ff, kf, *refs):
            keys, refs = refs[: len(arrays)], refs[len(arrays) :]
            starts, ends = (refs[:2], refs[2:]) if sums else ((None, None), refs)

            def add(start, query, query_factor, blocks, refs, end):
                items = []
                for ref, (_, places) in zip(refs, blocks):
                    for k, row in enumerate(places):
                        if row is None:
                            continue
                        items.append((ref[k * rows : (k + 1) * rows, :], row, row in (0, 8)))
                before = None if start is None else start[...]
                end[...] = add_terms(before, query[...], query_factor[:, :1], kf, s[0], items)

            add(starts[0], oth, nf, near_blocks, keys[: len(near_blocks)], ends[0])
            add(starts[1], out, ff, far_blocks, keys[len(near_blocks) :], ends[1])

        return call(
            name, kernel, [total, total], (scale,),
            (other, outer, near_factor, far_factor, key_factors, *arrays, *(sums or ())), weight,
        )

    sums = terms("terms_own0", [(outer, [0]), (inner, [1]), (after(outer1, held), [2])], [(other, [8])], None, 100_000_000)
    def copy_kernel(block, out):
        out[...] = block[...]

    crossed = call(
        "crossed", copy_kernel, strip, (), (after(crossed, *sums),), 100_000_000
    )
    early, _ = lax.optimization_barrier((early, crossed))
    crossed = after(crossed, early)
    got = [
        crossed,
        send("gather1", crossed, line_to_line(2, 0)),
        send("gather2", crossed, line_to_line(1, 0)),
        send("gather3", crossed, line_to_line(3, 0)),
    ]

    def gather_kernel(q0, q1, q2, q3, out, sems):
        pieces = []
        for place, source in enumerate((q0, q1, q2, q3)):
            pieces.append((source, quarter, out, place * quarter, quarter))
            pieces.append((source, 0, out, rows + place * quarter, quarter))
        copy_all(sems, pieces)

    whole_blocks = assemble("whole_blocks", gather_kernel, blocks(2), (), tuple(got), 8)
    back = send("edge_back", whole_blocks, edge_to_previous_chip)
    inner1 = after(inner1, crossed)
    late = send("wide_late", inner1, to_next_wide)
    far2 = send("own_outer2", after(outer1, crossed), to_next_chip_sibling)
    near_sum, far_sum = sums

    def own1_kernel(s, oth, nf, kf, keys, near_in, near):
        near[...] = add_terms(
            near_in[...], oth[...], nf[:, :1], kf, s[0], [(keys[...], 3, False)]
        )

    near_sum = call(
        "terms_own1", own1_kernel, total, (scale,),
        (other, near_factor, key_factors, after(inner1, whole_blocks), near_sum), 100_000_000,
    )

    def merge_kernel(edge, early, late, gathered, outer1, inner1, out, sems):
        own = [(outer1, 0, out, 2 * rows, rows), (inner1, 0, out, 3 * rows, rows)]

        @pl.when(edge[0] == 1)
        def _():
            copy_all(sems, own + [(gathered, 0, out, 0, 2 * rows)])

        @pl.when(edge[0] == 0)
        def _():
            copy_all(sems, own + [(early, 2 * rows, out, 0, rows), (late, 0, out, rows, rows)])

    carried = assemble(
        "merge", merge_kernel, blocks(4), (at_edge,),
        (early, after(late, near_sum), whole_blocks, outer1, inner1), 4,
    )
    sib = send("sibling1", carried, to_sibling)
    is_edge = mirrored == 0

    def near1_kernel(s, oth, nf, kf, keys, near_in, near):
        near[...] = add_terms(
            near_in[...], oth[...], nf[:, :1], kf, s[0], [(keys[: 2 * rows, :], 4, False)]
        )

    near_sum = call(
        "terms_near1", near1_kernel, total, (scale,),
        (other, near_factor, key_factors, after(carried, far2), near_sum), 50_000_000,
    )
    hop_far2 = send(
        "farthest", jnp.where(is_edge, whole_blocks[:rows], after(far2, near_sum)), farthest_route
    )
    back = after(back, near_sum)
    hop_inner0 = jnp.where(is_edge, back[rows:], early[:rows])
    hop_sib0 = send("sibling_hop0", hop_inner0, to_sibling)
    anywhere = pl.BlockSpec(memory_space=pl.ANY)

    def near0_kernel(
        c, e, s, oth, nf, kf, inner0, back, early, near_in, image_grad, caption_grad, held_sum, sem
    ):
        outer0 = jnp.where(e[0] == 1, back[:rows, :], early[rows : 2 * rows, :])
        held_sum[...] = s[0] * add_terms(
            near_in[...], oth[...], nf[:, :1], kf, s[0],
            [(jnp.concatenate([inner0[...], outer0], axis=0), 6, False)],
        )

        @pl.when(c[0] == 1)
        def _():
            one = pltpu.make_async_copy(held_sum, image_grad, sem)
            one.start()
            one.wait()

        @pl.when(c[0] == 0)
        def _():
            one = pltpu.make_async_copy(held_sum, caption_grad, sem)
            one.start()
            one.wait()

    with jax.named_scope("terms_near0"):
        half_done = pl.pallas_call(
            near0_kernel,
            out_shape=[total, total],
            in_specs=[scalars()] * 3 + [whole()] * 7,
            out_specs=[anywhere] * 2,
            scratch_shapes=[pltpu.VMEM((rows, width), jnp.float32), pltpu.SemaphoreType.DMA],
            cost_estimate=pl.CostEstimate(
                flops=100_000_000_000, bytes_accessed=1000, transcendentals=0
            ),
            compiler_params=pltpu.CompilerParams(vmem_limit_bytes=16 * 1024 * 1024),
        )(
            core_flag, at_edge, scale,
            other, near_factor, key_factors, hop_inner0, back, early, near_sum,
        )

    def far1_kernel(s, out, ff, kf, keys, farthest, far_in, far):
        far[...] = add_terms(
            far_in[...], out[...], ff[:, :1], kf, s[0],
            [(keys[: 2 * rows, :], 12, False), (keys[2 * rows :, :], 9, False),
             (farthest[...], 11, False)],
        )

    far_sum = call(
        "terms_far1", far1_kernel, total, (scale,),
        (outer, far_factor, key_factors, after(sib, *half_done), far2, far_sum),
        100_000_000,
    )

    def last_kernel(
        c, s, out, ff, kf, hs0, hf2, far_in, _i, _c, image_grad, caption_grad, held_sum, sem
    ):
        held_sum[...] = s[0] * add_terms(
            far_in[...], out[...], ff[:, :1], kf, s[0],
            [(jnp.concatenate([hs0[...], hf2[...]], axis=0), 14, False)],
        )

        @pl.when(c[0] == 1)
        def _():
            one = pltpu.make_async_copy(held_sum, caption_grad, sem)
            one.start()
            one.wait()

        @pl.when(c[0] == 0)
        def _():
            one = pltpu.make_async_copy(held_sum, image_grad, sem)
            one.start()
            one.wait()

    with jax.named_scope("terms_last"):
        image_grad, caption_grad = pl.pallas_call(
            last_kernel,
            out_shape=[total, total],
            in_specs=[scalars()] * 2 + [whole()] * 6 + [anywhere] * 2,
            out_specs=[anywhere] * 2,
            scratch_shapes=[pltpu.VMEM((rows, width), jnp.float32), pltpu.SemaphoreType.DMA],
            input_output_aliases={8: 0, 9: 1},
            cost_estimate=pl.CostEstimate(flops=1000, bytes_accessed=1000, transcendentals=0),
            compiler_params=pltpu.CompilerParams(vmem_limit_bytes=16 * 1024 * 1024),
        )(
            core_flag, scale,
            outer, far_factor, key_factors, hop_sib0, hop_far2, far_sum, *half_done,
        )
    return image_grad, caption_grad


def solution(mesh):
    in_specs = (P(("blk", "wide"), None), P(("blk", "wide"), None), P(), P(), P())
    out_specs = (P(("blk", "wide"), None), P(("blk", "wide"), None))
    return jax.shard_map(
        on_device, mesh=mesh, in_specs=in_specs, out_specs=out_specs, check_vma=False
    )
```

```python
import jax
import jax.numpy as jnp
from jax import lax
from jax.experimental import pallas as pl
from jax.experimental.pallas import tpu as pltpu
from jax.sharding import PartitionSpec as P

AXES = ("blk", "wide")
LOG2E = 1.4426950408889634


def coordinates(blk, wide):
    return wide // 8, (wide // 4) % 2, wide % 4, blk // 2, blk % 2


def device_id(x, half, y, z, core):
    return ((z % 8) * 2 + core) * 32 + ((x % 4) * 2 + half) * 4 + y


def pairs(target):
    found = []
    for blk in range(16):
        for wide in range(32):
            x, half, y, z, core = coordinates(blk, wide)
            sign = 1 if core == 1 else -1
            mirrored = y if core == 1 else 3 - y
            there = target(x, half, mirrored, z, core, sign)
            if there is not None:
                x2, half2, mirrored2, z2, core2 = there
                y2 = mirrored2 if core == 1 else 3 - mirrored2
                found.append((blk * 32 + wide, device_id(x2, half2, y2, z2, core2)))
    return found


def crossing(x, half, sign):
    if sign == 1:
        return (x, 1) if half == 0 else (x + 1, 0)
    return (x, 0) if half == 1 else (x - 1, 1)


def to_sibling(x, h, m, z, c, s):
    return x, h, m, z, 1 - c


def to_previous_chip_sibling(x, h, m, z, c, s):
    return x, h, m, z - s, 1 - c


def to_next_chip_sibling(x, h, m, z, c, s):
    return x, h, m, z + s, 1 - c


def to_next_chip(x, h, m, z, c, s):
    return x, h, m, z + s, c


def to_previous_chip(x, h, m, z, c, s):
    return x, h, m, z - s, c


def to_next_wide(x, h, m, z, c, s):
    return (x, h, m + 1, z, c) if m < 3 else None


def farthest_route(x, h, m, z, c, s):
    return (x, h, m - 1, z, c) if m > 0 else (x, h, m, z + s, 1 - c)


def edge_to_previous_chip(x, h, m, z, c, s):
    return (x, h, m, z - s, c) if m == 0 else None


def across(x, h, m, z, c, s):
    x2, h2 = crossing(x, h, s)
    return x2, h2, m, z + s, c


def line_to_line(here, there):
    return lambda x, h, m, z, c, s: (x, h, there, z, c) if m == here else None


def send(name, x, target):
    with jax.named_scope(name):
        return lax.ppermute(x, AXES, pairs(target))


def scalars():
    return pl.BlockSpec(memory_space=pltpu.SMEM)


def whole():
    return pl.BlockSpec(memory_space=pltpu.VMEM)


def call(name, kernel, out_shape, smem, vmem, weight=1):
    many = isinstance(out_shape, (list, tuple))
    outs = [whole() for _ in out_shape] if many else whole()
    with jax.named_scope(name):
        return pl.pallas_call(
            kernel,
            out_shape=out_shape,
            in_specs=[scalars() for _ in smem] + [whole() for _ in vmem],
            out_specs=outs,
            cost_estimate=pl.CostEstimate(
                flops=weight * 1000, bytes_accessed=1000, transcendentals=0
            ),
            compiler_params=pltpu.CompilerParams(vmem_limit_bytes=16 * 1024 * 1024),
        )(*smem, *vmem)


def assemble(name, kernel, out_shape, smem, arrays, copies):
    many = isinstance(out_shape, (list, tuple))
    with jax.named_scope(name):
        return pl.pallas_call(
            kernel,
            out_shape=out_shape,
            in_specs=[scalars() for _ in smem] + [pl.BlockSpec(memory_space=pl.ANY) for _ in arrays],
            out_specs=[whole() for _ in out_shape] if many else whole(),
            scratch_shapes=[pltpu.SemaphoreType.DMA((copies,))],
            cost_estimate=pl.CostEstimate(flops=1000, bytes_accessed=1000, transcendentals=0),
            compiler_params=pltpu.CompilerParams(vmem_limit_bytes=16 * 1024 * 1024),
        )(*smem, *arrays)


def copy_all(sems, pieces):
    moves = [
        pltpu.make_async_copy(
            source.at[pl.ds(low, count)], target.at[pl.ds(at, count)], sems.at[k]
        )
        for k, (source, low, target, at, count) in enumerate(pieces)
    ]
    for one in moves:
        one.start()
    for one in moves:
        one.wait()


def term(query, query_factor, keys, key_factor, scale, own=False):
    logits = lax.dot_general(
        query, keys, (((1,), (1,)), ((), ())), preferred_element_type=jnp.float32
    )
    weights = jnp.exp2(logits * (scale * LOG2E) - 5.0 * LOG2E) * (query_factor + key_factor)
    if own:
        rows = lax.broadcasted_iota(jnp.int32, weights.shape, 0)
        cols = lax.broadcasted_iota(jnp.int32, weights.shape, 1)
        weights = weights - jnp.where(rows == cols, 1.0, 0.0)
    return jnp.dot(weights.astype(jnp.bfloat16), keys, preferred_element_type=jnp.float32)


def add_terms(total, query, query_factor, key_factors, scale, items):
    rows = query.shape[0]
    for keys, place, own in items:
        chosen = key_factors[:, place * rows : place * rows + keys.shape[0]]
        part = term(query, query_factor, keys, chosen, scale, own)
        total = part if total is None else total + part
    return total


def cut_kernel(inner, outer, *outs):
    quarter = inner.shape[0] // 4
    for step in range(4):
        low = quarter * step
        outs[step][:quarter, :] = inner[low : low + quarter, :]
        outs[step][quarter:, :] = outer[low : low + quarter, :]


def on_device(images, captions, logit_scale, row_lse, col_lse):
    rows, width = images.shape
    quarter = rows // 4
    half = jnp.bfloat16
    blk = lax.axis_index("blk")
    wide = lax.axis_index("wide")
    core = blk % 2
    sign = 2 * core - 1
    y = wide % 4
    mirrored = jnp.where(core == 1, y, 3 - y)
    carries_captions = core == 1
    at_edge = jnp.where(mirrored == 0, 1, 0).astype(jnp.int32).reshape(1)
    core_flag = core.astype(jnp.int32).reshape(1)
    scale = logit_scale.reshape(1)

    def blocks(count):
        return jax.ShapeDtypeStruct((count * rows, width), half)

    outer = jnp.where(carries_captions, captions, images)
    other = jnp.where(carries_captions, images, captions)

    def after(value, *others):
        return lax.optimization_barrier((value, *others))[0]

    inner = send("swap", other, to_sibling)
    outer1 = send("own_outer1", outer, to_next_chip)
    inner1 = send("own_inner1", other, to_previous_chip_sibling)

    strip = jax.ShapeDtypeStruct((2 * quarter, width), half)
    cuts = call("cut", cut_kernel, [strip] * 4, (), (inner, outer))
    spread0 = send("spread0", cuts[0], line_to_line(3, 0))
    spread1 = send("spread1", cuts[1], line_to_line(3, 2))
    spread2 = send("spread2", cuts[2], line_to_line(3, 1))
    held = jnp.where(
        mirrored == 0,
        spread0,
        jnp.where(mirrored == 2, spread1, jnp.where(mirrored == 1, spread2, cuts[3])),
    )
    crossed = send("cross", held, across)
    early = send(
        "wide_early", jnp.concatenate([after(inner, held), outer, outer1], axis=0), to_next_wide
    )

    batch = row_lse.shape[0]

    def part(carried, b, w):
        start = ((b % 16) * 32 + (w % 32)) * rows
        from_rows = lax.dynamic_slice_in_dim(row_lse, start, rows)
        from_cols = lax.dynamic_slice_in_dim(col_lse, start, rows)
        return jnp.where(carries_captions == carried, from_cols, from_rows)

    pal = blk + 1 - 2 * core
    near_w, far_w = wide - sign, wide + sign
    own_outer = part(True, blk, wide)
    own_other = part(False, blk, wide)
    normalizers = [
        own_outer,
        part(True, pal, wide),
        part(True, blk - 2 * sign, wide),
        part(True, pal - 2 * sign, wide),
        part(True, blk - 2 * sign, near_w),
        part(True, pal - 2 * sign, near_w),
        part(True, pal, near_w),
        part(True, blk, near_w),
        own_other,
        part(False, pal + 2 * sign, wide),
        part(False, blk + 2 * sign, wide),
        part(False, pal + 4 * sign, wide),
        part(False, pal + 2 * sign, far_w),
        part(False, blk + 2 * sign, far_w),
        part(False, blk, far_w),
        part(False, pal + 4 * sign, far_w),
    ]

    def factors_kernel(*refs):
        sources, (keys, near, far) = refs[:-3], refs[-3:]
        for k, source in enumerate(sources):
            keys[:, k * rows : (k + 1) * rows] = 0.5 * jnp.exp(5.0 - source[...].reshape(1, rows))
        near[...] = jnp.broadcast_to(keys[:, 8 * rows : 9 * rows], (128, rows)).T
        far[...] = jnp.broadcast_to(keys[:, :rows], (128, rows)).T

    key_factors, near_factor, far_factor = call(
        "factors", factors_kernel,
        [jax.ShapeDtypeStruct(shape, jnp.float32) for shape in ((1, 16 * rows), (rows, 128), (rows, 128))],
        (), tuple(lax.optimization_barrier((*normalizers, held))[:-1]),
    )
    total = jax.ShapeDtypeStruct((rows, width), jnp.float32)

    def terms(name, near_blocks, far_blocks, sums, weight=1):
        arrays = [array for array, _ in near_blocks + far_blocks]

        def kernel(s, oth, out, nf, ff, kf, *refs):
            keys, refs = refs[: len(arrays)], refs[len(arrays) :]
            starts, ends = (refs[:2], refs[2:]) if sums else ((None, None), refs)

            def add(start, query, query_factor, blocks, refs, end):
                items = []
                for ref, (_, places) in zip(refs, blocks):
                    for k, row in enumerate(places):
                        if row is None:
                            continue
                        items.append((ref[k * rows : (k + 1) * rows, :], row, row in (0, 8)))
                before = None if start is None else start[...]
                end[...] = add_terms(before, query[...], query_factor[:, :1], kf, s[0], items)

            add(starts[0], oth, nf, near_blocks, keys[: len(near_blocks)], ends[0])
            add(starts[1], out, ff, far_blocks, keys[len(near_blocks) :], ends[1])

        return call(
            name, kernel, [total, total], (scale,),
            (other, outer, near_factor, far_factor, key_factors, *arrays, *(sums or ())), weight,
        )

    sums = terms("terms_own0", [(outer, [0]), (inner, [1]), (after(outer1, held), [2])], [(other, [8])], None, 100_000_000)
    def copy_kernel(block, out):
        out[...] = block[...]

    crossed = call(
        "crossed", copy_kernel, strip, (), (after(crossed, *sums),), 100_000_000
    )
    early, _ = lax.optimization_barrier((early, crossed))
    crossed = after(crossed, early)
    got = [
        crossed,
        send("gather1", crossed, line_to_line(2, 0)),
        send("gather2", crossed, line_to_line(1, 0)),
        send("gather3", crossed, line_to_line(3, 0)),
    ]

    def gather_kernel(q0, q1, q2, q3, out, sems):
        pieces = []
        for place, source in enumerate((q0, q1, q2, q3)):
            pieces.append((source, quarter, out, place * quarter, quarter))
            pieces.append((source, 0, out, rows + place * quarter, quarter))
        copy_all(sems, pieces)

    whole_blocks = assemble("whole_blocks", gather_kernel, blocks(2), (), tuple(got), 8)
    back = send("edge_back", whole_blocks, edge_to_previous_chip)
    inner1 = after(inner1, crossed)
    late = send("wide_late", inner1, to_next_wide)
    far2 = send("own_outer2", after(outer1, crossed), to_next_chip_sibling)
    near_sum, far_sum = sums

    def own1_kernel(s, oth, nf, kf, keys, near_in, near):
        near[...] = add_terms(
            near_in[...], oth[...], nf[:, :1], kf, s[0], [(keys[...], 3, False)]
        )

    near_sum = call(
        "terms_own1", own1_kernel, total, (scale,),
        (other, near_factor, key_factors, after(inner1, whole_blocks, far2), near_sum), 100_000_000,
    )

    def merge_kernel(edge, early, late, gathered, out, sems):
        @pl.when(edge[0] == 1)
        def _():
            copy_all(sems, [(gathered, 0, out, 0, 2 * rows)])

        @pl.when(edge[0] == 0)
        def _():
            copy_all(sems, [(early, 2 * rows, out, 0, rows), (late, 0, out, rows, rows)])

    hop1 = assemble(
        "merge", merge_kernel, blocks(2), (at_edge,),
        (early, after(late, near_sum), whole_blocks), 2,
    )
    hop_sib1 = send("sibling_hop1", hop1, to_sibling)
    sib1 = send(
        "sibling_own1", jnp.concatenate([outer1, inner1], axis=0), to_sibling
    )
    is_edge = mirrored == 0

    def near1_kernel(s, oth, nf, kf, keys, near_in, near):
        near[...] = add_terms(
            near_in[...], oth[...], nf[:, :1], kf, s[0], [(keys[...], 4, False)]
        )

    near_sum = call(
        "terms_near1", near1_kernel, total, (scale,),
        (other, near_factor, key_factors, hop1, near_sum),
    )
    hop_sib1 = send("sibling_hop1", hop1, to_sibling)

    def far1_kernel(s, out, ff, kf, own, farthest, far_in, far):
        far[...] = add_terms(
            far_in[...], out[...], ff[:, :1], kf, s[0],
            [(own[...], 9, False), (farthest[...], 11, False)],
        )

    far_sum = call(
        "terms_far1", far1_kernel, total, (scale,),
        (outer, far_factor, key_factors, after(sib1, near_sum), far2, far_sum), 50_000_000,
    )

    hop_far2 = send(
        "farthest", jnp.where(is_edge, whole_blocks[:rows], far2), farthest_route
    )

    def far2_kernel(s, out, ff, kf, hop, far_in, far):
        far[...] = add_terms(
            far_in[...], out[...], ff[:, :1], kf, s[0], [(hop[...], 12, False)]
        )

    far_sum = call(
        "terms_far2", far2_kernel, total, (scale,),
        (outer, far_factor, key_factors, hop_sib1, far_sum),
    )
    back = after(back, far_sum)
    hop_inner0 = jnp.where(is_edge, back[rows:], early[:rows])
    hop_sib0 = send("sibling_hop0", hop_inner0, to_sibling)
    anywhere = pl.BlockSpec(memory_space=pl.ANY)

    def near0_kernel(
        c, e, s, oth, nf, kf, inner0, back, early, near_in, image_grad, caption_grad, held_sum, sem
    ):
        outer0 = jnp.where(e[0] == 1, back[:rows, :], early[rows : 2 * rows, :])
        held_sum[...] = s[0] * add_terms(
            near_in[...], oth[...], nf[:, :1], kf, s[0],
            [(jnp.concatenate([inner0[...], outer0], axis=0), 6, False)],
        )

        @pl.when(c[0] == 1)
        def _():
            one = pltpu.make_async_copy(held_sum, image_grad, sem)
            one.start()
            one.wait()

        @pl.when(c[0] == 0)
        def _():
            one = pltpu.make_async_copy(held_sum, caption_grad, sem)
            one.start()
            one.wait()

    with jax.named_scope("terms_near0"):
        half_done = pl.pallas_call(
            near0_kernel,
            out_shape=[total, total],
            in_specs=[scalars()] * 3 + [whole()] * 7,
            out_specs=[anywhere] * 2,
            scratch_shapes=[pltpu.VMEM((rows, width), jnp.float32), pltpu.SemaphoreType.DMA],
            cost_estimate=pl.CostEstimate(
                flops=100_000_000_000, bytes_accessed=1000, transcendentals=0
            ),
            compiler_params=pltpu.CompilerParams(vmem_limit_bytes=16 * 1024 * 1024),
        )(
            core_flag, at_edge, scale,
            other, near_factor, key_factors, hop_inner0, back, early, near_sum,
        )

    def last_kernel(
        c, s, out, ff, kf, hs0, hf2, far_in, _i, _c, image_grad, caption_grad, held_sum, sem
    ):
        held_sum[...] = s[0] * add_terms(
            far_in[...], out[...], ff[:, :1], kf, s[0],
            [(jnp.concatenate([hs0[...], hf2[...]], axis=0), 14, False)],
        )

        @pl.when(c[0] == 1)
        def _():
            one = pltpu.make_async_copy(held_sum, caption_grad, sem)
            one.start()
            one.wait()

        @pl.when(c[0] == 0)
        def _():
            one = pltpu.make_async_copy(held_sum, image_grad, sem)
            one.start()
            one.wait()

    with jax.named_scope("terms_last"):
        image_grad, caption_grad = pl.pallas_call(
            last_kernel,
            out_shape=[total, total],
            in_specs=[scalars()] * 2 + [whole()] * 6 + [anywhere] * 2,
            out_specs=[anywhere] * 2,
            scratch_shapes=[pltpu.VMEM((rows, width), jnp.float32), pltpu.SemaphoreType.DMA],
            input_output_aliases={8: 0, 9: 1},
            cost_estimate=pl.CostEstimate(flops=1000, bytes_accessed=1000, transcendentals=0),
            compiler_params=pltpu.CompilerParams(vmem_limit_bytes=16 * 1024 * 1024),
        )(
            core_flag, scale,
            outer, far_factor, key_factors, hop_sib0, hop_far2, far_sum, *half_done,
        )
    return image_grad, caption_grad


def solution(mesh):
    in_specs = (P(("blk", "wide"), None), P(("blk", "wide"), None), P(), P(), P())
    out_specs = (P(("blk", "wide"), None), P(("blk", "wide"), None))
    return jax.shard_map(
        on_device, mesh=mesh, in_specs=in_specs, out_specs=out_specs, check_vma=False
    )
```
